32 devices in a mesh: dp: 8 (over y, x, core), seq: 4 (over z).
Axes of the slice: x: 2, y: 2, z: 4, core: 2. Of those that a mesh axis runs over, the one named last changes fastest.
Arguments:
- queries: bfloat16 [4096, 2048], P(('dp', 'seq')), may hold values from -6 to 6
- keys: bfloat16 [4096, 2048], P(('dp', 'seq')), may hold values from -6 to 6
- values: bfloat16 [4096, 2048], P(('dp', 'seq')), may hold values from -6 to 6
- text_kv: bfloat16 [64, 256, 2, 2048], P('dp', None, None, 'seq'), may hold values from -6 to 6
- text_lengths: int32 [64], P('dp'), may hold values from 1 to 256
- clip_lengths: int32 [8, 8], P('dp'), may hold values from 1 to 128, 512 in all within a row
- timesteps: int32 [64], P('dp'), may hold values from 0 to 999
- mod_weight: bfloat16 [256, 4096], replicated, may hold values from -0.375 to 0.375
- final_weight: bfloat16 [2048, 64], replicated, may hold values from -0.125 to 0.125
- noise: float32 [4096, 64], P(('dp', 'seq')), may hold values from -6 to 6
- clean: float32 [4096, 64], P(('dp', 'seq')), may hold values from -12 to 12
- report_order: int32 [64], P('dp'), may hold values from 0 to 63, each once
Outputs:
- scores: float32 [64], P('dp')
The draws below stay inside these ranges and needn't reach their ends.
Inputs may be any that keep to these rules, and one draw needn't show every extreme that they name: Each row of clip_lengths sums to 512, and its largest entry is exactly 128.
All inputs are finite; a program needn't handle non-finite values.
Results may differ from the reference program's by a relative error of at most 0.00055.
Values may be sent and summed in bfloat16 or wider, within the bound.
No kernel may reach another device: no remote copies, remote signals or barrier semaphores. Data moves between devices by JAX's collectives and lax.ppermute only.
A program may use at most 128 MiB of HBM per device.

```python
import math
import jax
import jax.numpy as jnp
import numpy as np
from jax import lax

HEADS = 16
HEAD_DIM = 128
CHANNELS = 64
TEXT_LEN = 256
FREQ = 256
STEPS = 1000
TOK_DEV = 128
CLIPS_GRP = 8
WIDTH = 2048
GROUPS = 8
GRP_TOK = 512
CLIP_MOST = 128
TOKENS = 4096
CLIPS = 64
N_DP = 8
N_SEQ = 4


def drawn_rows(key):
    return jnp.clip(jax.random.normal(key, (TOKENS, HEADS * HEAD_DIM), jnp.float32), -6.0, 6.0)


def draw_queries(key, part):
    key = jax.random.fold_in(key, 11)
    drawn = drawn_rows(key)
    return drawn.astype(jnp.bfloat16)


def draw_keys(key, part):
    key = jax.random.fold_in(key, 23)
    drawn = drawn_rows(key)
    return drawn.astype(jnp.bfloat16)


def draw_clean(key, part):
    key = jax.random.fold_in(key, 37)
    key_base, key_rows, key_cols = jax.random.split(key, 3)
    row_scale = jnp.exp(jax.random.uniform(key_rows, (TOKENS, 1), jnp.float32, -1.15, 1.15))
    col_scale = jnp.exp(jax.random.uniform(key_cols, (1, CHANNELS), jnp.float32, -0.6, 0.6))
    base = jax.random.normal(key_base, (TOKENS, CHANNELS), jnp.float32)
    return jnp.clip(base * row_scale * col_scale, -12.0, 12.0)


def plant(array, stream_key, low, largest):
    longest = array.shape.index(max(array.shape))
    spots = []
    for shift in (0, 1):
        where = [jax.random.randint(jax.random.fold_in(stream_key, axis), (), 0, length) for axis, length in enumerate(array.shape)]
        where[longest] = (where[longest] + shift) % array.shape[longest]
        spots.append(tuple(where))
    return array.at[spots[0]].set(low).at[spots[1]].set(largest)


def levels(stream_key, shape, shards, least, top_value):
    loudness = 1.0
    for dim, shards_of in shards:
        draws = jax.random.uniform(jax.random.fold_in(jax.random.fold_in(stream_key, 6), dim), (shards_of,), jnp.float32, least / len(shards), top_value / len(shards))
        loudness = loudness * jnp.repeat(jnp.exp(draws), shape[dim] // shards_of).reshape((-1,) + (1,) * (len(shape) - 1 - dim))
    return loudness


def split_up(number_of, total, reach, lean):
    portions = [(1 << 20) // math.isqrt(standing ** lean) + 1 for standing in range(2, number_of + 1)]
    rest, holding = total - reach - (number_of - 1), [1] * (number_of - 1)
    while rest > 0:
        movable = [i for i in range(number_of - 1) if holding[i] < reach]
        whole, remaining = sum([portions[i] for i in movable]), rest
        for i in movable:
            more = min(reach - holding[i], max(1, remaining * portions[i] // whole), rest)
            holding[i] = holding[i] + more
            rest = rest - more
    return np.array([reach] + holding)


def uneven_parts(rng, amount, total, limit, skew):
    if amount == 2:
        one = jax.random.randint(rng, (), max(1, total - limit), min(limit, total - 1) + 1)
        return jnp.stack([one, total - one])
    sizes = jnp.asarray(split_up(amount, total, limit, skew), jnp.int32)
    twos = (amount - 1) // 2
    donor, receiver = sizes[1:1 + 2 * twos:2], sizes[2:2 + 2 * twos:2]
    slack = jnp.minimum(donor - 1, limit - receiver)
    passed = jax.random.randint(jax.random.fold_in(rng, 1), (twos,), 0, 1 << 20) % (slack + 1)
    sizes = sizes.at[1:1 + 2 * twos:2].set(donor - passed).at[2:2 + 2 * twos:2].set(receiver + passed)
    return sizes[jax.random.permutation(jax.random.fold_in(rng, 2), amount)]


def scatter_about(own_key, dims, deviation, most, cuts=(), kind=jnp.bfloat16):
    loudness = levels(own_key, dims, cuts, -0.22, 0.18) if cuts else 1.0
    entries = jax.random.normal(own_key, dims, jnp.float32) * deviation * loudness
    return jnp.minimum(jnp.maximum(entries, -most), most).astype(kind)


def setup_inputs(seed: int = 0) -> dict:
    splits = jax.random.split(jax.random.key(seed), 13)
    queries = draw_queries(jax.random.fold_in(splits[12], 71), 0)
    keys = draw_keys(jax.random.fold_in(splits[12], 71), 0)
    values = scatter_about(splits[2], (TOKENS, WIDTH), 1.0, 6.0, ((0, 32),))
    text_kv = scatter_about(splits[3], (CLIPS, TEXT_LEN, 2, WIDTH), 1.0, 6.0, ((0, 8), (3, 4)))
    text_lengths = plant(jax.random.randint(splits[4], (CLIPS,), 1, TEXT_LEN + 1), jax.random.fold_in(splits[4], 1), 1, TEXT_LEN).astype(jnp.int32)
    clip_lengths = jax.vmap(lambda own: uneven_parts(own, CLIPS_GRP, GRP_TOK, CLIP_MOST, 2))(jax.random.split(splits[5], GROUPS)).reshape((GROUPS, CLIPS_GRP)).astype(jnp.int32)
    timesteps = plant(jax.random.randint(splits[6], (CLIPS,), 0, STEPS), jax.random.fold_in(splits[6], 1), 0, STEPS - 1).astype(jnp.int32)
    mod_weight = scatter_about(splits[7], (FREQ, 2 * WIDTH), FREQ ** -0.5, 0.375)
    final_weight = scatter_about(splits[8], (WIDTH, CHANNELS), WIDTH ** -0.5, 0.125)
    noise = scatter_about(splits[9], (TOKENS, CHANNELS), 1.0, 6.0, ((0, 32),), jnp.float32)
    clean = draw_clean(jax.random.fold_in(splits[12], 71), 0)
    report_order = jax.random.permutation(splits[11], CLIPS).astype(jnp.int32)
    return dict(queries=queries, keys=keys, values=values, text_kv=text_kv, text_lengths=text_lengths, clip_lengths=clip_lengths, timesteps=timesteps, mod_weight=mod_weight, final_weight=final_weight, noise=noise, clean=clean, report_order=report_order)


def step_embedding(timesteps):
    half_width = FREQ // 2
    frequency = jnp.exp(-math.log(10000.0) * jnp.arange(half_width, dtype=jnp.float32) / half_width)
    angles = timesteps.astype(jnp.float32)[:, None] * frequency[None, :]
    return jnp.concatenate([jnp.cos(angles), jnp.sin(angles)], axis=1)

def reference(queries, keys, values, text_kv, text_lengths, clip_lengths, timesteps, mod_weight, final_weight, noise, clean, report_order):
    group_rows = TOK_DEV * N_SEQ
    feat_width = HEADS * HEAD_DIM
    inverse_root = 1.0 / math.sqrt(HEAD_DIM)
    activated = jax.nn.silu(step_embedding(timesteps)).astype(jnp.bfloat16)
    modulation = jnp.dot(activated, mod_weight, preferred_element_type=jnp.float32)
    weight_full = final_weight.astype(jnp.float32)

    def one_group(group_rank):
        group_rank = group_rank.astype(jnp.int32)
        lengths = clip_lengths[group_rank]
        clip_ends = jnp.cumsum(lengths).astype(jnp.int32)
        places = jnp.arange(group_rows, dtype=jnp.int32)
        clip_of = lax.optimization_barrier(jnp.sum((places[:, None] >= clip_ends[None, :]).astype(jnp.int32), axis=1))
        first_row = (group_rank * group_rows).astype(jnp.int32)
        first_clip = (group_rank * CLIPS_GRP).astype(jnp.int32)
        query_rows = lax.dynamic_slice_in_dim(queries, first_row, group_rows, 0)
        key_rows = lax.dynamic_slice_in_dim(keys, first_row, group_rows, 0)
        value_rows = lax.dynamic_slice_in_dim(values, first_row, group_rows, 0)
        text_rows = lax.dynamic_slice_in_dim(text_kv, first_clip, CLIPS_GRP, 0)
        text_count = lax.dynamic_slice_in_dim(text_lengths, first_clip, CLIPS_GRP, 0)
        text_slots = jnp.arange(CLIPS_GRP * TEXT_LEN, dtype=jnp.int32)
        text_clip = text_slots // TEXT_LEN
        text_live = text_slots % TEXT_LEN < text_count[text_clip]
        live_mask = jnp.concatenate([clip_of[:, None] == clip_of[None, :], (clip_of[:, None] == text_clip[None, :]) & text_live[None, :]], axis=1)
        keys_all = jnp.concatenate([key_rows, text_rows[:, :, 0, :].reshape(CLIPS_GRP * TEXT_LEN, feat_width)], axis=0)
        values_all = jnp.concatenate([value_rows, text_rows[:, :, 1, :].reshape(CLIPS_GRP * TEXT_LEN, feat_width)], axis=0)
        query_split = query_rows.reshape(group_rows, HEADS, HEAD_DIM).transpose(1, 0, 2)
        key_split = keys_all.reshape(-1, HEADS, HEAD_DIM).transpose(1, 0, 2)
        value_split = values_all.reshape(-1, HEADS, HEAD_DIM).transpose(1, 0, 2)

        def one_head(items):
            query_head, key_head, value_head = items
            score_rows = jnp.dot(query_head, key_head.T, preferred_element_type=jnp.float32) * inverse_root
            score_rows = jnp.where(live_mask, score_rows, -jnp.inf)
            row_top = lax.optimization_barrier(jnp.max(score_rows, axis=1, keepdims=True))
            weights = jnp.exp(score_rows - row_top)
            weights = (weights / lax.optimization_barrier(jnp.sum(weights, axis=1, keepdims=True))).astype(jnp.bfloat16)
            return jnp.dot(weights, value_head, preferred_element_type=jnp.float32).astype(jnp.bfloat16)
        head_out = lax.map(one_head, (query_split, key_split, value_split))
        attended = head_out.transpose(1, 0, 2).reshape(group_rows, feat_width)
        values_full = attended.astype(jnp.float32)
        center = lax.optimization_barrier(jnp.mean(values_full, axis=1, keepdims=True))
        spread = lax.optimization_barrier(jnp.mean(values_full * values_full, axis=1, keepdims=True)) - center * center
        normed = (values_full - center) * lax.rsqrt(spread + 1e-06)
        group_mods = lax.dynamic_slice_in_dim(modulation, first_clip, CLIPS_GRP, 0)[clip_of]
        modulated = normed * (1.0 + group_mods[:, feat_width:]) + group_mods[:, :feat_width]
        predicted = jnp.dot(modulated, weight_full, precision=lax.Precision.HIGHEST)
        target = lax.dynamic_slice_in_dim(noise, first_row, group_rows, 0) - lax.dynamic_slice_in_dim(clean, first_row, group_rows, 0)
        difference = predicted - target
        error_rows = lax.optimization_barrier(jnp.mean(difference * difference, axis=1))
        token_picks = clip_of[:, None] == jnp.arange(CLIPS_GRP, dtype=jnp.int32)[None, :]
        clip_totals = lax.optimization_barrier(jnp.sum(jnp.where(token_picks, error_rows[:, None], 0.0), axis=0))
        return clip_totals / lengths.astype(jnp.float32)
    clip_loss = lax.map(one_group, jnp.arange(N_DP, dtype=jnp.int32)).reshape(-1)
    return clip_loss[report_order]
```

```python
import functools
import math

import jax
import jax.numpy as jnp
from jax import lax
from jax.experimental import pallas as pl
from jax.experimental.pallas import tpu as pltpu
from jax.sharding import PartitionSpec as P

HEAD_DIM = 128
FREQ = 256
EPS = 1e-06
NEG = -1e30
STAT_ROWS = 8
ALIGN = 16
F32 = jnp.float32
BF16 = jnp.bfloat16
EXACT = lax.Precision.HIGHEST
VMEM_LIMIT = 32 * 1024 * 1024
SCORE_SCALE = math.log2(math.e) / math.sqrt(HEAD_DIM)


def nt_dot(a, b, precision=None):
    return lax.dot_general(a, b, (((1,), (1,)), ((), ())), precision=precision, preferred_element_type=F32)


def two_parts(x):
    high = x.astype(BF16)
    return high, (x - high.astype(F32)).astype(BF16)


def head_cols(h):
    return slice(h * HEAD_DIM, (h + 1) * HEAD_DIM)


def step_embedding(timesteps):
    half_width = FREQ // 2
    frequency = jnp.exp(-math.log(10000.0) * jnp.arange(half_width, dtype=F32) / half_width)
    angles = timesteps.astype(F32)[:, None] * frequency[None, :]
    return jnp.concatenate([jnp.cos(angles), jnp.sin(angles)], axis=1)


def clip_index(info_ref, clips, shape, axis, first):
    places = lax.broadcasted_iota(jnp.int32, shape, axis) + first
    end = jnp.int32(0)
    index = jnp.zeros(shape, jnp.int32)
    for c in range(clips):
        end = end + info_ref[c]
        index = index + (places >= end).astype(jnp.int32)
    return index


def source_rows(sources, k, tok_dev):
    source = lax.rem(lax.axis_index("seq") + sources - k, sources)
    return pl.ds(pl.multiple_of(source * tok_dev, tok_dev), tok_dev)


def cut_kernel(sources, count, *refs):
    wholes, pieces, sems = refs[:count], refs[count:-1], refs[-1]
    local = pieces[0].shape[2]
    copies = []
    for k in [*range(1, sources), 0]:
        target = lax.rem(lax.axis_index("seq") + k, sources)
        for i in range(count):
            copies.append(
                pltpu.make_async_copy(
                    wholes[i].at[:, pl.ds(pl.multiple_of(target * local, HEAD_DIM), local)],
                    pieces[k].at[i],
                    sems.at[k * count + i],
                )
            )
            copies[-1].start()
    for copy in copies:
        copy.wait()


def prep_kernel(
    clips, info_ref, act_ref, mod_hbm, wt_hbm, noise_hbm, clean_hbm, kv_hbm,
    scale_ref, slope_ref, offset_ref, share_ref, weight_ref, keys_ref, values_ref,
    mods, mod_buf, wt_buf, noise_buf, clean_buf, kv_buf, sems,
):
    width = wt_buf.shape[1]
    group_rows, local = scale_ref.shape
    tok_dev = noise_buf.shape[1]
    rank = lax.axis_index("seq")
    pairs = [(mod_hbm, mod_buf), (wt_hbm, wt_buf), (noise_hbm, noise_buf), (clean_hbm, clean_buf)]
    pairs += [(kv_hbm.at[c], kv_buf.at[c]) for c in range(clips)]
    copies = [pltpu.make_async_copy(a, b, sems.at[i]) for i, (a, b) in enumerate(pairs)]
    for copy in copies:
        copy.start()
    for copy in copies[:4]:
        copy.wait()
    mods[...] = jnp.dot(act_ref[...], mod_buf[...], preferred_element_type=F32)
    scales = 1.0 + mods[:, width:]
    weight = wt_buf[...].astype(F32)
    slopes = nt_dot(weight, scales, EXACT)
    shifts = nt_dot(weight, mods[:, :width], EXACT)
    tok_clip = clip_index(info_ref, clips, (clips, tok_dev), 1, rank * tok_dev)
    picks = (tok_clip == lax.broadcasted_iota(jnp.int32, (clips, tok_dev), 0)).astype(F32)
    slot = lax.broadcasted_iota(jnp.int32, (clips, 1), 0)
    sizes = jnp.zeros((clips, 1), F32)
    for c in range(clips):
        sizes = jnp.where(slot == c, info_ref[c].astype(F32), sizes)
    share_ref[...] = picks / sizes
    slope_ref[...] = jnp.dot(slopes, picks, precision=EXACT, preferred_element_type=F32)
    offset_ref[...] = jnp.dot(shifts, picks, precision=EXACT, preferred_element_type=F32) - (
        noise_buf[...] - clean_buf[...]
    )
    row_clip = clip_index(info_ref, clips, (group_rows, clips), 0, 0)
    row_picks = (row_clip == lax.broadcasted_iota(jnp.int32, (group_rows, clips), 1)).astype(F32)
    mine = 1.0 + mods[:, pl.ds(pl.multiple_of(width + rank * local, HEAD_DIM), local)]
    scale_ref[...] = jnp.dot(row_picks, mine, precision=EXACT, preferred_element_type=F32)
    weight_ref[...] = wt_buf[:, pl.ds(pl.multiple_of(rank * local, HEAD_DIM), local)]
    for c in range(clips):
        copies[4 + c].wait()
        keys_ref[c] = kv_buf[c, :, 0, :]
        values_ref[c] = kv_buf[c, :, 1, :]


def text_kernel(sources, clips, window, info_ref, *refs):
    qk_refs = refs[:sources]
    keys_ref, values_ref, out_ref, level_ref, q_all = refs[sources:]
    tok_dev, local = qk_refs[0].shape[1:]
    heads = local // HEAD_DIM
    text_len = keys_ref.shape[1]
    for k, qk_ref in enumerate(qk_refs):
        q_all[source_rows(sources, k, tok_dev), :] = qk_ref[0]
    slots = lax.broadcasted_iota(jnp.int32, (1, text_len), 1)
    ones = jnp.ones((text_len, HEAD_DIM), BF16)

    def one_clip(clip, start):
        first = pl.multiple_of(start // ALIGN * ALIGN, ALIGN)
        rows = pl.ds(first, window)
        edge = pl.ds(first, ALIGN)
        live = slots < info_ref[clips + clip]
        before = lax.broadcasted_iota(jnp.int32, (ALIGN, 1), 0) + first < start
        kept = [(out_ref[edge, head_cols(h)], level_ref[h, edge, :]) for h in range(heads)]
        scores = [nt_dot(q_all[rows, head_cols(h)], keys_ref[clip, :, head_cols(h)]) for h in range(heads)]
        weights, tops = [], []
        for score in scores:
            score = jnp.where(live, score, NEG)
            top = jnp.max(score, axis=1, keepdims=True)
            weights.append(jnp.exp2((score - top) * SCORE_SCALE).astype(BF16))
            tops.append(top)
        results = []
        for h in range(heads):
            beside = jnp.concatenate([values_ref[clip, :, head_cols(h)], ones], axis=1)
            mixed = jnp.dot(weights[h], beside, preferred_element_type=F32)
            total = mixed[:, HEAD_DIM:]
            results.append((mixed[:, :HEAD_DIM] / total, tops[h] * SCORE_SCALE + jnp.log2(total)))
        for h in range(heads):
            out_ref[rows, head_cols(h)] = results[h][0]
            level_ref[h, rows, :] = results[h][1]
            out_ref[edge, head_cols(h)] = jnp.where(before, kept[h][0], results[h][0][:ALIGN])
            level_ref[h, edge, :] = jnp.where(before, kept[h][1], results[h][1][:ALIGN])
        return start + info_ref[clip]

    lax.fori_loop(0, clips, one_clip, jnp.int32(0))


def reach_of(first, reach, group_rows):
    span = group_rows - reach[1]
    return jnp.clip(first - reach[0], 0, span) if span else jnp.int32(0)


def weigh_kernel(sources, clips, reach, info_ref, *refs):
    qk_refs = refs[:sources]
    text_ref, level_ref, weight_ref, base_ref, q_all, k_all = refs[sources:]
    tok_dev, local = qk_refs[0].shape[1:]
    group_rows = q_all.shape[0]
    heads = local // HEAD_DIM
    for k in range(sources):
        rows = source_rows(sources, k, tok_dev)
        q_all[rows, :] = qk_refs[k][0]
        k_all[rows, :] = qk_refs[k][1]
    for first in range(0, group_rows, tok_dev):
        low = min(max(first - reach[0], 0), group_rows - reach[1])
        rows, span = slice(first, first + tok_dev), slice(low, low + reach[1])
        row_clip = clip_index(info_ref, clips, (tok_dev, 1), 0, first)
        live = row_clip == clip_index(info_ref, clips, (1, reach[1]), 1, low)
        scores = [nt_dot(q_all[rows, head_cols(h)], k_all[span, head_cols(h)]) for h in range(heads)]
        for h in range(heads):
            score = jnp.where(live, scores[h] * SCORE_SCALE, NEG)
            level = level_ref[h, rows, :]
            top = jnp.maximum(jnp.max(score, axis=1, keepdims=True), level)
            chunks = [slice(part, part + HEAD_DIM) for part in range(0, reach[1], HEAD_DIM)]
            weights = [jnp.exp2(score[:, cols] - top) for cols in chunks]
            fade = jnp.exp2(level - top)
            share = 1.0 / (jnp.sum(sum(weights[1:], weights[0]), axis=1, keepdims=True) + fade)
            for cols, weight in zip(chunks, weights):
                weight_ref[h, rows, cols] = (weight * share).astype(BF16)
            base_ref[rows, head_cols(h)] = (fade * share) * text_ref[rows, head_cols(h)]


def mix_kernel(sources, reach, ahead, *refs):
    v_refs = refs[:sources]
    weight_ref, base_ref, scale_ref, wt_ref, out_ref, v_all = refs[sources:]
    tok_dev, local = v_refs[0].shape[1:]
    group_rows = scale_ref.shape[0]
    heads = local // HEAD_DIM
    channels = wt_ref.shape[0]
    for k in range(sources):
        v_all[source_rows(sources, k, tok_dev), :] = v_refs[k][0]
    first = pl.multiple_of(lax.rem(lax.axis_index("seq") + ahead, sources) * tok_dev, tok_dev)
    rows = pl.ds(first, tok_dev)
    span = pl.ds(pl.multiple_of(reach_of(first, reach, group_rows), HEAD_DIM), reach[1])
    mixed = [
        jnp.dot(weight_ref[h, rows, :], v_all[span, head_cols(h)], preferred_element_type=F32) for h in range(heads)
    ]
    attended = jnp.concatenate([(mixed[h] + base_ref[rows, head_cols(h)]).astype(BF16) for h in range(heads)], axis=1)
    attended_full = attended.astype(F32)
    y_high, y_low = two_parts(attended_full * scale_ref[rows, :])
    s_high, s_low = two_parts(attended_full * attended_full)
    weight = wt_ref[...]
    every = jnp.ones((STAT_ROWS, local), BF16)
    out_ref[:channels, :] = nt_dot(weight, y_high) + nt_dot(weight, y_low)
    is_sum = lax.broadcasted_iota(jnp.int32, (STAT_ROWS, tok_dev), 0) == 0
    squares = nt_dot(every, s_high) + nt_dot(every, s_low)
    out_ref[channels:, :] = jnp.where(is_sum, nt_dot(every, attended), squares)


def loss_kernel(sources, width, *refs):
    part_refs = refs[:sources]
    slope_ref, offset_ref, share_ref, out_ref = refs[sources:]
    channels = slope_ref.shape[0]
    clips = share_ref.shape[0]
    total = part_refs[0][...]
    for part in part_refs[1:]:
        total = total + part[...]
    center = total[channels : channels + 1, :] * (1.0 / width)
    spread = total[channels + 1 : channels + 2, :] * (1.0 / width) - center * center
    diff = (total[:channels, :] - center * slope_ref[...]) * lax.rsqrt(spread + EPS) + offset_ref[...]
    error = jnp.sum(diff * diff, axis=0, keepdims=True) * (1.0 / channels)
    sums = jnp.sum(share_ref[...] * error, axis=1, keepdims=True)
    lanes = lax.broadcasted_iota(jnp.int32, (clips, out_ref.shape[2]), 1)
    mine = lanes == lax.broadcasted_iota(jnp.int32, lanes.shape, 0)
    row = jnp.sum(jnp.where(mine, sums, 0.0), axis=0, keepdims=True)
    out_ref[...] = jnp.broadcast_to(row[None], out_ref.shape)


def smem():
    return pl.BlockSpec(memory_space=pltpu.SMEM)


def vmem():
    return pl.BlockSpec(memory_space=pltpu.VMEM)


def hbm():
    return pl.BlockSpec(memory_space=pltpu.HBM)


def call(kernel, name, operands, results, scratch=(), scalars=(), in_hbm=(), limit=VMEM_LIMIT, flops=0, traffic=0, exps=0):
    return pl.pallas_call(
        kernel,
        in_specs=[smem()] * len(scalars) + [hbm() if i in in_hbm else vmem() for i in range(len(operands))],
        out_specs=[vmem()] * len(results),
        out_shape=[pltpu.VMEM(*r) for r in results],
        scratch_shapes=list(scratch),
        compiler_params=pltpu.CompilerParams(vmem_limit_bytes=limit),
        cost_estimate=pl.CostEstimate(flops=flops, bytes_accessed=traffic, transcendentals=exps),
        name=name,
    )(*scalars, *(pltpu.with_memory_space_constraint(x, pltpu.HBM) if i in in_hbm else x for i, x in enumerate(operands)))


def per_device(
    queries, keys, values, text_kv, text_lengths, clip_lengths, timesteps, mod_weight, final_weight, noise, clean,
    report_order,
):
    tok_dev, width = queries.shape
    sources = lax.axis_size("seq")
    groups = lax.axis_size("dp")
    local = width // sources
    heads = local // HEAD_DIM
    group_rows = tok_dev * sources
    clips = clip_lengths.shape[1]
    text_len = text_kv.shape[1]
    clip_most = 2 * group_rows // clips
    window = clip_most + ALIGN
    padded = group_rows + window
    reach = (clip_most, min(group_rows, tok_dev + 2 * clip_most))
    channels = final_weight.shape[1]
    info = jnp.concatenate([clip_lengths[0], text_lengths])

    def cut(arrays, name):
        return call(
            functools.partial(cut_kernel, sources, len(arrays)), name, arrays,
            [((len(arrays), tok_dev, local), BF16)] * sources,
            [pltpu.SemaphoreType.DMA((sources * len(arrays),))], in_hbm=range(len(arrays)),
            traffic=4 * tok_dev * width * len(arrays),
        )

    def onward(x, k):
        return lax.ppermute(x, "seq", [(i, (i + k) % sources) for i in range(sources)]) if k else x

    qk_pieces = list(cut([queries, keys], "cut_queries_keys"))
    qk_pieces[0], values = lax.optimization_barrier((qk_pieces[0], values))
    qk_blocks = [onward(piece, k) for k, piece in enumerate(qk_pieces)]
    v_pieces = cut([values], "cut_values")

    weight_t = final_weight.T
    activated = jax.nn.silu(step_embedding(timesteps)).astype(BF16)
    scale_tok, slope, offset, share, weight_local, text_keys, text_values = call(
        functools.partial(prep_kernel, clips), "prep",
        [activated, mod_weight, weight_t, noise.T, clean.T, text_kv],
        [
            ((group_rows, local), F32), ((channels, tok_dev), F32), ((channels, tok_dev), F32), ((clips, tok_dev), F32),
            ((channels, local), BF16), ((clips, text_len, local), BF16), ((clips, text_len, local), BF16),
        ],
        [
            pltpu.VMEM((clips, 2 * width), F32), pltpu.VMEM(mod_weight.shape, BF16),
            pltpu.VMEM(weight_t.shape, BF16), pltpu.VMEM((channels, tok_dev), F32),
            pltpu.VMEM((channels, tok_dev), F32), pltpu.VMEM(text_kv.shape, BF16),
            pltpu.SemaphoreType.DMA((4 + clips,)),
        ],
        scalars=[info], in_hbm=range(1, 6),
    )

    v_pieces, scale_tok = lax.optimization_barrier((v_pieces, scale_tok))
    v_blocks = [onward(piece, k) for k, piece in enumerate(v_pieces)]

    text_out, level = call(
        functools.partial(text_kernel, sources, clips, window), "text", [*qk_blocks, text_keys, text_values],
        [((padded, local), F32), ((heads, padded, HEAD_DIM), F32)],
        [pltpu.VMEM((padded, local), BF16)], scalars=[info],
    )

    weights, base = call(
        functools.partial(weigh_kernel, sources, clips, reach), "weigh", [*qk_blocks, text_out, level],
        [((heads, group_rows, reach[1]), BF16), ((group_rows, local), F32)],
        [pltpu.VMEM((group_rows, local), BF16)] * 2, scalars=[info],
    )

    parts = [None] * sources
    for k in [*range(1, sources), 0]:
        (part,) = call(
            functools.partial(mix_kernel, sources, reach, k), "mix",
            [*v_blocks, weights, base, scale_tok, weight_local], [((channels + STAT_ROWS, tok_dev), F32)],
            [pltpu.VMEM((group_rows, local), BF16)], flops=4 * tok_dev * reach[1] * local, traffic=2**20,
        )
        parts[k] = onward(part, k)

    (shares,) = call(
        functools.partial(loss_kernel, sources, width), "loss", [*parts, slope, offset, share],
        [((groups * sources, 1, HEAD_DIM), F32)],
    )
    everyone = lax.all_to_all(shares, ("dp", "seq"), split_axis=0, concat_axis=0, tiled=True)
    losses = jnp.sum(everyone.reshape(groups, sources, HEAD_DIM), axis=1)[:, :clips].reshape(1, -1)
    slots = jnp.arange(groups * clips, dtype=jnp.int32)
    return jnp.sum(jnp.where(report_order[:, None] == slots[None, :], losses, 0.0), axis=1)


def solution(mesh):
    in_specs = (
        P(("dp", "seq"), None),
        P(("dp", "seq"), None),
        P(("dp", "seq"), None),
        P("dp", None, None, "seq"),
        P("dp"),
        P("dp", None),
        P("dp"),
        P(),
        P(),
        P(("dp", "seq"), None),
        P(("dp", "seq"), None),
        P("dp"),
    )
    return jax.shard_map(per_device, mesh=mesh, in_specs=in_specs, out_specs=P("dp"), check_vma=False)
```

```python
import functools
import math

import jax
import jax.numpy as jnp
from jax import lax
from jax.experimental import pallas as pl
from jax.experimental.pallas import tpu as pltpu
from jax.sharding import PartitionSpec as P

HEAD_DIM = 128
FREQ = 256
EPS = 1e-06
NEG = -1e30
STAT_ROWS = 8
ALIGN = 16
NEAR = 2
F32 = jnp.float32
BF16 = jnp.bfloat16
EXACT = lax.Precision.HIGHEST
VMEM_LIMIT = 32 * 1024 * 1024
SCORE_SCALE = math.log2(math.e) / math.sqrt(HEAD_DIM)


def nt_dot(a, b, precision=None):
    return lax.dot_general(a, b, (((1,), (1,)), ((), ())), precision=precision, preferred_element_type=F32)


def two_parts(x):
    high = x.astype(BF16)
    return high, (x - high.astype(F32)).astype(BF16)


def head_cols(h):
    return slice(h * HEAD_DIM, (h + 1) * HEAD_DIM)


def step_embedding(timesteps):
    half_width = FREQ // 2
    frequency = jnp.exp(-math.log(10000.0) * jnp.arange(half_width, dtype=F32) / half_width)
    angles = timesteps.astype(F32)[:, None] * frequency[None, :]
    return jnp.concatenate([jnp.cos(angles), jnp.sin(angles)], axis=1)


def clip_index(info_ref, clips, shape, axis, first):
    places = lax.broadcasted_iota(jnp.int32, shape, axis) + first
    end = jnp.int32(0)
    index = jnp.zeros(shape, jnp.int32)
    for c in range(clips):
        end = end + info_ref[c]
        index = index + (places >= end).astype(jnp.int32)
    return index


def partner(rank, k, size):
    return rank ^ k if size & (size - 1) == 0 else (rank + k) % size


def source_rows(sources, k, tok_dev):
    rank = lax.axis_index("seq")
    source = partner(rank, k if sources & (sources - 1) == 0 else sources - k, sources)
    return pl.ds(pl.multiple_of(source * tok_dev, tok_dev), tok_dev)


def summed_here(rank, sources, tok_dev):
    if sources != 4:
        return rank * tok_dev, tok_dev, True
    return rank // 2 * 2 * tok_dev, 2 * tok_dev, (rank == 1) | (rank == 2)


def cut_kernel(sources, plan, *refs):
    count = len(refs) - 1 - len(plan)
    wholes, pieces, sems = refs[:count], refs[count:-1], refs[-1]
    local = pieces[0].shape[2]
    copies = []
    for (k, which), piece in zip(plan, pieces):
        target = partner(lax.axis_index("seq"), k, sources)
        for place, i in enumerate(which):
            columns = pl.ds(pl.multiple_of(target * local, HEAD_DIM), local)
            copies.append(pltpu.make_async_copy(wholes[i].at[:, columns], piece.at[place], sems.at[len(copies)]))
            copies[-1].start()
    for copy in copies:
        copy.wait()


def prep_kernel(
    sources, clips, info_ref, act_ref, mod_hbm, wt_hbm, noise_hbm, clean_hbm, kv_hbm,
    scale_ref, slope_ref, shift_ref, share_ref, target_ref, weight_ref, keys_ref, values_ref,
    mods, mod_buf, wt_buf, noise_buf, clean_buf, kv_buf, sems,
):
    width = wt_buf.shape[1]
    group_rows, local = scale_ref.shape
    tok_dev = noise_buf.shape[1]
    rank = lax.axis_index("seq")
    pairs = [(mod_hbm, mod_buf), (wt_hbm, wt_buf), (noise_hbm, noise_buf), (clean_hbm, clean_buf)]
    pairs += [(kv_hbm.at[c], kv_buf.at[c]) for c in range(clips)]
    copies = [pltpu.make_async_copy(a, b, sems.at[i]) for i, (a, b) in enumerate(pairs)]
    for copy in copies:
        copy.start()
    for copy in copies[:4]:
        copy.wait()
    mods[...] = jnp.dot(act_ref[...], mod_buf[...], preferred_element_type=F32)
    scales = 1.0 + mods[:, width:]
    weight = wt_buf[...].astype(F32)
    slopes = nt_dot(weight, scales, EXACT)
    shifts = nt_dot(weight, mods[:, :width], EXACT)
    first, count, active = summed_here(rank, sources, tok_dev)
    tok_clip = clip_index(info_ref, clips, (clips, count), 1, first)
    picks = (tok_clip == lax.broadcasted_iota(jnp.int32, (clips, count), 0)).astype(F32)
    slot = lax.broadcasted_iota(jnp.int32, (clips, 1), 0)
    sizes = jnp.zeros((clips, 1), F32)
    for c in range(clips):
        sizes = jnp.where(slot == c, info_ref[c].astype(F32), sizes)
    share_ref[...] = jnp.where(active, picks / sizes, 0.0)
    slope_ref[...] = jnp.dot(slopes, picks, precision=EXACT, preferred_element_type=F32)
    shift_ref[...] = jnp.dot(shifts, picks, precision=EXACT, preferred_element_type=F32)
    target_ref[...] = noise_buf[...] - clean_buf[...]
    row_clip = clip_index(info_ref, clips, (group_rows, clips), 0, 0)
    row_picks = (row_clip == lax.broadcasted_iota(jnp.int32, (group_rows, clips), 1)).astype(F32)
    mine = 1.0 + mods[:, pl.ds(pl.multiple_of(width + rank * local, HEAD_DIM), local)]
    scale_ref[...] = jnp.dot(row_picks, mine, precision=EXACT, preferred_element_type=F32)
    weight_ref[...] = wt_buf[:, pl.ds(pl.multiple_of(rank * local, HEAD_DIM), local)]
    for c in range(clips):
        copies[4 + c].wait()
        keys_ref[c] = kv_buf[c, :, 0, :]
        values_ref[c] = kv_buf[c, :, 1, :]


def text_kernel(sources, clips, window, info_ref, *refs):
    q_refs = refs[:sources]
    keys_ref, values_ref, out_ref, level_ref, q_all = refs[sources:]
    tok_dev, local = q_refs[0].shape[1:]
    heads = local // HEAD_DIM
    text_len = keys_ref.shape[1]
    for k, q_ref in enumerate(q_refs):
        q_all[source_rows(sources, k, tok_dev), :] = q_ref[0]
    slots = lax.broadcasted_iota(jnp.int32, (1, text_len), 1)
    ones = jnp.ones((text_len, HEAD_DIM), BF16)

    def one_clip(clip, start):
        first = pl.multiple_of(start // ALIGN * ALIGN, ALIGN)
        rows = pl.ds(first, window)
        edge = pl.ds(first, ALIGN)
        live = slots < info_ref[clips + clip]
        before = lax.broadcasted_iota(jnp.int32, (ALIGN, 1), 0) + first < start
        kept = [(out_ref[edge, head_cols(h)], level_ref[h, edge, :]) for h in range(heads)]
        scores = [nt_dot(q_all[rows, head_cols(h)], keys_ref[clip, :, head_cols(h)]) for h in range(heads)]
        weights, tops = [], []
        for score in scores:
            score = jnp.where(live, score, NEG)
            top = jnp.max(score, axis=1, keepdims=True)
            weights.append(jnp.exp2((score - top) * SCORE_SCALE).astype(BF16))
            tops.append(top)
        results = []
        for h in range(heads):
            beside = jnp.concatenate([values_ref[clip, :, head_cols(h)], ones], axis=1)
            mixed = jnp.dot(weights[h], beside, preferred_element_type=F32)
            total = mixed[:, HEAD_DIM:]
            results.append((mixed[:, :HEAD_DIM] / total, tops[h] * SCORE_SCALE + jnp.log2(total)))
        for h in range(heads):
            out_ref[rows, head_cols(h)] = results[h][0]
            level_ref[h, rows, :] = results[h][1]
            out_ref[edge, head_cols(h)] = jnp.where(before, kept[h][0], results[h][0][:ALIGN])
            level_ref[h, edge, :] = jnp.where(before, kept[h][1], results[h][1][:ALIGN])
        return start + info_ref[clip]

    lax.fori_loop(0, clips, one_clip, jnp.int32(0))


def reach_of(first, reach, group_rows):
    span = group_rows - reach[1]
    return jnp.clip(first - reach[0], 0, span) if span else jnp.int32(0)


def weigh_kernel(sources, clips, reach, info_ref, *refs):
    q_refs, kv_refs = refs[:sources], refs[sources : 2 * sources - NEAR]
    text_ref, level_ref, weight_ref, base_ref, q_all, k_all = refs[2 * sources - NEAR :]
    tok_dev, local = q_refs[0].shape[1:]
    group_rows = q_all.shape[0]
    heads = local // HEAD_DIM
    for k in range(sources):
        rows = source_rows(sources, k, tok_dev)
        q_all[rows, :] = q_refs[k][0]
        k_all[rows, :] = q_refs[k][1] if k < NEAR else kv_refs[k - NEAR][0]
    for first in range(0, group_rows, tok_dev):
        low = min(max(first - reach[0], 0), group_rows - reach[1])
        rows, span = slice(first, first + tok_dev), slice(low, low + reach[1])
        row_clip = clip_index(info_ref, clips, (tok_dev, 1), 0, first)
        live = row_clip == clip_index(info_ref, clips, (1, reach[1]), 1, low)
        scores = [nt_dot(q_all[rows, head_cols(h)], k_all[span, head_cols(h)]) for h in range(heads)]
        for h in range(heads):
            score = jnp.where(live, scores[h] * SCORE_SCALE, NEG)
            level = level_ref[h, rows, :]
            top = jnp.maximum(jnp.max(score, axis=1, keepdims=True), level)
            chunks = [slice(part, part + HEAD_DIM) for part in range(0, reach[1], HEAD_DIM)]
            weights = [jnp.exp2(score[:, cols] - top) for cols in chunks]
            fade = jnp.exp2(level - top)
            share = 1.0 / (jnp.sum(sum(weights[1:], weights[0]), axis=1, keepdims=True) + fade)
            for cols, weight in zip(chunks, weights):
                weight_ref[h, rows, cols] = (weight * share).astype(BF16)
            base_ref[rows, head_cols(h)] = (fade * share) * text_ref[rows, head_cols(h)]


def mix_kernel(sources, reach, place, *refs):
    v_refs = refs[:sources]
    weight_ref, base_ref, scale_ref, wt_ref, out_ref, v_all = refs[sources:]
    tok_dev, local = v_refs[0].shape[1:]
    group_rows = scale_ref.shape[0]
    heads = local // HEAD_DIM
    channels = wt_ref.shape[0]
    for k in range(sources):
        v_all[source_rows(sources, k, tok_dev), :] = v_refs[k][2 if k < NEAR else 1]
    count = out_ref.shape[1]
    first = pl.multiple_of(place(lax.axis_index("seq")) * tok_dev, tok_dev)
    rows = pl.ds(first, count)
    span = pl.ds(pl.multiple_of(reach_of(first, reach, group_rows), HEAD_DIM), reach[1])
    mixed = [
        jnp.dot(weight_ref[h, rows, :], v_all[span, head_cols(h)], preferred_element_type=F32) for h in range(heads)
    ]
    attended = jnp.concatenate([(mixed[h] + base_ref[rows, head_cols(h)]).astype(BF16) for h in range(heads)], axis=1)
    attended_full = attended.astype(F32)
    y_high, y_low = two_parts(attended_full * scale_ref[rows, :])
    s_high, s_low = two_parts(attended_full * attended_full)
    weight = wt_ref[...]
    every = jnp.ones((STAT_ROWS, local), BF16)
    out_ref[:channels, :] = nt_dot(weight, y_high) + nt_dot(weight, y_low)
    is_sum = lax.broadcasted_iota(jnp.int32, (STAT_ROWS, count), 0) == 0
    squares = nt_dot(every, s_high) + nt_dot(every, s_low)
    out_ref[channels:, :] = jnp.where(is_sum, nt_dot(every, attended), squares)


def loss_kernel(count, width, *refs):
    part_refs = refs[:count]
    slope_ref, shift_ref, share_ref, *target_refs, out_ref = refs[count:]
    channels = slope_ref.shape[0]
    clips = share_ref.shape[0]
    total = part_refs[0][...]
    for part in part_refs[1:]:
        total = total + part[...]
    targets = [target[...] for target in target_refs]
    if len(targets) == 2:
        swap = lax.axis_index("seq") == 1
        targets = [jnp.where(swap, *targets[::-1]), jnp.where(swap, *targets)]
    offset = shift_ref[...] - jnp.concatenate(targets, axis=1)
    center = total[channels : channels + 1, :] * (1.0 / width)
    spread = total[channels + 1 : channels + 2, :] * (1.0 / width) - center * center
    diff = (total[:channels, :] - center * slope_ref[...]) * lax.rsqrt(spread + EPS) + offset
    error = jnp.sum(diff * diff, axis=0, keepdims=True) * (1.0 / channels)
    share = share_ref[...]
    sums = jnp.sum(jnp.where(share > 0.0, share * error, 0.0), axis=1, keepdims=True)
    lanes = lax.broadcasted_iota(jnp.int32, (clips, out_ref.shape[2]), 1)
    mine = lanes == lax.broadcasted_iota(jnp.int32, lanes.shape, 0)
    row = jnp.sum(jnp.where(mine, sums, 0.0), axis=0, keepdims=True)
    out_ref[...] = jnp.broadcast_to(row[None], out_ref.shape)


def smem():
    return pl.BlockSpec(memory_space=pltpu.SMEM)


def vmem():
    return pl.BlockSpec(memory_space=pltpu.VMEM)


def hbm():
    return pl.BlockSpec(memory_space=pltpu.HBM)


def call(kernel, name, operands, results, scratch=(), scalars=(), in_hbm=(), limit=VMEM_LIMIT, flops=0, traffic=0, exps=0):
    return pl.pallas_call(
        kernel,
        in_specs=[smem()] * len(scalars) + [hbm() if i in in_hbm else vmem() for i in range(len(operands))],
        out_specs=[vmem()] * len(results),
        out_shape=[pltpu.VMEM(*r) for r in results],
        scratch_shapes=list(scratch),
        compiler_params=pltpu.CompilerParams(vmem_limit_bytes=limit),
        cost_estimate=pl.CostEstimate(flops=flops, bytes_accessed=traffic, transcendentals=exps),
        name=name,
    )(*scalars, *(pltpu.with_memory_space_constraint(x, pltpu.HBM) if i in in_hbm else x for i, x in enumerate(operands)))


def per_device(
    queries, keys, values, text_kv, text_lengths, clip_lengths, timesteps, mod_weight, final_weight, noise, clean,
    report_order,
):
    tok_dev, width = queries.shape
    sources = lax.axis_size("seq")
    groups = lax.axis_size("dp")
    local = width // sources
    heads = local // HEAD_DIM
    group_rows = tok_dev * sources
    clips = clip_lengths.shape[1]
    text_len = text_kv.shape[1]
    clip_most = 2 * group_rows // clips
    window = clip_most + ALIGN
    padded = group_rows + window
    reach = (clip_most, min(group_rows, tok_dev + 2 * clip_most))
    channels = final_weight.shape[1]
    info = jnp.concatenate([clip_lengths[0], text_lengths])

    def cut(arrays, plan, name):
        count = sum(len(which) for _, which in plan)
        return list(
            call(
                functools.partial(cut_kernel, sources, plan), name, arrays,
                [((len(which), tok_dev, local), BF16) for _, which in plan],
                [pltpu.SemaphoreType.DMA((count,))], in_hbm=range(len(arrays)), traffic=4 * tok_dev * local * count,
            )
        )

    def onward(x, k):
        return lax.ppermute(x, "seq", [(i, partner(i, k, sources)) for i in range(sources)]) if k else x

    far = [*range(NEAR, sources)]
    pieces = cut(
        [queries, keys, values],
        [(k, (0,)) for k in far] + [(k, (0, 1, 2)) for k in reversed(range(NEAR))],
        "cut_first",
    )
    pieces[-1], keys = lax.optimization_barrier((pieces[-1], keys))
    kv_pieces = cut([keys, values], [(k, (0, 1)) for k in far], "cut_far")
    q_blocks = [onward(piece, k) for k, piece in zip(far, pieces)]
    near_blocks = [onward(pieces[-1 - k], k) for k in range(NEAR)]
    q_blocks = near_blocks + q_blocks
    kv_blocks = [onward(piece, k) for k, piece in zip(far, kv_pieces)]

    weight_t = final_weight.T
    activated = jax.nn.silu(step_embedding(timesteps)).astype(BF16)
    _, summed, _ = summed_here(0, sources, tok_dev)
    scale_tok, slope, shift, share, target, weight_local, text_keys, text_values = call(
        functools.partial(prep_kernel, sources, clips), "prep",
        [activated, mod_weight, weight_t, noise.T, clean.T, text_kv],
        [
            ((group_rows, local), F32), ((channels, summed), F32), ((channels, summed), F32), ((clips, summed), F32),
            ((channels, tok_dev), F32),
            ((channels, local), BF16), ((clips, text_len, local), BF16), ((clips, text_len, local), BF16),
        ],
        [
            pltpu.VMEM((clips, 2 * width), F32), pltpu.VMEM(mod_weight.shape, BF16),
            pltpu.VMEM(weight_t.shape, BF16), pltpu.VMEM((channels, tok_dev), F32),
            pltpu.VMEM((channels, tok_dev), F32), pltpu.VMEM(text_kv.shape, BF16),
            pltpu.SemaphoreType.DMA((4 + clips,)),
        ],
        scalars=[info], in_hbm=range(1, 6),
    )

    text_out, level = call(
        functools.partial(text_kernel, sources, clips, window), "text", [*q_blocks, text_keys, text_values],
        [((padded, local), F32), ((heads, padded, HEAD_DIM), F32)],
        [pltpu.VMEM((padded, local), BF16)], scalars=[info],
    )

    targets = [target]
    if sources == 4:
        text_out, moved = lax.optimization_barrier((text_out, lax.ppermute(target, "seq", [(0, 1), (3, 2)])))
        targets.append(moved)

    weights, base = call(
        functools.partial(weigh_kernel, sources, clips, reach), "weigh", [*q_blocks, *kv_blocks, text_out, level],
        [((heads, group_rows, reach[1]), BF16), ((group_rows, local), F32)],
        [pltpu.VMEM((group_rows, local), BF16)] * 2, scalars=[info],
    )

    def mix(place):
        return call(
            functools.partial(mix_kernel, sources, reach, place), "mix",
            [*near_blocks, *kv_blocks, weights, base, scale_tok, weight_local],
            [((channels + STAT_ROWS, summed), F32)],
            [pltpu.VMEM((group_rows, local), BF16)], flops=4 * summed * reach[1] * local, traffic=2**20,
        )[0]

    if sources == 4:
        here = mix(lambda rank: rank // 2 * 2)
        parts = [here, lax.ppermute(here, "seq", [(0, 1), (3, 2)])]
        there = mix(lambda rank: 2 - rank // 2 * 2)
        parts += [lax.ppermute(there, "seq", pairs) for pairs in ([(0, 2), (3, 1)], [(1, 2), (2, 1)])]
    else:
        parts = [onward(mix(lambda rank, k=k: partner(rank, k, sources)), k) for k in reversed(range(sources))]

    (shares,) = call(
        functools.partial(loss_kernel, len(parts), width), "loss", [*parts, slope, shift, share, *targets],
        [((groups * sources, 1, HEAD_DIM), F32)],
    )
    everyone = lax.all_to_all(shares, ("dp", "seq"), split_axis=0, concat_axis=0, tiled=True)
    losses = jnp.sum(everyone.reshape(groups, sources, HEAD_DIM), axis=1)[:, :clips].reshape(1, -1)
    slots = jnp.arange(groups * clips, dtype=jnp.int32)
    return jnp.sum(jnp.where(report_order[:, None] == slots[None, :], losses, 0.0), axis=1)


def solution(mesh):
    in_specs = (
        P(("dp", "seq"), None),
        P(("dp", "seq"), None),
        P(("dp", "seq"), None),
        P("dp", None, None, "seq"),
        P("dp"),
        P("dp", None),
        P("dp"),
        P(),
        P(),
        P(("dp", "seq"), None),
        P(("dp", "seq"), None),
        P("dp"),
    )
    return jax.shard_map(per_device, mesh=mesh, in_specs=in_specs, out_specs=P("dp"), check_vma=False)
```

```python
import functools
import math

import jax
import jax.numpy as jnp
from jax import lax
from jax.experimental import pallas as pl
from jax.experimental.pallas import tpu as pltpu
from jax.sharding import PartitionSpec as P

HEAD_DIM = 128
FREQ = 256
EPS = 1e-06
NEG = -1e30
STAT_ROWS = 8
ALIGN = 16
NEAR = 2
F32 = jnp.float32
BF16 = jnp.bfloat16
EXACT = lax.Precision.HIGHEST
VMEM_LIMIT = 32 * 1024 * 1024
SCORE_SCALE = math.log2(math.e) / math.sqrt(HEAD_DIM)


def nt_dot(a, b, precision=None):
    return lax.dot_general(a, b, (((1,), (1,)), ((), ())), precision=precision, preferred_element_type=F32)


def two_parts(x):
    high = x.astype(BF16)
    return high, (x - high.astype(F32)).astype(BF16)


def head_cols(h):
    return slice(h * HEAD_DIM, (h + 1) * HEAD_DIM)


def step_embedding(timesteps):
    half_width = FREQ // 2
    frequency = jnp.exp(-math.log(10000.0) * jnp.arange(half_width, dtype=F32) / half_width)
    angles = timesteps.astype(F32)[:, None] * frequency[None, :]
    return jnp.concatenate([jnp.cos(angles), jnp.sin(angles)], axis=1)


def clip_index(info_ref, clips, shape, axis, first):
    places = lax.broadcasted_iota(jnp.int32, shape, axis) + first
    end = jnp.int32(0)
    index = jnp.zeros(shape, jnp.int32)
    for c in range(clips):
        end = end + info_ref[c]
        index = index + (places >= end).astype(jnp.int32)
    return index


def partner(rank, k, size):
    return rank ^ k if size & (size - 1) == 0 else (rank + k) % size


def source_rows(sources, k, tok_dev):
    rank = lax.axis_index("seq")
    source = partner(rank, k if sources & (sources - 1) == 0 else sources - k, sources)
    return pl.ds(pl.multiple_of(source * tok_dev, tok_dev), tok_dev)


def summed_here(rank, sources, tok_dev):
    if sources != 4:
        return rank * tok_dev, tok_dev, True
    return rank // 2 * 2 * tok_dev, 2 * tok_dev, (rank == 1) | (rank == 2)


def cut_kernel(sources, plan, *refs):
    count = len(refs) - 1 - len(plan)
    wholes, pieces, sems = refs[:count], refs[count:-1], refs[-1]
    local = pieces[0].shape[2]
    copies = []
    for (k, which), piece in zip(plan, pieces):
        target = partner(lax.axis_index("seq"), k, sources)
        for place, i in enumerate(which):
            columns = pl.ds(pl.multiple_of(target * local, HEAD_DIM), local)
            copies.append(pltpu.make_async_copy(wholes[i].at[:, columns], piece.at[place], sems.at[len(copies)]))
            copies[-1].start()
    for copy in copies:
        copy.wait()


def prep_kernel(
    sources, clips, info_ref, act_ref, mod_hbm, wt_hbm, noise_hbm, clean_hbm, kv_hbm,
    scale_ref, slope_ref, shift_ref, share_ref, target_ref, weight_ref, keys_ref, values_ref,
    mods, mod_buf, wt_buf, noise_buf, clean_buf, kv_buf, sems,
):
    width = wt_buf.shape[1]
    group_rows, local = scale_ref.shape
    tok_dev = noise_buf.shape[1]
    rank = lax.axis_index("seq")
    pairs = [(mod_hbm, mod_buf), (wt_hbm, wt_buf), (noise_hbm, noise_buf), (clean_hbm, clean_buf)]
    pairs += [(kv_hbm.at[c], kv_buf.at[c]) for c in range(clips)]
    copies = [pltpu.make_async_copy(a, b, sems.at[i]) for i, (a, b) in enumerate(pairs)]
    for copy in copies:
        copy.start()
    for copy in copies[:4]:
        copy.wait()
    mods[...] = jnp.dot(act_ref[...], mod_buf[...], preferred_element_type=F32)
    scales = 1.0 + mods[:, width:]
    weight = wt_buf[...].astype(F32)
    slopes = nt_dot(weight, scales, EXACT)
    shifts = nt_dot(weight, mods[:, :width], EXACT)
    first, count, active = summed_here(rank, sources, tok_dev)
    tok_clip = clip_index(info_ref, clips, (clips, count), 1, first)
    picks = (tok_clip == lax.broadcasted_iota(jnp.int32, (clips, count), 0)).astype(F32)
    slot = lax.broadcasted_iota(jnp.int32, (clips, 1), 0)
    sizes = jnp.zeros((clips, 1), F32)
    for c in range(clips):
        sizes = jnp.where(slot == c, info_ref[c].astype(F32), sizes)
    share_ref[...] = jnp.where(active, picks / sizes, 0.0)
    slope_ref[...] = jnp.dot(slopes, picks, precision=EXACT, preferred_element_type=F32)
    shift_ref[...] = jnp.dot(shifts, picks, precision=EXACT, preferred_element_type=F32)
    target_ref[...] = noise_buf[...] - clean_buf[...]
    row_clip = clip_index(info_ref, clips, (group_rows, clips), 0, 0)
    row_picks = (row_clip == lax.broadcasted_iota(jnp.int32, (group_rows, clips), 1)).astype(F32)
    mine = 1.0 + mods[:, pl.ds(pl.multiple_of(width + rank * local, HEAD_DIM), local)]
    scale_ref[...] = jnp.dot(row_picks, mine, precision=EXACT, preferred_element_type=F32)
    weight_ref[...] = wt_buf[:, pl.ds(pl.multiple_of(rank * local, HEAD_DIM), local)]
    for c in range(clips):
        copies[4 + c].wait()
        keys_ref[c] = kv_buf[c, :, 0, :]
        values_ref[c] = kv_buf[c, :, 1, :]


def text_kernel(sources, clips, window, info_ref, *refs):
    q_refs = refs[:sources]
    keys_ref, values_ref, out_ref, level_ref, q_all = refs[sources:]
    tok_dev, local = q_refs[0].shape[1:]
    heads = local // HEAD_DIM
    text_len = keys_ref.shape[1]
    for k, q_ref in enumerate(q_refs):
        q_all[source_rows(sources, k, tok_dev), :] = q_ref[0]
    slots = lax.broadcasted_iota(jnp.int32, (1, text_len), 1)
    ones = jnp.ones((text_len, HEAD_DIM), BF16)

    def one_clip(clip, start):
        first = pl.multiple_of(start // ALIGN * ALIGN, ALIGN)
        rows = pl.ds(first, window)
        edge = pl.ds(first, ALIGN)
        live = slots < info_ref[clips + clip]
        before = lax.broadcasted_iota(jnp.int32, (ALIGN, 1), 0) + first < start
        kept = [(out_ref[edge, head_cols(h)], level_ref[h, edge, :]) for h in range(heads)]
        scores = [nt_dot(q_all[rows, head_cols(h)], keys_ref[clip, :, head_cols(h)]) for h in range(heads)]
        weights, tops = [], []
        for score in scores:
            score = jnp.where(live, score, NEG)
            top = jnp.max(score, axis=1, keepdims=True)
            weights.append(jnp.exp2((score - top) * SCORE_SCALE).astype(BF16))
            tops.append(top)
        results = []
        for h in range(heads):
            beside = jnp.concatenate([values_ref[clip, :, head_cols(h)], ones], axis=1)
            mixed = jnp.dot(weights[h], beside, preferred_element_type=F32)
            total = mixed[:, HEAD_DIM:]
            results.append((mixed[:, :HEAD_DIM] / total, tops[h] * SCORE_SCALE + jnp.log2(total)))
        for h in range(heads):
            out_ref[rows, head_cols(h)] = results[h][0]
            level_ref[h, rows, :] = results[h][1]
            out_ref[edge, head_cols(h)] = jnp.where(before, kept[h][0], results[h][0][:ALIGN])
            level_ref[h, edge, :] = jnp.where(before, kept[h][1], results[h][1][:ALIGN])
        return start + info_ref[clip]

    lax.fori_loop(0, clips, one_clip, jnp.int32(0))


def reach_of(first, reach, group_rows):
    span = group_rows - reach[1]
    return jnp.clip(first - reach[0], 0, span) if span else jnp.int32(0)


def weigh_kernel(sources, clips, reach, info_ref, *refs):
    q_refs, k_refs = refs[:sources], refs[sources : 2 * sources - NEAR]
    text_ref, level_ref, weight_ref, base_ref, q_all, k_all = refs[2 * sources - NEAR :]
    tok_dev, local = q_refs[0].shape[1:]
    group_rows = q_all.shape[0]
    heads = local // HEAD_DIM
    for k in range(sources):
        rows = source_rows(sources, k, tok_dev)
        q_all[rows, :] = q_refs[k][0]
        k_all[rows, :] = q_refs[k][1] if k < NEAR else k_refs[k - NEAR][0]
    for first in range(0, group_rows, tok_dev):
        low = min(max(first - reach[0], 0), group_rows - reach[1])
        rows, span = slice(first, first + tok_dev), slice(low, low + reach[1])
        row_clip = clip_index(info_ref, clips, (tok_dev, 1), 0, first)
        live = row_clip == clip_index(info_ref, clips, (1, reach[1]), 1, low)
        scores = [nt_dot(q_all[rows, head_cols(h)], k_all[span, head_cols(h)]) for h in range(heads)]
        for h in range(heads):
            score = jnp.where(live, scores[h] * SCORE_SCALE, NEG)
            level = level_ref[h, rows, :]
            top = jnp.maximum(jnp.max(score, axis=1, keepdims=True), level)
            chunks = [slice(part, part + HEAD_DIM) for part in range(0, reach[1], HEAD_DIM)]
            weights = [jnp.exp2(score[:, cols] - top) for cols in chunks]
            fade = jnp.exp2(level - top)
            share = 1.0 / (jnp.sum(sum(weights[1:], weights[0]), axis=1, keepdims=True) + fade)
            for cols, weight in zip(chunks, weights):
                weight_ref[h, rows, cols] = (weight * share).astype(BF16)
            base_ref[rows, head_cols(h)] = (fade * share) * text_ref[rows, head_cols(h)]


def mix_kernel(sources, reach, place, *refs):
    v_refs = refs[:sources]
    weight_ref, base_ref, scale_ref, wt_ref, out_ref, v_all = refs[sources:]
    tok_dev, local = v_refs[0].shape[1:]
    group_rows = scale_ref.shape[0]
    heads = local // HEAD_DIM
    channels = wt_ref.shape[0]
    for k in range(sources):
        v_all[source_rows(sources, k, tok_dev), :] = v_refs[k][2 if k < NEAR else 0]
    count = out_ref.shape[1]
    first = pl.multiple_of(place(lax.axis_index("seq")) * tok_dev, tok_dev)
    rows = pl.ds(first, count)
    span = pl.ds(pl.multiple_of(reach_of(first, reach, group_rows), HEAD_DIM), reach[1])
    mixed = [
        jnp.dot(weight_ref[h, rows, :], v_all[span, head_cols(h)], preferred_element_type=F32) for h in range(heads)
    ]
    attended = jnp.concatenate([(mixed[h] + base_ref[rows, head_cols(h)]).astype(BF16) for h in range(heads)], axis=1)
    attended_full = attended.astype(F32)
    y_high, y_low = two_parts(attended_full * scale_ref[rows, :])
    s_high, s_low = two_parts(attended_full * attended_full)
    weight = wt_ref[...]
    every = jnp.ones((STAT_ROWS, local), BF16)
    out_ref[:channels, :] = nt_dot(weight, y_high) + nt_dot(weight, y_low)
    is_sum = lax.broadcasted_iota(jnp.int32, (STAT_ROWS, count), 0) == 0
    squares = nt_dot(every, s_high) + nt_dot(every, s_low)
    out_ref[channels:, :] = jnp.where(is_sum, nt_dot(every, attended), squares)


def loss_kernel(count, width, *refs):
    part_refs = refs[:count]
    slope_ref, shift_ref, share_ref, *target_refs, out_ref = refs[count:]
    channels = slope_ref.shape[0]
    clips = share_ref.shape[0]
    total = part_refs[0][...]
    for part in part_refs[1:]:
        total = total + part[...]
    targets = [target[...] for target in target_refs]
    if len(targets) == 2:
        swap = lax.axis_index("seq") == 1
        targets = [jnp.where(swap, *targets[::-1]), jnp.where(swap, *targets)]
    offset = shift_ref[...] - jnp.concatenate(targets, axis=1)
    center = total[channels : channels + 1, :] * (1.0 / width)
    spread = total[channels + 1 : channels + 2, :] * (1.0 / width) - center * center
    diff = (total[:channels, :] - center * slope_ref[...]) * lax.rsqrt(spread + EPS) + offset
    error = jnp.sum(diff * diff, axis=0, keepdims=True) * (1.0 / channels)
    share = share_ref[...]
    sums = jnp.sum(jnp.where(share > 0.0, share * error, 0.0), axis=1, keepdims=True)
    lanes = lax.broadcasted_iota(jnp.int32, (clips, out_ref.shape[2]), 1)
    mine = lanes == lax.broadcasted_iota(jnp.int32, lanes.shape, 0)
    row = jnp.sum(jnp.where(mine, sums, 0.0), axis=0, keepdims=True)
    out_ref[...] = jnp.broadcast_to(row[None], out_ref.shape)


def smem():
    return pl.BlockSpec(memory_space=pltpu.SMEM)


def vmem():
    return pl.BlockSpec(memory_space=pltpu.VMEM)


def hbm():
    return pl.BlockSpec(memory_space=pltpu.HBM)


def call(kernel, name, operands, results, scratch=(), scalars=(), in_hbm=(), pinned=True, flops=0, traffic=0):
    return pl.pallas_call(
        kernel,
        in_specs=[smem()] * len(scalars) + [hbm() if i in in_hbm else vmem() for i in range(len(operands))],
        out_specs=[vmem()] * len(results),
        out_shape=[pltpu.VMEM(*r) if pinned else jax.ShapeDtypeStruct(*r) for r in results],
        scratch_shapes=list(scratch),
        compiler_params=pltpu.CompilerParams(vmem_limit_bytes=VMEM_LIMIT),
        cost_estimate=pl.CostEstimate(flops=flops, bytes_accessed=traffic, transcendentals=0),
        name=name,
    )(*scalars, *(pltpu.with_memory_space_constraint(x, pltpu.HBM) if i in in_hbm else x for i, x in enumerate(operands)))


def per_device(
    queries, keys, values, text_kv, text_lengths, clip_lengths, timesteps, mod_weight, final_weight, noise, clean,
    report_order,
):
    tok_dev, width = queries.shape
    sources = lax.axis_size("seq")
    groups = lax.axis_size("dp")
    local = width // sources
    heads = local // HEAD_DIM
    group_rows = tok_dev * sources
    clips = clip_lengths.shape[1]
    text_len = text_kv.shape[1]
    clip_most = 2 * group_rows // clips
    window = clip_most + ALIGN
    padded = group_rows + window
    reach = (clip_most, min(group_rows, tok_dev + 2 * clip_most))
    channels = final_weight.shape[1]
    info = jnp.concatenate([clip_lengths[0], text_lengths])

    def cut(arrays, plan, name):
        count = sum(len(which) for _, which in plan)
        return list(
            call(
                functools.partial(cut_kernel, sources, plan), name, arrays,
                [((len(which), tok_dev, local), BF16) for _, which in plan],
                [pltpu.SemaphoreType.DMA((count,))], in_hbm=range(len(arrays)), traffic=4 * tok_dev * local * count,
            )
        )

    def onward(x, k):
        return lax.ppermute(x, "seq", [(i, partner(i, k, sources)) for i in range(sources)]) if k else x

    far = [*range(NEAR, sources)]
    q_pieces = cut([queries], [(k, (0,)) for k in far], "cut_first")
    q_blocks = [onward(piece, k) for k, piece in zip(far, q_pieces)]
    q_pieces[0], keys = lax.optimization_barrier((q_pieces[0], keys))
    pieces = cut(
        [queries, keys, values],
        [(k, (0, 1, 2)) for k in reversed(range(NEAR))] + [(k, (i,)) for i in (1, 2) for k in far],
        "cut_rest",
    )
    near_blocks = [onward(pieces[NEAR - 1 - k], k) for k in range(NEAR)]
    q_blocks = near_blocks + q_blocks
    k_blocks = [onward(piece, k) for k, piece in zip(far, pieces[NEAR:])]

    weight_t = final_weight.T
    activated = jax.nn.silu(step_embedding(timesteps)).astype(BF16)
    _, summed, _ = summed_here(0, sources, tok_dev)
    scale_tok, slope, shift, share, target, weight_local, text_keys, text_values = call(
        functools.partial(prep_kernel, sources, clips), "prep",
        [activated, mod_weight, weight_t, noise.T, clean.T, text_kv],
        [
            ((group_rows, local), F32), ((channels, summed), F32), ((channels, summed), F32), ((clips, summed), F32),
            ((channels, tok_dev), F32),
            ((channels, local), BF16), ((clips, text_len, local), BF16), ((clips, text_len, local), BF16),
        ],
        [
            pltpu.VMEM((clips, 2 * width), F32), pltpu.VMEM(mod_weight.shape, BF16),
            pltpu.VMEM(weight_t.shape, BF16), pltpu.VMEM((channels, tok_dev), F32),
            pltpu.VMEM((channels, tok_dev), F32), pltpu.VMEM(text_kv.shape, BF16),
            pltpu.SemaphoreType.DMA((4 + clips,)),
        ],
        scalars=[info], in_hbm=range(1, 6),
    )

    v_pieces, scale_tok = lax.optimization_barrier((pieces[NEAR + len(far) :], scale_tok))
    v_blocks = [onward(piece, k) for k, piece in zip(far, v_pieces)]

    text_out, level = call(
        functools.partial(text_kernel, sources, clips, window), "text", [*q_blocks, text_keys, text_values],
        [((padded, local), F32), ((heads, padded, HEAD_DIM), F32)],
        [pltpu.VMEM((padded, local), BF16)], scalars=[info],
    )

    swap = [(0, 1), (1, 0), (2, 3), (3, 2)]
    targets = [target]
    if sources == 4:
        text_out, moved = lax.optimization_barrier((text_out, lax.ppermute(target, "seq", swap)))
        targets.append(moved)

    weights, base = call(
        functools.partial(weigh_kernel, sources, clips, reach), "weigh", [*q_blocks, *k_blocks, text_out, level],
        [((heads, group_rows, reach[1]), BF16), ((group_rows, local), F32)],
        [pltpu.VMEM((group_rows, local), BF16)] * 2, scalars=[info],
    )

    def mix(place):
        return call(
            functools.partial(mix_kernel, sources, reach, place), "mix",
            [*near_blocks, *v_blocks, weights, base, scale_tok, weight_local],
            [((channels + STAT_ROWS, summed), F32)],
            [pltpu.VMEM((group_rows, local), BF16)], flops=4 * summed * reach[1] * local, traffic=2**20,
        )[0]

    if sources == 4:
        here = mix(lambda rank: rank // 2 * 2)
        parts = [here, lax.ppermute(here, "seq", swap)]
        there = mix(lambda rank: 2 - rank // 2 * 2)
        for pairs in ([(1, 2), (2, 1), (0, 0), (3, 3)], [(0, 2), (2, 3), (3, 1), (1, 0)]):
            parts.append(lax.ppermute(there, "seq", pairs))
    else:
        parts = [onward(mix(lambda rank, k=k: partner(rank, k, sources)), k) for k in reversed(range(sources))]

    (shares,) = call(
        functools.partial(loss_kernel, len(parts), width), "loss", [*parts, slope, shift, share, *targets],
        [((groups * sources, 1, HEAD_DIM), F32)],
    )
    everyone = lax.all_to_all(shares, ("dp", "seq"), split_axis=0, concat_axis=0, tiled=True)
    losses = jnp.sum(everyone.reshape(groups, sources, HEAD_DIM), axis=1)[:, :clips].reshape(1, -1)
    slots = jnp.arange(groups * clips, dtype=jnp.int32)
    return jnp.sum(jnp.where(report_order[:, None] == slots[None, :], losses, 0.0), axis=1)


def solution(mesh):
    in_specs = (
        P(("dp", "seq"), None),
        P(("dp", "seq"), None),
        P(("dp", "seq"), None),
        P("dp", None, None, "seq"),
        P("dp"),
        P("dp", None),
        P("dp"),
        P(),
        P(),
        P(("dp", "seq"), None),
        P(("dp", "seq"), None),
        P("dp"),
    )
    return jax.shard_map(per_device, mesh=mesh, in_specs=in_specs, out_specs=P("dp"), check_vma=False)
```

```python
import functools
import math

import jax
import jax.numpy as jnp
from jax import lax
from jax.experimental import pallas as pl
from jax.experimental.pallas import tpu as pltpu
from jax.sharding import PartitionSpec as P

HEAD_DIM = 128
FREQ = 256
EPS = 1e-06
NEG = -1e30
STAT_ROWS = 16
ALIGN = 16
NEAR = 2
F32 = jnp.float32
BF16 = jnp.bfloat16
EXACT = lax.Precision.HIGHEST
VMEM_LIMIT = 32 * 1024 * 1024
SCORE_SCALE = math.log2(math.e) / math.sqrt(HEAD_DIM)


def nt_dot(a, b, precision=None):
    return lax.dot_general(a, b, (((1,), (1,)), ((), ())), precision=precision, preferred_element_type=F32)


def two_parts(x):
    high = x.astype(BF16)
    return high, (x - high.astype(F32)).astype(BF16)


def head_cols(h):
    return slice(h * HEAD_DIM, (h + 1) * HEAD_DIM)


def step_embedding(timesteps):
    half_width = FREQ // 2
    frequency = jnp.exp(-math.log(10000.0) * jnp.arange(half_width, dtype=F32) / half_width)
    angles = timesteps.astype(F32)[:, None] * frequency[None, :]
    return jnp.concatenate([jnp.cos(angles), jnp.sin(angles)], axis=1)


def clip_index(info_ref, clips, shape, axis, first):
    places = lax.broadcasted_iota(jnp.int32, shape, axis) + first
    end = jnp.int32(0)
    index = jnp.zeros(shape, jnp.int32)
    for c in range(clips):
        end = end + info_ref[c]
        index = index + (places >= end).astype(jnp.int32)
    return index


def partner(rank, k, size):
    return rank ^ k if size & (size - 1) == 0 else (rank + k) % size


def source_rows(sources, k, tok_dev):
    rank = lax.axis_index("seq")
    source = partner(rank, k if sources & (sources - 1) == 0 else sources - k, sources)
    return pl.ds(pl.multiple_of(source * tok_dev, tok_dev), tok_dev)


def summed_here(rank, sources, tok_dev):
    if sources != 4:
        return rank * tok_dev, tok_dev, True
    return rank // 2 * 2 * tok_dev, 2 * tok_dev, (rank == 1) | (rank == 2)


def origins(rank, sources):
    if sources == 4:
        return [rank, rank ^ 1, 3 - rank, (3 - rank) ^ 1]
    ahead = reversed(range(sources))
    return [partner(rank, k if sources & (sources - 1) == 0 else sources - k, sources) for k in ahead]


def cut_kernel(sources, plan, *refs):
    count = len(refs) - 1 - len(plan)
    wholes, pieces, sems = refs[:count], refs[count:-1], refs[-1]
    local = pieces[0].shape[2]
    copies = []
    for (k, which), piece in zip(plan, pieces):
        target = partner(lax.axis_index("seq"), k, sources)
        for place, i in enumerate(which):
            columns = pl.ds(pl.multiple_of(target * local, HEAD_DIM), local)
            copies.append(pltpu.make_async_copy(wholes[i].at[:, columns], piece.at[place], sems.at[len(copies)]))
            copies[-1].start()
    for copy in copies:
        copy.wait()


def prep_kernel(
    sources, clips, info_ref, act_ref, mod_hbm, wt_hbm, noise_hbm, clean_hbm, kv_hbm,
    scale_ref, slope_ref, shift_ref, share_ref, target_ref, weight_ref, keys_ref, values_ref,
    mods, mod_buf, wt_buf, noise_buf, clean_buf, kv_buf, sems,
):
    width = wt_buf.shape[1]
    group_rows, local = scale_ref.shape
    tok_dev = noise_buf.shape[1]
    rank = lax.axis_index("seq")
    pairs = [(mod_hbm, mod_buf), (wt_hbm, wt_buf), (noise_hbm, noise_buf), (clean_hbm, clean_buf)]
    pairs += [(kv_hbm.at[c], kv_buf.at[c]) for c in range(clips)]
    copies = [pltpu.make_async_copy(a, b, sems.at[i]) for i, (a, b) in enumerate(pairs)]
    for copy in copies:
        copy.start()
    for copy in copies[:4]:
        copy.wait()
    mods[...] = jnp.dot(act_ref[...], mod_buf[...], preferred_element_type=F32)
    weight = wt_buf[...].astype(F32)
    shifts = nt_dot(weight, mods[:, :width], EXACT)
    first, count, active = summed_here(rank, sources, tok_dev)
    tok_clip = clip_index(info_ref, clips, (clips, count), 1, first)
    picks = (tok_clip == lax.broadcasted_iota(jnp.int32, (clips, count), 0)).astype(F32)
    slot = lax.broadcasted_iota(jnp.int32, (clips, 1), 0)
    sizes = jnp.zeros((clips, 1), F32)
    for c in range(clips):
        sizes = jnp.where(slot == c, info_ref[c].astype(F32), sizes)
    share_ref[...] = jnp.where(active, picks / sizes, 0.0)
    for place, source in enumerate(origins(rank, sources)):
        low = pl.multiple_of(source * local, HEAD_DIM)
        scales = 1.0 + mods[:, pl.ds(pl.multiple_of(width + low, HEAD_DIM), local)]
        slopes = nt_dot(wt_buf[:, pl.ds(low, local)].astype(F32), scales, EXACT)
        slope_ref[place] = jnp.dot(slopes, picks, precision=EXACT, preferred_element_type=F32)
    shift_ref[...] = jnp.dot(shifts, picks, precision=EXACT, preferred_element_type=F32)
    target_ref[...] = noise_buf[...] - clean_buf[...]
    row_clip = clip_index(info_ref, clips, (group_rows, clips), 0, 0)
    row_picks = (row_clip == lax.broadcasted_iota(jnp.int32, (group_rows, clips), 1)).astype(F32)
    mine = 1.0 + mods[:, pl.ds(pl.multiple_of(width + rank * local, HEAD_DIM), local)]
    scale_ref[...] = jnp.dot(row_picks, mine, precision=EXACT, preferred_element_type=F32)
    weight_ref[...] = wt_buf[:, pl.ds(pl.multiple_of(rank * local, HEAD_DIM), local)]
    for c in range(clips):
        copies[4 + c].wait()
        keys_ref[c] = kv_buf[c, :, 0, :]
        values_ref[c] = kv_buf[c, :, 1, :]


def text_kernel(sources, clips, window, info_ref, *refs):
    q_refs = refs[:sources]
    keys_ref, values_ref, out_ref, level_ref, q_all = refs[sources:]
    tok_dev, local = q_refs[0].shape[1:]
    heads = local // HEAD_DIM
    text_len = keys_ref.shape[1]
    for k, q_ref in enumerate(q_refs):
        q_all[source_rows(sources, k, tok_dev), :] = q_ref[0]
    slots = lax.broadcasted_iota(jnp.int32, (1, text_len), 1)
    ones = jnp.ones((text_len, HEAD_DIM), BF16)

    def one_clip(clip, start):
        first = pl.multiple_of(start // ALIGN * ALIGN, ALIGN)
        rows = pl.ds(first, window)
        edge = pl.ds(first, ALIGN)
        live = slots < info_ref[clips + clip]
        before = lax.broadcasted_iota(jnp.int32, (ALIGN, 1), 0) + first < start
        kept = [(out_ref[edge, head_cols(h)], level_ref[h, edge, :]) for h in range(heads)]
        scores = [nt_dot(q_all[rows, head_cols(h)], keys_ref[clip, :, head_cols(h)]) for h in range(heads)]
        weights, tops = [], []
        for score in scores:
            score = jnp.where(live, score, NEG)
            top = jnp.max(score, axis=1, keepdims=True)
            weights.append(jnp.exp2((score - top) * SCORE_SCALE).astype(BF16))
            tops.append(top)
        results = []
        for h in range(heads):
            beside = jnp.concatenate([values_ref[clip, :, head_cols(h)], ones], axis=1)
            mixed = jnp.dot(weights[h], beside, preferred_element_type=F32)
            total = mixed[:, HEAD_DIM:]
            results.append((mixed[:, :HEAD_DIM] / total, tops[h] * SCORE_SCALE + jnp.log2(total)))
        for h in range(heads):
            out_ref[rows, head_cols(h)] = results[h][0]
            level_ref[h, rows, :] = results[h][1]
            out_ref[edge, head_cols(h)] = jnp.where(before, kept[h][0], results[h][0][:ALIGN])
            level_ref[h, edge, :] = jnp.where(before, kept[h][1], results[h][1][:ALIGN])
        return start + info_ref[clip]

    lax.fori_loop(0, clips, one_clip, jnp.int32(0))


def reach_of(first, reach, group_rows):
    span = group_rows - reach[1]
    return jnp.clip(first - reach[0], 0, span) if span else jnp.int32(0)


def weigh_kernel(sources, clips, reach, info_ref, *refs):
    q_refs, k_refs = refs[:sources], refs[sources : 2 * sources - NEAR]
    text_ref, level_ref, weight_ref, base_ref, q_all, k_all = refs[2 * sources - NEAR :]
    tok_dev, local = q_refs[0].shape[1:]
    group_rows = q_all.shape[0]
    heads = local // HEAD_DIM
    for k in range(sources):
        rows = source_rows(sources, k, tok_dev)
        q_all[rows, :] = q_refs[k][0]
        k_all[rows, :] = q_refs[k][1] if k < NEAR else k_refs[k - NEAR][0]
    for first in range(0, group_rows, tok_dev):
        low = min(max(first - reach[0], 0), group_rows - reach[1])
        rows, span = slice(first, first + tok_dev), slice(low, low + reach[1])
        row_clip = clip_index(info_ref, clips, (tok_dev, 1), 0, first)
        live = row_clip == clip_index(info_ref, clips, (1, reach[1]), 1, low)
        scores = [nt_dot(q_all[rows, head_cols(h)], k_all[span, head_cols(h)]) for h in range(heads)]
        for h in range(heads):
            score = jnp.where(live, scores[h] * SCORE_SCALE, NEG)
            level = level_ref[h, rows, :]
            top = jnp.maximum(jnp.max(score, axis=1, keepdims=True), level)
            chunks = [slice(part, part + HEAD_DIM) for part in range(0, reach[1], HEAD_DIM)]
            weights = [jnp.exp2(score[:, cols] - top) for cols in chunks]
            fade = jnp.exp2(level - top)
            share = 1.0 / (jnp.sum(sum(weights[1:], weights[0]), axis=1, keepdims=True) + fade)
            for cols, weight in zip(chunks, weights):
                weight_ref[h, rows, cols] = (weight * share).astype(BF16)
            base_ref[rows, head_cols(h)] = (fade * share) * text_ref[rows, head_cols(h)]


def mix_kernel(sources, reach, place, *refs):
    v_refs = refs[:sources]
    weight_ref, base_ref, scale_ref, wt_ref, out_ref, v_all = refs[sources:]
    tok_dev, local = v_refs[0].shape[1:]
    group_rows = scale_ref.shape[0]
    heads = local // HEAD_DIM
    channels = wt_ref.shape[0]
    for k in range(sources):
        v_all[source_rows(sources, k, tok_dev), :] = v_refs[k][2 if k < NEAR else 0]
    count = out_ref.shape[1]
    first = pl.multiple_of(place(lax.axis_index("seq")) * tok_dev, tok_dev)
    rows = pl.ds(first, count)
    span = pl.ds(pl.multiple_of(reach_of(first, reach, group_rows), HEAD_DIM), reach[1])
    mixed = [
        jnp.dot(weight_ref[h, rows, :], v_all[span, head_cols(h)], preferred_element_type=F32) for h in range(heads)
    ]
    attended = jnp.concatenate([(mixed[h] + base_ref[rows, head_cols(h)]).astype(BF16) for h in range(heads)], axis=1)
    attended_full = attended.astype(F32)
    local_mean = jnp.sum(attended_full, axis=1, keepdims=True) * (1.0 / local)
    y_high, y_low = two_parts((attended_full - local_mean) * scale_ref[rows, :])
    s_high, s_low = two_parts(attended_full * attended_full)
    weight = wt_ref[...]
    every = jnp.ones((STAT_ROWS, local), BF16)
    out_ref[:channels, :] = (nt_dot(weight, y_high) + nt_dot(weight, y_low)).astype(BF16)
    row = lax.broadcasted_iota(jnp.int32, (STAT_ROWS, count), 0)
    rest = jnp.where(row < 3, nt_dot(every, attended), nt_dot(every, s_high) + nt_dot(every, s_low))
    terms = jnp.zeros((STAT_ROWS, count), F32)
    for place in range(3):
        term = rest.astype(BF16).astype(F32)
        terms = jnp.where((row == place) | (row == place + 3), term, terms)
        rest = rest - term
    out_ref[channels:, :] = terms.astype(BF16)


def loss_kernel(count, width, *refs):
    part_refs = refs[:count]
    slope_ref, shift_ref, share_ref, *target_refs, out_ref = refs[count:]
    channels = slope_ref.shape[1]
    clips = share_ref.shape[0]
    parts = [part[...].astype(F32) for part in part_refs]
    stats = [part[channels:] for part in parts]
    sums = [stat[0:1] + stat[1:2] + stat[2:3] for stat in stats]
    squares = [stat[3:4] + stat[4:5] + stat[5:6] for stat in stats]
    center = sum(sums[1:], sums[0]) * (1.0 / width)
    spread = sum(squares[1:], squares[0]) * (1.0 / width) - center * center
    total = jnp.zeros(slope_ref.shape[1:], F32)
    for place, part in enumerate(parts):
        total = total + part[:channels] + (sums[place] * (count / width) - center) * slope_ref[place]
    targets = [target[...] for target in target_refs]
    if len(targets) == 2:
        swap = lax.axis_index("seq") == 1
        targets = [jnp.where(swap, *targets[::-1]), jnp.where(swap, *targets)]
    offset = shift_ref[...] - jnp.concatenate(targets, axis=1)
    diff = total * lax.rsqrt(spread + EPS) + offset
    error = jnp.sum(diff * diff, axis=0, keepdims=True) * (1.0 / channels)
    share = share_ref[...]
    sums = jnp.sum(jnp.where(share > 0.0, share * error, 0.0), axis=1, keepdims=True)
    lanes = lax.broadcasted_iota(jnp.int32, (clips, out_ref.shape[2]), 1)
    mine = lanes == lax.broadcasted_iota(jnp.int32, lanes.shape, 0)
    row = jnp.sum(jnp.where(mine, sums, 0.0), axis=0, keepdims=True)
    out_ref[...] = jnp.broadcast_to(row[None], out_ref.shape)


def smem():
    return pl.BlockSpec(memory_space=pltpu.SMEM)


def vmem():
    return pl.BlockSpec(memory_space=pltpu.VMEM)


def hbm():
    return pl.BlockSpec(memory_space=pltpu.HBM)


def call(kernel, name, operands, results, scratch=(), scalars=(), in_hbm=(), pinned=True, flops=0, traffic=0):
    return pl.pallas_call(
        kernel,
        in_specs=[smem()] * len(scalars) + [hbm() if i in in_hbm else vmem() for i in range(len(operands))],
        out_specs=[vmem()] * len(results),
        out_shape=[pltpu.VMEM(*r) if pinned else jax.ShapeDtypeStruct(*r) for r in results],
        scratch_shapes=list(scratch),
        compiler_params=pltpu.CompilerParams(vmem_limit_bytes=VMEM_LIMIT),
        cost_estimate=pl.CostEstimate(flops=flops, bytes_accessed=traffic, transcendentals=0),
        name=name,
    )(*scalars, *(pltpu.with_memory_space_constraint(x, pltpu.HBM) if i in in_hbm else x for i, x in enumerate(operands)))


def per_device(
    queries, keys, values, text_kv, text_lengths, clip_lengths, timesteps, mod_weight, final_weight, noise, clean,
    report_order,
):
    tok_dev, width = queries.shape
    sources = lax.axis_size("seq")
    groups = lax.axis_size("dp")
    local = width // sources
    heads = local // HEAD_DIM
    group_rows = tok_dev * sources
    clips = clip_lengths.shape[1]
    text_len = text_kv.shape[1]
    clip_most = 2 * group_rows // clips
    window = clip_most + ALIGN
    padded = group_rows + window
    reach = (clip_most, min(group_rows, tok_dev + 2 * clip_most))
    channels = final_weight.shape[1]
    info = jnp.concatenate([clip_lengths[0], text_lengths])

    def cut(arrays, plan, name):
        count = sum(len(which) for _, which in plan)
        return list(
            call(
                functools.partial(cut_kernel, sources, plan), name, arrays,
                [((len(which), tok_dev, local), BF16) for _, which in plan],
                [pltpu.SemaphoreType.DMA((count,))], in_hbm=range(len(arrays)), traffic=4 * tok_dev * local * count,
            )
        )

    def onward(x, k):
        return lax.ppermute(x, "seq", [(i, partner(i, k, sources)) for i in range(sources)]) if k else x

    far = [*range(NEAR, sources)]
    q_pieces = cut([queries], [(k, (0,)) for k in far], "cut_first")
    q_blocks = [onward(piece, k) for k, piece in zip(far, q_pieces)]
    q_pieces[0], keys = lax.optimization_barrier((q_pieces[0], keys))
    pieces = cut(
        [queries, keys, values],
        [(k, (0, 1, 2)) for k in reversed(range(NEAR))] + [(k, (i,)) for i in (1, 2) for k in far],
        "cut_rest",
    )
    near_blocks = [onward(pieces[NEAR - 1 - k], k) for k in range(NEAR)]
    q_blocks = near_blocks + q_blocks
    k_blocks = [onward(piece, k) for k, piece in zip(far, pieces[NEAR:])]

    weight_t = final_weight.T
    activated = jax.nn.silu(step_embedding(timesteps)).astype(BF16)
    _, summed, _ = summed_here(0, sources, tok_dev)
    scale_tok, slope, shift, share, target, weight_local, text_keys, text_values = call(
        functools.partial(prep_kernel, sources, clips), "prep",
        [activated, mod_weight, weight_t, noise.T, clean.T, text_kv],
        [
            ((group_rows, local), F32), ((sources, channels, summed), F32), ((channels, summed), F32),
            ((clips, summed), F32), ((channels, tok_dev), F32),
            ((channels, local), BF16), ((clips, text_len, local), BF16), ((clips, text_len, local), BF16),
        ],
        [
            pltpu.VMEM((clips, 2 * width), F32), pltpu.VMEM(mod_weight.shape, BF16),
            pltpu.VMEM(weight_t.shape, BF16), pltpu.VMEM((channels, tok_dev), F32),
            pltpu.VMEM((channels, tok_dev), F32), pltpu.VMEM(text_kv.shape, BF16),
            pltpu.SemaphoreType.DMA((4 + clips,)),
        ],
        scalars=[info], in_hbm=range(1, 6),
    )

    v_pieces, scale_tok = lax.optimization_barrier((pieces[NEAR + len(far) :], scale_tok))
    v_blocks = [onward(piece, k) for k, piece in zip(far, v_pieces)]

    text_out, level = call(
        functools.partial(text_kernel, sources, clips, window), "text", [*q_blocks, text_keys, text_values],
        [((padded, local), F32), ((heads, padded, HEAD_DIM), F32)],
        [pltpu.VMEM((padded, local), BF16)], scalars=[info],
    )

    swap = [(0, 1), (1, 0), (2, 3), (3, 2)]
    targets = [target]
    if sources == 4:
        text_out, moved = lax.optimization_barrier((text_out, lax.ppermute(target, "seq", swap)))
        targets.append(moved)

    weights, base = call(
        functools.partial(weigh_kernel, sources, clips, reach), "weigh", [*q_blocks, *k_blocks, text_out, level],
        [((heads, group_rows, reach[1]), BF16), ((group_rows, local), F32)],
        [pltpu.VMEM((group_rows, local), BF16)] * 2, scalars=[info],
    )

    def mix(place):
        return call(
            functools.partial(mix_kernel, sources, reach, place), "mix",
            [*near_blocks, *v_blocks, weights, base, scale_tok, weight_local],
            [((channels + STAT_ROWS, summed), BF16)],
            [pltpu.VMEM((group_rows, local), BF16)], flops=4 * summed * reach[1] * local, traffic=2**20,
        )[0]

    if sources == 4:
        here = mix(lambda rank: rank // 2 * 2)
        parts = [here, lax.ppermute(here, "seq", swap)]
        there = mix(lambda rank: 2 - rank // 2 * 2)
        for pairs in ([(1, 2), (2, 1), (0, 0), (3, 3)], [(0, 2), (2, 3), (3, 1), (1, 0)]):
            parts.append(lax.ppermute(there, "seq", pairs))
    else:
        parts = [onward(mix(lambda rank, k=k: partner(rank, k, sources)), k) for k in reversed(range(sources))]

    (shares,) = call(
        functools.partial(loss_kernel, len(parts), width), "loss", [*parts, slope, shift, share, *targets],
        [((groups * sources, 1, HEAD_DIM), F32)],
    )
    everyone = lax.all_to_all(shares, ("dp", "seq"), split_axis=0, concat_axis=0, tiled=True)
    losses = jnp.sum(everyone.reshape(groups, sources, HEAD_DIM), axis=1)[:, :clips].reshape(1, -1)
    slots = jnp.arange(groups * clips, dtype=jnp.int32)
    return jnp.sum(jnp.where(report_order[:, None] == slots[None, :], losses, 0.0), axis=1)


def solution(mesh):
    in_specs = (
        P(("dp", "seq"), None),
        P(("dp", "seq"), None),
        P(("dp", "seq"), None),
        P("dp", None, None, "seq"),
        P("dp"),
        P("dp", None),
        P("dp"),
        P(),
        P(),
        P(("dp", "seq"), None),
        P(("dp", "seq"), None),
        P("dp"),
    )
    return jax.shard_map(per_device, mesh=mesh, in_specs=in_specs, out_specs=P("dp"), check_vma=False)
```

```python
import functools
import math

import jax
import jax.numpy as jnp
from jax import lax
from jax.experimental import pallas as pl
from jax.experimental.pallas import tpu as pltpu
from jax.sharding import PartitionSpec as P

HEAD_DIM = 128
FREQ = 256
EPS = 1e-06
NEG = -1e30
STAT_ROWS = 16
ALIGN = 16
NEAR = 2
F32 = jnp.float32
BF16 = jnp.bfloat16
EXACT = lax.Precision.HIGHEST
VMEM_LIMIT = 32 * 1024 * 1024
SCORE_SCALE = math.log2(math.e) / math.sqrt(HEAD_DIM)


def nt_dot(a, b, precision=None):
    return lax.dot_general(a, b, (((1,), (1,)), ((), ())), precision=precision, preferred_element_type=F32)


def two_parts(x):
    high = x.astype(BF16)
    return high, (x - high.astype(F32)).astype(BF16)


def head_cols(h):
    return slice(h * HEAD_DIM, (h + 1) * HEAD_DIM)


def step_embedding(timesteps):
    half_width = FREQ // 2
    frequency = jnp.exp(-math.log(10000.0) * jnp.arange(half_width, dtype=F32) / half_width)
    angles = timesteps.astype(F32)[:, None] * frequency[None, :]
    return jnp.concatenate([jnp.cos(angles), jnp.sin(angles)], axis=1)


def clip_index(info_ref, clips, shape, axis, first):
    places = lax.broadcasted_iota(jnp.int32, shape, axis) + first
    end = jnp.int32(0)
    index = jnp.zeros(shape, jnp.int32)
    for c in range(clips):
        end = end + info_ref[c]
        index = index + (places >= end).astype(jnp.int32)
    return index


def partner(rank, k, size):
    return rank ^ k if size & (size - 1) == 0 else (rank + k) % size


def source_rows(sources, k, tok_dev):
    rank = lax.axis_index("seq")
    source = partner(rank, k if sources & (sources - 1) == 0 else sources - k, sources)
    return pl.ds(pl.multiple_of(source * tok_dev, tok_dev), tok_dev)


def summed_here(rank, sources, tok_dev):
    if sources != 4:
        return rank * tok_dev, tok_dev, True
    return rank // 2 * 2 * tok_dev, 2 * tok_dev, (rank == 1) | (rank == 2)


def origins(rank, sources):
    if sources == 4:
        return [rank, rank ^ 1, 3 - rank, (3 - rank) ^ 1]
    ahead = reversed(range(sources))
    return [partner(rank, k if sources & (sources - 1) == 0 else sources - k, sources) for k in ahead]


def cut_kernel(sources, plan, *refs):
    count = len(refs) - 1 - len(plan)
    wholes, pieces, sems = refs[:count], refs[count:-1], refs[-1]
    local = pieces[0].shape[2]
    copies = []
    for (k, which), piece in zip(plan, pieces):
        target = partner(lax.axis_index("seq"), k, sources)
        for place, i in enumerate(which):
            columns = pl.ds(pl.multiple_of(target * local, HEAD_DIM), local)
            copies.append(pltpu.make_async_copy(wholes[i].at[:, columns], piece.at[place], sems.at[len(copies)]))
            copies[-1].start()
    for copy in copies:
        copy.wait()


def prep_kernel(
    sources, clips, info_ref, act_ref, mod_hbm, wt_hbm, noise_hbm, clean_hbm, kv_hbm,
    scale_ref, slope_ref, shift_ref, share_ref, target_ref, weight_ref, keys_ref, values_ref,
    mods, mod_buf, wt_buf, noise_buf, clean_buf, kv_buf, sems,
):
    width = wt_buf.shape[1]
    group_rows, local = scale_ref.shape
    tok_dev = noise_buf.shape[1]
    rank = lax.axis_index("seq")
    pairs = [(mod_hbm, mod_buf), (wt_hbm, wt_buf), (noise_hbm, noise_buf), (clean_hbm, clean_buf)]
    pairs += [(kv_hbm.at[c], kv_buf.at[c]) for c in range(clips)]
    copies = [pltpu.make_async_copy(a, b, sems.at[i]) for i, (a, b) in enumerate(pairs)]
    for copy in copies:
        copy.start()
    for copy in copies[:4]:
        copy.wait()
    mods[...] = jnp.dot(act_ref[...], mod_buf[...], preferred_element_type=F32)
    weight = wt_buf[...].astype(F32)
    shifts = nt_dot(weight, mods[:, :width], EXACT)
    first, count, active = summed_here(rank, sources, tok_dev)
    tok_clip = clip_index(info_ref, clips, (clips, count), 1, first)
    picks = (tok_clip == lax.broadcasted_iota(jnp.int32, (clips, count), 0)).astype(F32)
    slot = lax.broadcasted_iota(jnp.int32, (clips, 1), 0)
    sizes = jnp.zeros((clips, 1), F32)
    for c in range(clips):
        sizes = jnp.where(slot == c, info_ref[c].astype(F32), sizes)
    share_ref[...] = jnp.where(active, picks / sizes, 0.0)
    for place, source in enumerate(origins(rank, sources)):
        low = pl.multiple_of(source * local, HEAD_DIM)
        scales = 1.0 + mods[:, pl.ds(pl.multiple_of(width + low, HEAD_DIM), local)]
        slopes = nt_dot(wt_buf[:, pl.ds(low, local)].astype(F32), scales, EXACT)
        slope_ref[place] = jnp.dot(slopes, picks, precision=EXACT, preferred_element_type=F32)
    shift_ref[...] = jnp.dot(shifts, picks, precision=EXACT, preferred_element_type=F32)
    target_ref[...] = noise_buf[...] - clean_buf[...]
    row_clip = clip_index(info_ref, clips, (group_rows, clips), 0, 0)
    row_picks = (row_clip == lax.broadcasted_iota(jnp.int32, (group_rows, clips), 1)).astype(F32)
    mine = 1.0 + mods[:, pl.ds(pl.multiple_of(width + rank * local, HEAD_DIM), local)]
    scale_ref[...] = jnp.dot(row_picks, mine, precision=EXACT, preferred_element_type=F32)
    weight_ref[...] = wt_buf[:, pl.ds(pl.multiple_of(rank * local, HEAD_DIM), local)]
    for c in range(clips):
        copies[4 + c].wait()
        keys_ref[c] = kv_buf[c, :, 0, :]
        values_ref[c] = kv_buf[c, :, 1, :]


def text_kernel(sources, clips, window, info_ref, *refs):
    q_refs = refs[:sources]
    keys_ref, values_ref, out_ref, level_ref, q_all = refs[sources:]
    tok_dev, local = q_refs[0].shape[1:]
    heads = local // HEAD_DIM
    text_len = keys_ref.shape[1]
    for k, q_ref in enumerate(q_refs):
        q_all[source_rows(sources, k, tok_dev), :] = q_ref[0]
    slots = lax.broadcasted_iota(jnp.int32, (1, text_len), 1)
    ones = jnp.ones((text_len, HEAD_DIM), BF16)

    def one_clip(clip, start):
        first = pl.multiple_of(start // ALIGN * ALIGN, ALIGN)
        rows = pl.ds(first, window)
        edge = pl.ds(first, ALIGN)
        live = slots < info_ref[clips + clip]
        before = lax.broadcasted_iota(jnp.int32, (ALIGN, 1), 0) + first < start
        kept = [(out_ref[edge, head_cols(h)], level_ref[h, edge, :]) for h in range(heads)]
        scores = [nt_dot(q_all[rows, head_cols(h)], keys_ref[clip, :, head_cols(h)]) for h in range(heads)]
        weights, tops = [], []
        for score in scores:
            score = jnp.where(live, score, NEG)
            top = jnp.max(score, axis=1, keepdims=True)
            weights.append(jnp.exp2((score - top) * SCORE_SCALE).astype(BF16))
            tops.append(top)
        results = []
        for h in range(heads):
            beside = jnp.concatenate([values_ref[clip, :, head_cols(h)], ones], axis=1)
            mixed = jnp.dot(weights[h], beside, preferred_element_type=F32)
            total = mixed[:, HEAD_DIM:]
            results.append((mixed[:, :HEAD_DIM] / total, tops[h] * SCORE_SCALE + jnp.log2(total)))
        for h in range(heads):
            out_ref[rows, head_cols(h)] = results[h][0]
            level_ref[h, rows, :] = results[h][1]
            out_ref[edge, head_cols(h)] = jnp.where(before, kept[h][0], results[h][0][:ALIGN])
            level_ref[h, edge, :] = jnp.where(before, kept[h][1], results[h][1][:ALIGN])
        return start + info_ref[clip]

    lax.fori_loop(0, clips, one_clip, jnp.int32(0))


def reach_of(first, reach, group_rows):
    span = group_rows - reach[1]
    return jnp.clip(first - reach[0], 0, span) if span else jnp.int32(0)


def weigh_kernel(sources, clips, reach, info_ref, *refs):
    q_refs, k_refs = refs[:sources], refs[sources : 2 * sources - NEAR]
    text_ref, level_ref, weight_ref, base_ref, q_all, k_all = refs[2 * sources - NEAR :]
    tok_dev, local = q_refs[0].shape[1:]
    group_rows = q_all.shape[0]
    heads = local // HEAD_DIM
    for k in range(sources):
        rows = source_rows(sources, k, tok_dev)
        q_all[rows, :] = q_refs[k][0]
        k_all[rows, :] = q_refs[k][1] if k < NEAR else k_refs[k - NEAR][0]
    for first in range(0, group_rows, tok_dev):
        low = min(max(first - reach[0], 0), group_rows - reach[1])
        rows, span = slice(first, first + tok_dev), slice(low, low + reach[1])
        row_clip = clip_index(info_ref, clips, (tok_dev, 1), 0, first)
        live = row_clip == clip_index(info_ref, clips, (1, reach[1]), 1, low)
        scores = [nt_dot(q_all[rows, head_cols(h)], k_all[span, head_cols(h)]) for h in range(heads)]
        for h in range(heads):
            score = jnp.where(live, scores[h] * SCORE_SCALE, NEG)
            level = level_ref[h, rows, :]
            top = jnp.maximum(jnp.max(score, axis=1, keepdims=True), level)
            chunks = [slice(part, part + HEAD_DIM) for part in range(0, reach[1], HEAD_DIM)]
            weights = [jnp.exp2(score[:, cols] - top) for cols in chunks]
            fade = jnp.exp2(level - top)
            share = 1.0 / (jnp.sum(sum(weights[1:], weights[0]), axis=1, keepdims=True) + fade)
            for cols, weight in zip(chunks, weights):
                weight_ref[h, rows, cols] = (weight * share).astype(BF16)
            base_ref[rows, head_cols(h)] = (fade * share) * text_ref[rows, head_cols(h)]


def mix_kernel(sources, reach, place, *refs):
    v_refs = refs[:sources]
    weight_ref, base_ref, scale_ref, wt_ref, out_ref, v_all = refs[sources:]
    tok_dev, local = v_refs[0].shape[1:]
    group_rows = scale_ref.shape[0]
    heads = local // HEAD_DIM
    channels = wt_ref.shape[0]
    for k in range(sources):
        v_all[source_rows(sources, k, tok_dev), :] = v_refs[k][2 if k < NEAR else 0]
    count = out_ref.shape[1]
    first = pl.multiple_of(place(lax.axis_index("seq")) * tok_dev, tok_dev)
    rows = pl.ds(first, count)
    span = pl.ds(pl.multiple_of(reach_of(first, reach, group_rows), HEAD_DIM), reach[1])
    mixed = [
        jnp.dot(weight_ref[h, rows, :], v_all[span, head_cols(h)], preferred_element_type=F32) for h in range(heads)
    ]
    attended = jnp.concatenate([(mixed[h] + base_ref[rows, head_cols(h)]).astype(BF16) for h in range(heads)], axis=1)
    attended_full = attended.astype(F32)
    local_mean = jnp.sum(attended_full, axis=1, keepdims=True) * (1.0 / local)
    y_high, y_low = two_parts((attended_full - local_mean) * scale_ref[rows, :])
    s_high, s_low = two_parts(attended_full * attended_full)
    weight = wt_ref[...]
    every = jnp.ones((STAT_ROWS, local), BF16)
    out_ref[:channels, :] = (nt_dot(weight, y_high) + nt_dot(weight, y_low)).astype(BF16)
    row = lax.broadcasted_iota(jnp.int32, (STAT_ROWS, count), 0)
    rest = jnp.where(row < 3, nt_dot(every, attended), nt_dot(every, s_high) + nt_dot(every, s_low))
    terms = jnp.zeros((STAT_ROWS, count), F32)
    for place in range(3):
        term = rest.astype(BF16).astype(F32)
        terms = jnp.where((row == place) | (row == place + 3), term, terms)
        rest = rest - term
    out_ref[channels:, :] = terms.astype(BF16)


def loss_kernel(count, width, *refs):
    part_refs = refs[:count]
    slope_ref, shift_ref, share_ref, *target_refs, out_ref = refs[count:]
    channels = slope_ref.shape[1]
    clips = share_ref.shape[0]
    parts = [part[...].astype(F32) for part in part_refs]
    stats = [part[channels:] for part in parts]
    sums = [stat[0:1] + stat[1:2] + stat[2:3] for stat in stats]
    squares = [stat[3:4] + stat[4:5] + stat[5:6] for stat in stats]
    center = sum(sums[1:], sums[0]) * (1.0 / width)
    spread = sum(squares[1:], squares[0]) * (1.0 / width) - center * center
    total = jnp.zeros(slope_ref.shape[1:], F32)
    for place, part in enumerate(parts):
        total = total + part[:channels] + (sums[place] * (count / width) - center) * slope_ref[place]
    targets = [target[...] for target in target_refs]
    if len(targets) == 2:
        swap = lax.axis_index("seq") == 1
        targets = [jnp.where(swap, *targets[::-1]), jnp.where(swap, *targets)]
    offset = shift_ref[...] - jnp.concatenate(targets, axis=1)
    diff = total * lax.rsqrt(spread + EPS) + offset
    error = jnp.sum(diff * diff, axis=0, keepdims=True) * (1.0 / channels)
    share = share_ref[...]
    sums = jnp.sum(jnp.where(share > 0.0, share * error, 0.0), axis=1, keepdims=True)
    lanes = lax.broadcasted_iota(jnp.int32, (clips, out_ref.shape[2]), 1)
    mine = lanes == lax.broadcasted_iota(jnp.int32, lanes.shape, 0)
    row = jnp.sum(jnp.where(mine, sums, 0.0), axis=0, keepdims=True)
    out_ref[...] = jnp.broadcast_to(row[None], out_ref.shape)


def smem():
    return pl.BlockSpec(memory_space=pltpu.SMEM)


def vmem():
    return pl.BlockSpec(memory_space=pltpu.VMEM)


def hbm():
    return pl.BlockSpec(memory_space=pltpu.HBM)


def call(kernel, name, operands, results, scratch=(), scalars=(), in_hbm=(), pinned=True, flops=0, traffic=0):
    return pl.pallas_call(
        kernel,
        in_specs=[smem()] * len(scalars) + [hbm() if i in in_hbm else vmem() for i in range(len(operands))],
        out_specs=[vmem()] * len(results),
        out_shape=[pltpu.VMEM(*r) if pinned else jax.ShapeDtypeStruct(*r) for r in results],
        scratch_shapes=list(scratch),
        compiler_params=pltpu.CompilerParams(vmem_limit_bytes=VMEM_LIMIT),
        cost_estimate=pl.CostEstimate(flops=flops, bytes_accessed=traffic, transcendentals=0),
        name=name,
    )(*scalars, *(pltpu.with_memory_space_constraint(x, pltpu.HBM) if i in in_hbm else x for i, x in enumerate(operands)))


def per_device(
    queries, keys, values, text_kv, text_lengths, clip_lengths, timesteps, mod_weight, final_weight, noise, clean,
    report_order,
):
    tok_dev, width = queries.shape
    sources = lax.axis_size("seq")
    groups = lax.axis_size("dp")
    local = width // sources
    heads = local // HEAD_DIM
    group_rows = tok_dev * sources
    clips = clip_lengths.shape[1]
    text_len = text_kv.shape[1]
    clip_most = 2 * group_rows // clips
    window = clip_most + ALIGN
    padded = group_rows + window
    reach = (clip_most, min(group_rows, tok_dev + 2 * clip_most))
    channels = final_weight.shape[1]
    info = jnp.concatenate([clip_lengths[0], text_lengths])

    def cut(arrays, plan, name):
        count = sum(len(which) for _, which in plan)
        return list(
            call(
                functools.partial(cut_kernel, sources, plan), name, arrays,
                [((len(which), tok_dev, local), BF16) for _, which in plan],
                [pltpu.SemaphoreType.DMA((count,))], in_hbm=range(len(arrays)), traffic=4 * tok_dev * local * count,
            )
        )

    def onward(x, k):
        return lax.ppermute(x, "seq", [(i, partner(i, k, sources)) for i in range(sources)]) if k else x

    far = [*range(NEAR, sources)]
    q_pieces = cut([queries], [(k, (0,)) for k in far], "cut_first")
    q_blocks = [onward(piece, k) for k, piece in zip(far, q_pieces)]
    q_pieces[0], keys = lax.optimization_barrier((q_pieces[0], keys))
    pieces = cut(
        [queries, keys, values],
        [(k, (0, 1, 2)) for k in reversed(range(NEAR))] + [(k, (i,)) for i in (1, 2) for k in far],
        "cut_rest",
    )
    near_blocks = [onward(pieces[NEAR - 1 - k], k) for k in range(NEAR)]
    q_blocks = near_blocks + q_blocks
    k_blocks = [onward(piece, k) for k, piece in zip(far, pieces[NEAR:])]

    weight_t = final_weight.T
    activated = jax.nn.silu(step_embedding(timesteps)).astype(BF16)
    _, summed, _ = summed_here(0, sources, tok_dev)
    scale_tok, slope, shift, share, target, weight_local, text_keys, text_values = call(
        functools.partial(prep_kernel, sources, clips), "prep",
        [activated, mod_weight, weight_t, noise.T, clean.T, text_kv],
        [
            ((group_rows, local), F32), ((sources, channels, summed), F32), ((channels, summed), F32),
            ((clips, summed), F32), ((channels, tok_dev), F32),
            ((channels, local), BF16), ((clips, text_len, local), BF16), ((clips, text_len, local), BF16),
        ],
        [
            pltpu.VMEM((clips, 2 * width), F32), pltpu.VMEM(mod_weight.shape, BF16),
            pltpu.VMEM(weight_t.shape, BF16), pltpu.VMEM((channels, tok_dev), F32),
            pltpu.VMEM((channels, tok_dev), F32), pltpu.VMEM(text_kv.shape, BF16),
            pltpu.SemaphoreType.DMA((4 + clips,)),
        ],
        scalars=[info], in_hbm=range(1, 6),
    )

    v_pieces, scale_tok = lax.optimization_barrier((pieces[NEAR + len(far) :], scale_tok))
    v_blocks = [onward(piece, k) for k, piece in zip(far, v_pieces)]

    text_out, level = call(
        functools.partial(text_kernel, sources, clips, window), "text", [*q_blocks, text_keys, text_values],
        [((padded, local), F32), ((heads, padded, HEAD_DIM), F32)],
        [pltpu.VMEM((padded, local), BF16)], scalars=[info],
    )

    weights, base = call(
        functools.partial(weigh_kernel, sources, clips, reach), "weigh", [*q_blocks, *k_blocks, text_out, level],
        [((heads, group_rows, reach[1]), BF16), ((group_rows, local), F32)],
        [pltpu.VMEM((group_rows, local), BF16)] * 2, scalars=[info],
    )

    swap = [(0, 1), (1, 0), (2, 3), (3, 2)]
    targets = [target]
    if sources == 4:
        weights, moved = lax.optimization_barrier((weights, lax.ppermute(target, "seq", swap)))
        targets.append(moved)

    def mix(place):
        return call(
            functools.partial(mix_kernel, sources, reach, place), "mix",
            [*near_blocks, *v_blocks, weights, base, scale_tok, weight_local],
            [((channels + STAT_ROWS, summed), BF16)],
            [pltpu.VMEM((group_rows, local), BF16)], flops=4 * summed * reach[1] * local, traffic=2**20,
        )[0]

    if sources == 4:
        here = mix(lambda rank: rank // 2 * 2)
        parts = [here, lax.ppermute(here, "seq", swap)]
        there = mix(lambda rank: 2 - rank // 2 * 2)
        for pairs in ([(1, 2), (2, 1), (0, 3), (3, 0)], [(0, 2), (2, 3), (3, 1), (1, 0)]):
            parts.append(lax.ppermute(there, "seq", pairs))
    else:
        parts = [onward(mix(lambda rank, k=k: partner(rank, k, sources)), k) for k in reversed(range(sources))]

    (shares,) = call(
        functools.partial(loss_kernel, len(parts), width), "loss", [*parts, slope, shift, share, *targets],
        [((groups * sources, 1, HEAD_DIM), F32)],
    )
    everyone = lax.all_to_all(shares, ("dp", "seq"), split_axis=0, concat_axis=0, tiled=True)
    losses = jnp.sum(everyone.reshape(groups, sources, HEAD_DIM), axis=1)[:, :clips].reshape(1, -1)
    slots = jnp.arange(groups * clips, dtype=jnp.int32)
    return jnp.sum(jnp.where(report_order[:, None] == slots[None, :], losses, 0.0), axis=1)


def solution(mesh):
    in_specs = (
        P(("dp", "seq"), None),
        P(("dp", "seq"), None),
        P(("dp", "seq"), None),
        P("dp", None, None, "seq"),
        P("dp"),
        P("dp", None),
        P("dp"),
        P(),
        P(),
        P(("dp", "seq"), None),
        P(("dp", "seq"), None),
        P("dp"),
    )
    return jax.shard_map(per_device, mesh=mesh, in_specs=in_specs, out_specs=P("dp"), check_vma=False)
```

```python
import functools
import math

import jax
import jax.numpy as jnp
from jax import lax
from jax.experimental import pallas as pl
from jax.experimental.pallas import tpu as pltpu
from jax.sharding import PartitionSpec as P

HEAD_DIM = 128
FREQ = 256
EPS = 1e-06
NEG = -1e30
STAT_ROWS = 16
MERGED_ROWS = 8
ALIGN = 16
NEAR = 2
F32 = jnp.float32
BF16 = jnp.bfloat16
EXACT = lax.Precision.HIGHEST
VMEM_LIMIT = 32 * 1024 * 1024
SCORE_SCALE = math.log2(math.e) / math.sqrt(HEAD_DIM)


def nt_dot(a, b, precision=None):
    return lax.dot_general(a, b, (((1,), (1,)), ((), ())), precision=precision, preferred_element_type=F32)


def two_parts(x):
    high = x.astype(BF16)
    return high, (x - high.astype(F32)).astype(BF16)


def head_cols(h):
    return slice(h * HEAD_DIM, (h + 1) * HEAD_DIM)


def step_embedding(timesteps):
    half_width = FREQ // 2
    frequency = jnp.exp(-math.log(10000.0) * jnp.arange(half_width, dtype=F32) / half_width)
    angles = timesteps.astype(F32)[:, None] * frequency[None, :]
    return jnp.concatenate([jnp.cos(angles), jnp.sin(angles)], axis=1)


def clip_index(info_ref, clips, shape, axis, first):
    places = lax.broadcasted_iota(jnp.int32, shape, axis) + first
    end = jnp.int32(0)
    index = jnp.zeros(shape, jnp.int32)
    for c in range(clips):
        end = end + info_ref[c]
        index = index + (places >= end).astype(jnp.int32)
    return index


def partner(rank, k, size):
    return rank ^ k if size & (size - 1) == 0 else (rank + k) % size


def source_rows(sources, k, tok_dev):
    rank = lax.axis_index("seq")
    source = partner(rank, k if sources & (sources - 1) == 0 else sources - k, sources)
    return pl.ds(pl.multiple_of(source * tok_dev, tok_dev), tok_dev)


def origins(rank, sources):
    if sources == 4:
        return [rank, rank ^ 2, rank ^ 1, rank ^ 3]
    ahead = reversed(range(sources))
    return [partner(rank, k if sources & (sources - 1) == 0 else sources - k, sources) for k in ahead]


def cut_kernel(sources, plan, *refs):
    count = len(refs) - 1 - len(plan)
    wholes, pieces, sems = refs[:count], refs[count:-1], refs[-1]
    local = pieces[0].shape[2]
    copies = []
    for (k, which), piece in zip(plan, pieces):
        target = partner(lax.axis_index("seq"), k, sources)
        for place, i in enumerate(which):
            columns = pl.ds(pl.multiple_of(target * local, HEAD_DIM), local)
            copies.append(pltpu.make_async_copy(wholes[i].at[:, columns], piece.at[place], sems.at[len(copies)]))
            copies[-1].start()
    for copy in copies:
        copy.wait()


def prep_kernel(
    sources, clips, info_ref, act_ref, mod_hbm, wt_hbm, noise_hbm, clean_hbm, kv_hbm,
    scale_ref, slope_ref, offset_ref, share_ref, weight_ref, keys_ref, values_ref,
    mods, mod_buf, wt_buf, noise_buf, clean_buf, kv_buf, sems,
):
    width = wt_buf.shape[1]
    group_rows, local = scale_ref.shape
    tok_dev = noise_buf.shape[1]
    rank = lax.axis_index("seq")
    pairs = [(mod_hbm, mod_buf), (wt_hbm, wt_buf), (noise_hbm, noise_buf), (clean_hbm, clean_buf)]
    pairs += [(kv_hbm.at[c], kv_buf.at[c]) for c in range(clips)]
    copies = [pltpu.make_async_copy(a, b, sems.at[i]) for i, (a, b) in enumerate(pairs)]
    for copy in copies:
        copy.start()
    for copy in copies[:4]:
        copy.wait()
    mods[...] = jnp.dot(act_ref[...], mod_buf[...], preferred_element_type=F32)
    weight = wt_buf[...].astype(F32)
    shifts = nt_dot(weight, mods[:, :width], EXACT)
    tok_clip = clip_index(info_ref, clips, (clips, tok_dev), 1, rank * tok_dev)
    picks = (tok_clip == lax.broadcasted_iota(jnp.int32, (clips, tok_dev), 0)).astype(F32)
    slot = lax.broadcasted_iota(jnp.int32, (clips, 1), 0)
    sizes = jnp.zeros((clips, 1), F32)
    for c in range(clips):
        sizes = jnp.where(slot == c, info_ref[c].astype(F32), sizes)
    share_ref[...] = picks / sizes
    for place, source in enumerate(origins(rank, sources)):
        low = pl.multiple_of(source * local, HEAD_DIM)
        scales = 1.0 + mods[:, pl.ds(pl.multiple_of(width + low, HEAD_DIM), local)]
        slopes = nt_dot(wt_buf[:, pl.ds(low, local)].astype(F32), scales, EXACT)
        slope_ref[place] = jnp.dot(slopes, picks, precision=EXACT, preferred_element_type=F32)
    offset_ref[...] = jnp.dot(shifts, picks, precision=EXACT, preferred_element_type=F32) - (
        noise_buf[...] - clean_buf[...]
    )
    row_clip = clip_index(info_ref, clips, (group_rows, clips), 0, 0)
    row_picks = (row_clip == lax.broadcasted_iota(jnp.int32, (group_rows, clips), 1)).astype(F32)
    mine = 1.0 + mods[:, pl.ds(pl.multiple_of(width + rank * local, HEAD_DIM), local)]
    scale_ref[...] = jnp.dot(row_picks, mine, precision=EXACT, preferred_element_type=F32)
    weight_ref[...] = wt_buf[:, pl.ds(pl.multiple_of(rank * local, HEAD_DIM), local)]
    for c in range(clips):
        copies[4 + c].wait()
        keys_ref[c] = kv_buf[c, :, 0, :]
        values_ref[c] = kv_buf[c, :, 1, :]


def text_kernel(sources, clips, window, info_ref, *refs):
    q_refs = refs[:sources]
    keys_ref, values_ref, out_ref, level_ref, q_all = refs[sources:]
    tok_dev, local = q_refs[0].shape[1:]
    heads = local // HEAD_DIM
    text_len = keys_ref.shape[1]
    for k, q_ref in enumerate(q_refs):
        q_all[source_rows(sources, k, tok_dev), :] = q_ref[0]
    slots = lax.broadcasted_iota(jnp.int32, (1, text_len), 1)
    ones = jnp.ones((text_len, HEAD_DIM), BF16)

    def one_clip(clip, start):
        first = pl.multiple_of(start // ALIGN * ALIGN, ALIGN)
        rows = pl.ds(first, window)
        edge = pl.ds(first, ALIGN)
        live = slots < info_ref[clips + clip]
        before = lax.broadcasted_iota(jnp.int32, (ALIGN, 1), 0) + first < start
        kept = [(out_ref[edge, head_cols(h)], level_ref[h, edge, :]) for h in range(heads)]
        scores = [nt_dot(q_all[rows, head_cols(h)], keys_ref[clip, :, head_cols(h)]) for h in range(heads)]
        weights, tops = [], []
        for score in scores:
            score = jnp.where(live, score, NEG)
            top = jnp.max(score, axis=1, keepdims=True)
            weights.append(jnp.exp2((score - top) * SCORE_SCALE).astype(BF16))
            tops.append(top)
        results = []
        for h in range(heads):
            beside = jnp.concatenate([values_ref[clip, :, head_cols(h)], ones], axis=1)
            mixed = jnp.dot(weights[h], beside, preferred_element_type=F32)
            total = mixed[:, HEAD_DIM:]
            results.append((mixed[:, :HEAD_DIM] / total, tops[h] * SCORE_SCALE + jnp.log2(total)))
        for h in range(heads):
            out_ref[rows, head_cols(h)] = results[h][0]
            level_ref[h, rows, :] = results[h][1]
            out_ref[edge, head_cols(h)] = jnp.where(before, kept[h][0], results[h][0][:ALIGN])
            level_ref[h, edge, :] = jnp.where(before, kept[h][1], results[h][1][:ALIGN])
        return start + info_ref[clip]

    lax.fori_loop(0, clips, one_clip, jnp.int32(0))


def reach_of(first, reach, group_rows):
    span = group_rows - reach[1]
    return jnp.clip(first - reach[0], 0, span) if span else jnp.int32(0)


def weigh_kernel(sources, clips, reach, info_ref, *refs):
    q_refs, k_refs = refs[:sources], refs[sources : 2 * sources - NEAR]
    text_ref, level_ref, weight_ref, base_ref, q_all, k_all = refs[2 * sources - NEAR :]
    tok_dev, local = q_refs[0].shape[1:]
    group_rows = q_all.shape[0]
    heads = local // HEAD_DIM
    for k in range(sources):
        rows = source_rows(sources, k, tok_dev)
        q_all[rows, :] = q_refs[k][0]
        k_all[rows, :] = q_refs[k][1] if k < NEAR else k_refs[k - NEAR][0]
    for first in range(0, group_rows, tok_dev):
        low = min(max(first - reach[0], 0), group_rows - reach[1])
        rows, span = slice(first, first + tok_dev), slice(low, low + reach[1])
        row_clip = clip_index(info_ref, clips, (tok_dev, 1), 0, first)
        live = row_clip == clip_index(info_ref, clips, (1, reach[1]), 1, low)
        scores = [nt_dot(q_all[rows, head_cols(h)], k_all[span, head_cols(h)]) for h in range(heads)]
        for h in range(heads):
            score = jnp.where(live, scores[h] * SCORE_SCALE, NEG)
            level = level_ref[h, rows, :]
            top = jnp.maximum(jnp.max(score, axis=1, keepdims=True), level)
            chunks = [slice(part, part + HEAD_DIM) for part in range(0, reach[1], HEAD_DIM)]
            weights = [jnp.exp2(score[:, cols] - top) for cols in chunks]
            fade = jnp.exp2(level - top)
            share = 1.0 / (jnp.sum(sum(weights[1:], weights[0]), axis=1, keepdims=True) + fade)
            for cols, weight in zip(chunks, weights):
                weight_ref[h, rows, cols] = (weight * share).astype(BF16)
            base_ref[rows, head_cols(h)] = (fade * share) * text_ref[rows, head_cols(h)]


def mix_kernel(sources, reach, place, *refs):
    v_refs = refs[:sources]
    weight_ref, base_ref, scale_ref, wt_ref, out_ref, v_all = refs[sources:]
    tok_dev, local = v_refs[0].shape[1:]
    group_rows = scale_ref.shape[0]
    heads = local // HEAD_DIM
    channels = wt_ref.shape[0]
    for k in range(sources):
        v_all[source_rows(sources, k, tok_dev), :] = v_refs[k][2 if k < NEAR else 0]
    count = out_ref.shape[1]
    first = pl.multiple_of(place(lax.axis_index("seq")) * tok_dev, tok_dev)
    rows = pl.ds(first, count)
    span = pl.ds(pl.multiple_of(reach_of(first, reach, group_rows), HEAD_DIM), reach[1])
    mixed = [
        jnp.dot(weight_ref[h, rows, :], v_all[span, head_cols(h)], preferred_element_type=F32) for h in range(heads)
    ]
    attended = jnp.concatenate([(mixed[h] + base_ref[rows, head_cols(h)]).astype(BF16) for h in range(heads)], axis=1)
    attended_full = attended.astype(F32)
    local_mean = jnp.sum(attended_full, axis=1, keepdims=True) * (1.0 / local)
    y_high, y_low = two_parts((attended_full - local_mean) * scale_ref[rows, :])
    s_high, s_low = two_parts(attended_full * attended_full)
    weight = wt_ref[...]
    every = jnp.ones((STAT_ROWS, local), BF16)
    out_ref[:channels, :] = (nt_dot(weight, y_high) + nt_dot(weight, y_low)).astype(out_ref.dtype)
    row = lax.broadcasted_iota(jnp.int32, (STAT_ROWS, count), 0)
    rest = jnp.where(row < 3, nt_dot(every, attended), nt_dot(every, s_high) + nt_dot(every, s_low))
    terms = jnp.zeros((STAT_ROWS, count), F32)
    for place in range(3):
        term = rest.astype(out_ref.dtype).astype(F32)
        terms = jnp.where((row == place) | (row == place + 3), term, terms)
        rest = rest - term
    out_ref[channels:, :] = terms.astype(out_ref.dtype)


def read_part(part, channels):
    stat = part[channels:]
    return part[:channels], stat[0:1] + stat[1:2] + stat[2:3], stat[3:4] + stat[4:5] + stat[5:6]


def merge_kernel(near_ref, far_ref, keep_ref, send_ref):
    tok_dev = keep_ref.shape[1]
    channels = near_ref.shape[0] - STAT_ROWS
    mine = lax.axis_index("seq") & 1
    for ref, half in ((send_ref, 1 - mine), (keep_ref, mine)):
        cols = pl.ds(pl.multiple_of(half * tok_dev, HEAD_DIM), tok_dev)
        near, near_sum, near_square = read_part(near_ref[:, cols], channels)
        far, far_sum, far_square = read_part(far_ref[:, cols].astype(F32), channels)
        ref[:channels, :] = near + far
        row = lax.broadcasted_iota(jnp.int32, (MERGED_ROWS, tok_dev), 0)
        stats = jnp.where(row == 0, near_sum, jnp.where(row == 1, far_sum, near_square + far_square))
        ref[channels:, :] = stats


def loss_kernel(count, merged, width, *refs):
    part_refs = refs[:count]
    slope_ref, offset_ref, share_ref, out_ref = refs[count:]
    sources, channels = slope_ref.shape[:2]
    clips = share_ref.shape[0]
    projected, sums, squares = [], [], []
    for ref in part_refs:
        part = ref[...].astype(F32)
        if merged:
            projected.append(part[:channels])
            sums += [part[channels : channels + 1], part[channels + 1 : channels + 2]]
            squares.append(part[channels + 2 : channels + 3])
        else:
            for place, value in zip((projected, sums, squares), read_part(part, channels)):
                place.append(value)
    center = sum(sums[1:], sums[0]) * (1.0 / width)
    spread = sum(squares[1:], squares[0]) * (1.0 / width) - center * center
    total = sum(projected[1:], projected[0])
    for place in range(sources):
        total = total + (sums[place] * (sources / width) - center) * slope_ref[place]
    diff = total * lax.rsqrt(spread + EPS) + offset_ref[...]
    error = jnp.sum(diff * diff, axis=0, keepdims=True) * (1.0 / channels)
    sums = jnp.sum(share_ref[...] * error, axis=1, keepdims=True)
    lanes = lax.broadcasted_iota(jnp.int32, (clips, out_ref.shape[2]), 1)
    mine = lanes == lax.broadcasted_iota(jnp.int32, lanes.shape, 0)
    row = jnp.sum(jnp.where(mine, sums, 0.0), axis=0, keepdims=True)
    out_ref[...] = jnp.broadcast_to(row[None], out_ref.shape)


def smem():
    return pl.BlockSpec(memory_space=pltpu.SMEM)


def vmem():
    return pl.BlockSpec(memory_space=pltpu.VMEM)


def hbm():
    return pl.BlockSpec(memory_space=pltpu.HBM)


def call(kernel, name, operands, results, scratch=(), scalars=(), in_hbm=(), pinned=True, flops=0, traffic=0):
    return pl.pallas_call(
        kernel,
        in_specs=[smem()] * len(scalars) + [hbm() if i in in_hbm else vmem() for i in range(len(operands))],
        out_specs=[vmem()] * len(results),
        out_shape=[pltpu.VMEM(*r) if pinned else jax.ShapeDtypeStruct(*r) for r in results],
        scratch_shapes=list(scratch),
        compiler_params=pltpu.CompilerParams(vmem_limit_bytes=VMEM_LIMIT),
        cost_estimate=pl.CostEstimate(flops=flops, bytes_accessed=traffic, transcendentals=0),
        name=name,
    )(*scalars, *(pltpu.with_memory_space_constraint(x, pltpu.HBM) if i in in_hbm else x for i, x in enumerate(operands)))


def per_device(
    queries, keys, values, text_kv, text_lengths, clip_lengths, timesteps, mod_weight, final_weight, noise, clean,
    report_order,
):
    tok_dev, width = queries.shape
    sources = lax.axis_size("seq")
    groups = lax.axis_size("dp")
    local = width // sources
    heads = local // HEAD_DIM
    group_rows = tok_dev * sources
    clips = clip_lengths.shape[1]
    text_len = text_kv.shape[1]
    clip_most = 2 * group_rows // clips
    window = clip_most + ALIGN
    padded = group_rows + window
    reach = (clip_most, min(group_rows, tok_dev + 2 * clip_most))
    channels = final_weight.shape[1]
    info = jnp.concatenate([clip_lengths[0], text_lengths])

    def cut(arrays, plan, name):
        count = sum(len(which) for _, which in plan)
        return list(
            call(
                functools.partial(cut_kernel, sources, plan), name, arrays,
                [((len(which), tok_dev, local), BF16) for _, which in plan],
                [pltpu.SemaphoreType.DMA((count,))], in_hbm=range(len(arrays)), traffic=4 * tok_dev * local * count,
            )
        )

    def onward(x, k):
        return lax.ppermute(x, "seq", [(i, partner(i, k, sources)) for i in range(sources)]) if k else x

    far = [*range(NEAR, sources)]
    q_pieces = cut([queries], [(k, (0,)) for k in far], "cut_first")
    q_blocks = [onward(piece, k) for k, piece in zip(far, q_pieces)]
    q_pieces[0], keys = lax.optimization_barrier((q_pieces[0], keys))
    pieces = cut(
        [queries, keys, values],
        [(k, (0, 1, 2)) for k in reversed(range(NEAR))] + [(k, (i,)) for i in (1, 2) for k in far],
        "cut_rest",
    )
    near_blocks = [onward(pieces[NEAR - 1 - k], k) for k in range(NEAR)]
    q_blocks = near_blocks + q_blocks
    k_blocks = [onward(piece, k) for k, piece in zip(far, pieces[NEAR:])]

    weight_t = final_weight.T
    activated = jax.nn.silu(step_embedding(timesteps)).astype(BF16)
    scale_tok, slope, offset, share, weight_local, text_keys, text_values = call(
        functools.partial(prep_kernel, sources, clips), "prep",
        [activated, mod_weight, weight_t, noise.T, clean.T, text_kv],
        [
            ((group_rows, local), F32), ((sources, channels, tok_dev), F32), ((channels, tok_dev), F32),
            ((clips, tok_dev), F32),
            ((channels, local), BF16), ((clips, text_len, local), BF16), ((clips, text_len, local), BF16),
        ],
        [
            pltpu.VMEM((clips, 2 * width), F32), pltpu.VMEM(mod_weight.shape, BF16),
            pltpu.VMEM(weight_t.shape, BF16), pltpu.VMEM((channels, tok_dev), F32),
            pltpu.VMEM((channels, tok_dev), F32), pltpu.VMEM(text_kv.shape, BF16),
            pltpu.SemaphoreType.DMA((4 + clips,)),
        ],
        scalars=[info], in_hbm=range(1, 6),
    )

    v_pieces, scale_tok = lax.optimization_barrier((pieces[NEAR + len(far) :], scale_tok))
    v_blocks = [onward(piece, k) for k, piece in zip(far, v_pieces)]

    text_out, level = call(
        functools.partial(text_kernel, sources, clips, window), "text", [*q_blocks, text_keys, text_values],
        [((padded, local), F32), ((heads, padded, HEAD_DIM), F32)],
        [pltpu.VMEM((padded, local), BF16)], scalars=[info],
    )

    weights, base = call(
        functools.partial(weigh_kernel, sources, clips, reach), "weigh", [*q_blocks, *k_blocks, text_out, level],
        [((heads, group_rows, reach[1]), BF16), ((group_rows, local), F32)],
        [pltpu.VMEM((group_rows, local), BF16)] * 2, scalars=[info],
    )

    def mix(place, tiles=1, dtype=BF16):
        return call(
            functools.partial(mix_kernel, sources, reach, place), "mix",
            [*near_blocks, *v_blocks, weights, base, scale_tok, weight_local],
            [((channels + STAT_ROWS, tiles * tok_dev), dtype)],
            [pltpu.VMEM((group_rows, local), BF16)], flops=4 * tok_dev * reach[1] * local, traffic=2**20,
        )[0]

    if sources == 4:
        arrived = onward(mix(lambda rank: (rank ^ 2) // 2 * 2, 2), 2)
        keep, send = call(
            merge_kernel, "merge", [mix(lambda rank: rank // 2 * 2, 2, F32), arrived],
            [((channels + MERGED_ROWS, tok_dev), F32)] * 2,
        )
        parts = [keep, onward(send, 1)]
    else:
        parts = [onward(mix(lambda rank, k=k: partner(rank, k, sources)), k) for k in reversed(range(sources))]

    (shares,) = call(
        functools.partial(loss_kernel, len(parts), sources == 4, width), "loss", [*parts, slope, offset, share],
        [((groups * sources, 1, HEAD_DIM), F32)],
    )
    everyone = lax.all_to_all(shares, ("dp", "seq"), split_axis=0, concat_axis=0, tiled=True)
    losses = jnp.sum(everyone.reshape(groups, sources, HEAD_DIM), axis=1)[:, :clips].reshape(1, -1)
    slots = jnp.arange(groups * clips, dtype=jnp.int32)
    return jnp.sum(jnp.where(report_order[:, None] == slots[None, :], losses, 0.0), axis=1)


def solution(mesh):
    in_specs = (
        P(("dp", "seq"), None),
        P(("dp", "seq"), None),
        P(("dp", "seq"), None),
        P("dp", None, None, "seq"),
        P("dp"),
        P("dp", None),
        P("dp"),
        P(),
        P(),
        P(("dp", "seq"), None),
        P(("dp", "seq"), None),
        P("dp"),
    )
    return jax.shard_map(per_device, mesh=mesh, in_specs=in_specs, out_specs=P("dp"), check_vma=False)
```

```python
import functools
import math

import jax
import jax.numpy as jnp
from jax import lax
from jax.experimental import pallas as pl
from jax.experimental.pallas import tpu as pltpu
from jax.sharding import PartitionSpec as P

HEAD_DIM = 128
FREQ = 256
EPS = 1e-06
NEG = -1e30
STAT_ROWS = 16
ALIGN = 16
NEAR = 2
F32 = jnp.float32
BF16 = jnp.bfloat16
EXACT = lax.Precision.HIGHEST
VMEM_LIMIT = 32 * 1024 * 1024
SCORE_SCALE = math.log2(math.e) / math.sqrt(HEAD_DIM)


def nt_dot(a, b, precision=None):
    return lax.dot_general(a, b, (((1,), (1,)), ((), ())), precision=precision, preferred_element_type=F32)


def two_parts(x):
    high = x.astype(BF16)
    return high, (x - high.astype(F32)).astype(BF16)


def head_cols(h):
    return slice(h * HEAD_DIM, (h + 1) * HEAD_DIM)


def step_embedding(timesteps):
    half_width = FREQ // 2
    frequency = jnp.exp(-math.log(10000.0) * jnp.arange(half_width, dtype=F32) / half_width)
    angles = timesteps.astype(F32)[:, None] * frequency[None, :]
    return jnp.concatenate([jnp.cos(angles), jnp.sin(angles)], axis=1)


def clip_index(info_ref, clips, shape, axis, first):
    places = lax.broadcasted_iota(jnp.int32, shape, axis) + first
    end = jnp.int32(0)
    index = jnp.zeros(shape, jnp.int32)
    for c in range(clips):
        end = end + info_ref[c]
        index = index + (places >= end).astype(jnp.int32)
    return index


def partner(rank, k, size):
    return rank ^ k if size & (size - 1) == 0 else (rank + k) % size


def source_rows(sources, k, tok_dev):
    rank = lax.axis_index("seq")
    source = partner(rank, k if sources & (sources - 1) == 0 else sources - k, sources)
    return pl.ds(pl.multiple_of(source * tok_dev, tok_dev), tok_dev)


def origins(rank, sources):
    ahead = reversed(range(sources))
    return [partner(rank, k if sources & (sources - 1) == 0 else sources - k, sources) for k in ahead]


def cut_kernel(sources, plan, *refs):
    count = len(refs) - 1 - len(plan)
    wholes, pieces, sems = refs[:count], refs[count:-1], refs[-1]
    local = pieces[0].shape[2]
    copies = []
    for (k, which), piece in zip(plan, pieces):
        target = partner(lax.axis_index("seq"), k, sources)
        for place, i in enumerate(which):
            columns = pl.ds(pl.multiple_of(target * local, HEAD_DIM), local)
            copies.append(pltpu.make_async_copy(wholes[i].at[:, columns], piece.at[place], sems.at[len(copies)]))
            copies[-1].start()
    for copy in copies:
        copy.wait()


def prep_kernel(
    sources, clips, info_ref, act_ref, mod_hbm, wt_hbm, noise_hbm, clean_hbm, kv_hbm,
    scale_ref, slope_ref, offset_ref, share_ref, weight_ref, keys_ref, values_ref,
    mods, mod_buf, wt_buf, noise_buf, clean_buf, kv_buf, sems,
):
    width = wt_buf.shape[1]
    group_rows, local = scale_ref.shape
    tok_dev = noise_buf.shape[1]
    rank = lax.axis_index("seq")
    pairs = [(mod_hbm, mod_buf), (wt_hbm, wt_buf), (noise_hbm, noise_buf), (clean_hbm, clean_buf)]
    pairs += [(kv_hbm.at[c], kv_buf.at[c]) for c in range(clips)]
    copies = [pltpu.make_async_copy(a, b, sems.at[i]) for i, (a, b) in enumerate(pairs)]
    for copy in copies:
        copy.start()
    for copy in copies[:4]:
        copy.wait()
    mods[...] = jnp.dot(act_ref[...], mod_buf[...], preferred_element_type=F32)
    weight = wt_buf[...].astype(F32)
    shifts = nt_dot(weight, mods[:, :width], EXACT)
    tok_clip = clip_index(info_ref, clips, (clips, tok_dev), 1, rank * tok_dev)
    picks = (tok_clip == lax.broadcasted_iota(jnp.int32, (clips, tok_dev), 0)).astype(F32)
    slot = lax.broadcasted_iota(jnp.int32, (clips, 1), 0)
    sizes = jnp.zeros((clips, 1), F32)
    for c in range(clips):
        sizes = jnp.where(slot == c, info_ref[c].astype(F32), sizes)
    share_ref[...] = picks / sizes
    for place, source in enumerate(origins(rank, sources)):
        low = pl.multiple_of(source * local, HEAD_DIM)
        scales = 1.0 + mods[:, pl.ds(pl.multiple_of(width + low, HEAD_DIM), local)]
        slopes = nt_dot(wt_buf[:, pl.ds(low, local)].astype(F32), scales, EXACT)
        slope_ref[place] = jnp.dot(slopes, picks, precision=EXACT, preferred_element_type=F32)
    offset_ref[...] = jnp.dot(shifts, picks, precision=EXACT, preferred_element_type=F32) - (
        noise_buf[...] - clean_buf[...]
    )
    row_clip = clip_index(info_ref, clips, (group_rows, clips), 0, 0)
    row_picks = (row_clip == lax.broadcasted_iota(jnp.int32, (group_rows, clips), 1)).astype(F32)
    mine = 1.0 + mods[:, pl.ds(pl.multiple_of(width + rank * local, HEAD_DIM), local)]
    scale_ref[...] = jnp.dot(row_picks, mine, precision=EXACT, preferred_element_type=F32)
    weight_ref[...] = wt_buf[:, pl.ds(pl.multiple_of(rank * local, HEAD_DIM), local)]
    for c in range(clips):
        copies[4 + c].wait()
        keys_ref[c] = kv_buf[c, :, 0, :]
        values_ref[c] = kv_buf[c, :, 1, :]


def text_kernel(sources, clips, window, info_ref, *refs):
    q_refs = refs[:sources]
    keys_ref, values_ref, out_ref, level_ref, q_all = refs[sources:]
    tok_dev, local = q_refs[0].shape[1:]
    heads = local // HEAD_DIM
    text_len = keys_ref.shape[1]
    for k, q_ref in enumerate(q_refs):
        q_all[source_rows(sources, k, tok_dev), :] = q_ref[0]
    slots = lax.broadcasted_iota(jnp.int32, (1, text_len), 1)
    ones = jnp.ones((text_len, HEAD_DIM), BF16)

    def one_clip(clip, start):
        first = pl.multiple_of(start // ALIGN * ALIGN, ALIGN)
        rows = pl.ds(first, window)
        edge = pl.ds(first, ALIGN)
        live = slots < info_ref[clips + clip]
        before = lax.broadcasted_iota(jnp.int32, (ALIGN, 1), 0) + first < start
        kept = [(out_ref[edge, head_cols(h)], level_ref[h, edge, :]) for h in range(heads)]
        scores = [nt_dot(q_all[rows, head_cols(h)], keys_ref[clip, :, head_cols(h)]) for h in range(heads)]
        weights, tops = [], []
        for score in scores:
            score = jnp.where(live, score, NEG)
            top = jnp.max(score, axis=1, keepdims=True)
            weights.append(jnp.exp2((score - top) * SCORE_SCALE).astype(BF16))
            tops.append(top)
        results = []
        for h in range(heads):
            beside = jnp.concatenate([values_ref[clip, :, head_cols(h)], ones], axis=1)
            mixed = jnp.dot(weights[h], beside, preferred_element_type=F32)
            total = mixed[:, HEAD_DIM:]
            results.append((mixed[:, :HEAD_DIM] / total, tops[h] * SCORE_SCALE + jnp.log2(total)))
        for h in range(heads):
            out_ref[rows, head_cols(h)] = results[h][0]
            level_ref[h, rows, :] = results[h][1]
            out_ref[edge, head_cols(h)] = jnp.where(before, kept[h][0], results[h][0][:ALIGN])
            level_ref[h, edge, :] = jnp.where(before, kept[h][1], results[h][1][:ALIGN])
        return start + info_ref[clip]

    lax.fori_loop(0, clips, one_clip, jnp.int32(0))


def reach_of(first, reach, group_rows):
    span = group_rows - reach[1]
    return jnp.clip(first - reach[0], 0, span) if span else jnp.int32(0)


def weigh_kernel(sources, clips, reach, info_ref, *refs):
    q_refs, k_refs = refs[:sources], refs[sources : 2 * sources - NEAR]
    text_ref, level_ref, weight_ref, base_ref, q_all, k_all = refs[2 * sources - NEAR :]
    tok_dev, local = q_refs[0].shape[1:]
    group_rows = q_all.shape[0]
    heads = local // HEAD_DIM
    for k in range(sources):
        rows = source_rows(sources, k, tok_dev)
        q_all[rows, :] = q_refs[k][0]
        k_all[rows, :] = q_refs[k][1] if k < NEAR else k_refs[k - NEAR][0]
    for first in range(0, group_rows, tok_dev):
        low = min(max(first - reach[0], 0), group_rows - reach[1])
        rows, span = slice(first, first + tok_dev), slice(low, low + reach[1])
        row_clip = clip_index(info_ref, clips, (tok_dev, 1), 0, first)
        live = row_clip == clip_index(info_ref, clips, (1, reach[1]), 1, low)
        scores = [nt_dot(q_all[rows, head_cols(h)], k_all[span, head_cols(h)]) for h in range(heads)]
        for h in range(heads):
            score = jnp.where(live, scores[h] * SCORE_SCALE, NEG)
            level = level_ref[h, rows, :]
            top = jnp.maximum(jnp.max(score, axis=1, keepdims=True), level)
            chunks = [slice(part, part + HEAD_DIM) for part in range(0, reach[1], HEAD_DIM)]
            weights = [jnp.exp2(score[:, cols] - top) for cols in chunks]
            fade = jnp.exp2(level - top)
            share = 1.0 / (jnp.sum(sum(weights[1:], weights[0]), axis=1, keepdims=True) + fade)
            for cols, weight in zip(chunks, weights):
                weight_ref[h, rows, cols] = (weight * share).astype(BF16)
            base_ref[rows, head_cols(h)] = (fade * share) * text_ref[rows, head_cols(h)]


def mix_kernel(sources, reach, k_target, *refs):
    v_refs = refs[:sources]
    weight_ref, base_ref, scale_ref, wt_ref, out_ref, v_all = refs[sources:]
    tok_dev, local = v_refs[0].shape[1:]
    group_rows = scale_ref.shape[0]
    heads = local // HEAD_DIM
    channels = wt_ref.shape[0]
    for k in range(sources):
        v_all[source_rows(sources, k, tok_dev), :] = v_refs[k][2 if k < NEAR else 0]
    count = out_ref.shape[1]
    first = pl.multiple_of(partner(lax.axis_index("seq"), k_target, sources) * tok_dev, tok_dev)
    rows = pl.ds(first, count)
    span = pl.ds(pl.multiple_of(reach_of(first, reach, group_rows), HEAD_DIM), reach[1])
    mixed = [
        jnp.dot(weight_ref[h, rows, :], v_all[span, head_cols(h)], preferred_element_type=F32) for h in range(heads)
    ]
    attended = jnp.concatenate([(mixed[h] + base_ref[rows, head_cols(h)]).astype(BF16) for h in range(heads)], axis=1)
    attended_full = attended.astype(F32)
    local_mean = jnp.sum(attended_full, axis=1, keepdims=True) * (1.0 / local)
    y_high, y_low = two_parts((attended_full - local_mean) * scale_ref[rows, :])
    s_high, s_low = two_parts(attended_full * attended_full)
    weight = wt_ref[...]
    every = jnp.ones((STAT_ROWS, local), BF16)
    out_ref[:channels, :] = (nt_dot(weight, y_high) + nt_dot(weight, y_low)).astype(out_ref.dtype)
    row = lax.broadcasted_iota(jnp.int32, (STAT_ROWS, count), 0)
    rest = jnp.where(row < 3, nt_dot(every, attended), nt_dot(every, s_high) + nt_dot(every, s_low))
    terms = jnp.zeros((STAT_ROWS, count), F32)
    for place in range(3):
        term = rest.astype(out_ref.dtype).astype(F32)
        terms = jnp.where((row == place) | (row == place + 3), term, terms)
        rest = rest - term
    out_ref[channels:, :] = terms.astype(out_ref.dtype)


def read_part(part, channels):
    stat = part[channels:]
    return part[:channels], stat[0:1] + stat[1:2] + stat[2:3], stat[3:4] + stat[4:5] + stat[5:6]


def loss_kernel(sources, width, *refs):
    part_refs = refs[:sources]
    slope_ref, offset_ref, share_ref, out_ref = refs[sources:]
    channels = slope_ref.shape[1]
    clips = share_ref.shape[0]
    projected, sums, squares = [], [], []
    for ref in part_refs:
        for place, value in zip((projected, sums, squares), read_part(ref[...].astype(F32), channels)):
            place.append(value)
    center = sum(sums[1:], sums[0]) * (1.0 / width)
    spread = sum(squares[1:], squares[0]) * (1.0 / width) - center * center
    total = sum(projected[1:], projected[0])
    for place in range(sources):
        total = total + (sums[place] * (sources / width) - center) * slope_ref[place]
    diff = total * lax.rsqrt(spread + EPS) + offset_ref[...]
    error = jnp.sum(diff * diff, axis=0, keepdims=True) * (1.0 / channels)
    sums = jnp.sum(share_ref[...] * error, axis=1, keepdims=True)
    lanes = lax.broadcasted_iota(jnp.int32, (clips, out_ref.shape[2]), 1)
    mine = lanes == lax.broadcasted_iota(jnp.int32, lanes.shape, 0)
    row = jnp.sum(jnp.where(mine, sums, 0.0), axis=0, keepdims=True)
    out_ref[...] = jnp.broadcast_to(row[None], out_ref.shape)


def smem():
    return pl.BlockSpec(memory_space=pltpu.SMEM)


def vmem():
    return pl.BlockSpec(memory_space=pltpu.VMEM)


def hbm():
    return pl.BlockSpec(memory_space=pltpu.HBM)


def call(kernel, name, operands, results, scratch=(), scalars=(), in_hbm=(), pinned=True, flops=0, traffic=0):
    return pl.pallas_call(
        kernel,
        in_specs=[smem()] * len(scalars) + [hbm() if i in in_hbm else vmem() for i in range(len(operands))],
        out_specs=[vmem()] * len(results),
        out_shape=[pltpu.VMEM(*r) if pinned else jax.ShapeDtypeStruct(*r) for r in results],
        scratch_shapes=list(scratch),
        compiler_params=pltpu.CompilerParams(vmem_limit_bytes=VMEM_LIMIT),
        cost_estimate=pl.CostEstimate(flops=flops, bytes_accessed=traffic, transcendentals=0),
        name=name,
    )(*scalars, *(pltpu.with_memory_space_constraint(x, pltpu.HBM) if i in in_hbm else x for i, x in enumerate(operands)))


def per_device(
    queries, keys, values, text_kv, text_lengths, clip_lengths, timesteps, mod_weight, final_weight, noise, clean,
    report_order,
):
    tok_dev, width = queries.shape
    sources = lax.axis_size("seq")
    groups = lax.axis_size("dp")
    local = width // sources
    heads = local // HEAD_DIM
    group_rows = tok_dev * sources
    clips = clip_lengths.shape[1]
    text_len = text_kv.shape[1]
    clip_most = 2 * group_rows // clips
    window = clip_most + ALIGN
    padded = group_rows + window
    reach = (clip_most, min(group_rows, tok_dev + 2 * clip_most))
    channels = final_weight.shape[1]
    info = jnp.concatenate([clip_lengths[0], text_lengths])

    def cut(arrays, plan, name):
        count = sum(len(which) for _, which in plan)
        return list(
            call(
                functools.partial(cut_kernel, sources, plan), name, arrays,
                [((len(which), tok_dev, local), BF16) for _, which in plan],
                [pltpu.SemaphoreType.DMA((count,))], in_hbm=range(len(arrays)), traffic=4 * tok_dev * local * count,
            )
        )

    def onward(x, k):
        return lax.ppermute(x, "seq", [(i, partner(i, k, sources)) for i in range(sources)]) if k else x

    far = [*range(NEAR, sources)]
    q_pieces = cut([queries], [(k, (0,)) for k in far], "cut_first")
    q_blocks = [onward(piece, k) for k, piece in zip(far, q_pieces)]
    q_pieces[0], keys = lax.optimization_barrier((q_pieces[0], keys))
    pieces = cut(
        [queries, keys, values],
        [(k, (0, 1, 2)) for k in reversed(range(NEAR))] + [(k, (i,)) for i in (1, 2) for k in far],
        "cut_rest",
    )
    near_blocks = [onward(pieces[NEAR - 1 - k], k) for k in range(NEAR)]
    q_blocks = near_blocks + q_blocks
    k_blocks = [onward(piece, k) for k, piece in zip(far, pieces[NEAR:])]

    weight_t = final_weight.T
    activated = jax.nn.silu(step_embedding(timesteps)).astype(BF16)
    scale_tok, slope, offset, share, weight_local, text_keys, text_values = call(
        functools.partial(prep_kernel, sources, clips), "prep",
        [activated, mod_weight, weight_t, noise.T, clean.T, text_kv],
        [
            ((group_rows, local), F32), ((sources, channels, tok_dev), F32), ((channels, tok_dev), F32),
            ((clips, tok_dev), F32),
            ((channels, local), BF16), ((clips, text_len, local), BF16), ((clips, text_len, local), BF16),
        ],
        [
            pltpu.VMEM((clips, 2 * width), F32), pltpu.VMEM(mod_weight.shape, BF16),
            pltpu.VMEM(weight_t.shape, BF16), pltpu.VMEM((channels, tok_dev), F32),
            pltpu.VMEM((channels, tok_dev), F32), pltpu.VMEM(text_kv.shape, BF16),
            pltpu.SemaphoreType.DMA((4 + clips,)),
        ],
        scalars=[info], in_hbm=range(1, 6),
    )

    v_pieces, scale_tok = lax.optimization_barrier((pieces[NEAR + len(far) :], scale_tok))
    v_blocks = [onward(piece, k) for k, piece in zip(far, v_pieces)]

    text_out, level = call(
        functools.partial(text_kernel, sources, clips, window), "text", [*q_blocks, text_keys, text_values],
        [((padded, local), F32), ((heads, padded, HEAD_DIM), F32)],
        [pltpu.VMEM((padded, local), BF16)], scalars=[info],
    )

    weights, base = call(
        functools.partial(weigh_kernel, sources, clips, reach), "weigh", [*q_blocks, *k_blocks, text_out, level],
        [((heads, group_rows, reach[1]), BF16), ((group_rows, local), F32)],
        [pltpu.VMEM((group_rows, local), BF16)] * 2, scalars=[info],
    )

    parts = []
    for k in reversed(range(sources)):
        (part,) = call(
            functools.partial(mix_kernel, sources, reach, k), "mix",
            [*near_blocks, *v_blocks, weights, base, scale_tok, weight_local],
            [((channels + STAT_ROWS, tok_dev), BF16)],
            [pltpu.VMEM((group_rows, local), BF16)], flops=4 * tok_dev * reach[1] * local, traffic=2**20,
        )
        parts.append(onward(part, k))

    (shares,) = call(
        functools.partial(loss_kernel, sources, width), "loss", [*parts, slope, offset, share],
        [((groups * sources, 1, HEAD_DIM), F32)],
    )
    everyone = lax.all_to_all(shares, ("dp", "seq"), split_axis=0, concat_axis=0, tiled=True)
    losses = jnp.sum(everyone.reshape(groups, sources, HEAD_DIM), axis=1)[:, :clips].reshape(1, -1)
    slots = jnp.arange(groups * clips, dtype=jnp.int32)
    return jnp.sum(jnp.where(report_order[:, None] == slots[None, :], losses, 0.0), axis=1)


def solution(mesh):
    in_specs = (
        P(("dp", "seq"), None),
        P(("dp", "seq"), None),
        P(("dp", "seq"), None),
        P("dp", None, None, "seq"),
        P("dp"),
        P("dp", None),
        P("dp"),
        P(),
        P(),
        P(("dp", "seq"), None),
        P(("dp", "seq"), None),
        P("dp"),
    )
    return jax.shard_map(per_device, mesh=mesh, in_specs=in_specs, out_specs=P("dp"), check_vma=False)
```

```python
import functools
import math

import jax
import jax.numpy as jnp
from jax import lax
from jax.experimental import pallas as pl
from jax.experimental.pallas import tpu as pltpu
from jax.sharding import PartitionSpec as P

HEAD_DIM = 128
FREQ = 256
EPS = 1e-06
NEG = -1e30
STAT_ROWS = 16
ALIGN = 16
NEAR = 2
F32 = jnp.float32
BF16 = jnp.bfloat16
EXACT = lax.Precision.HIGHEST
VMEM_LIMIT = 32 * 1024 * 1024
SCORE_SCALE = math.log2(math.e) / math.sqrt(HEAD_DIM)


def nt_dot(a, b, precision=None):
    return lax.dot_general(a, b, (((1,), (1,)), ((), ())), precision=precision, preferred_element_type=F32)


def head_cols(h):
    return slice(h * HEAD_DIM, (h + 1) * HEAD_DIM)


def step_embedding(timesteps):
    half_width = FREQ // 2
    frequency = jnp.exp(-math.log(10000.0) * jnp.arange(half_width, dtype=F32) / half_width)
    angles = timesteps.astype(F32)[:, None] * frequency[None, :]
    return jnp.concatenate([jnp.cos(angles), jnp.sin(angles)], axis=1)


def clip_index(info_ref, clips, shape, axis, first):
    places = lax.broadcasted_iota(jnp.int32, shape, axis) + first
    end = jnp.int32(0)
    index = jnp.zeros(shape, jnp.int32)
    for c in range(clips):
        end = end + info_ref[c]
        index = index + (places >= end).astype(jnp.int32)
    return index


def partner(rank, k, size):
    return rank ^ k if size & (size - 1) == 0 else (rank + k) % size


def source_rows(sources, k, tok_dev):
    rank = lax.axis_index("seq")
    source = partner(rank, k if sources & (sources - 1) == 0 else sources - k, sources)
    return pl.ds(pl.multiple_of(source * tok_dev, tok_dev), tok_dev)


def origins(rank, sources):
    ahead = reversed(range(sources))
    return [partner(rank, k if sources & (sources - 1) == 0 else sources - k, sources) for k in ahead]


def cut_kernel(sources, plan, *refs):
    count = len(refs) - 1 - len(plan)
    wholes, pieces, sems = refs[:count], refs[count:-1], refs[-1]
    local = pieces[0].shape[2]
    copies = []
    for (k, which), piece in zip(plan, pieces):
        target = partner(lax.axis_index("seq"), k, sources)
        for place, i in enumerate(which):
            columns = pl.ds(pl.multiple_of(target * local, HEAD_DIM), local)
            copies.append(pltpu.make_async_copy(wholes[i].at[:, columns], piece.at[place], sems.at[len(copies)]))
            copies[-1].start()
    for copy in copies:
        copy.wait()


def prep_kernel(
    sources, clips, info_ref, act_ref, mod_hbm, wt_hbm, noise_hbm, clean_hbm, kv_hbm,
    scale_ref, slope_ref, offset_ref, share_ref, weight_ref, keys_ref, values_ref,
    mods, mod_buf, wt_buf, noise_buf, clean_buf, kv_buf, sems,
):
    width = wt_buf.shape[1]
    group_rows, local = scale_ref.shape
    tok_dev = noise_buf.shape[1]
    rank = lax.axis_index("seq")
    pairs = [(mod_hbm, mod_buf), (wt_hbm, wt_buf), (noise_hbm, noise_buf), (clean_hbm, clean_buf)]
    pairs += [(kv_hbm.at[c], kv_buf.at[c]) for c in range(clips)]
    copies = [pltpu.make_async_copy(a, b, sems.at[i]) for i, (a, b) in enumerate(pairs)]
    for copy in copies:
        copy.start()
    for copy in copies[:4]:
        copy.wait()
    mods[...] = jnp.dot(act_ref[...], mod_buf[...], preferred_element_type=F32)
    weight = wt_buf[...].astype(F32)
    shifts = nt_dot(weight, mods[:, :width], EXACT)
    tok_clip = clip_index(info_ref, clips, (clips, tok_dev), 1, rank * tok_dev)
    picks = (tok_clip == lax.broadcasted_iota(jnp.int32, (clips, tok_dev), 0)).astype(F32)
    slot = lax.broadcasted_iota(jnp.int32, (clips, 1), 0)
    sizes = jnp.zeros((clips, 1), F32)
    for c in range(clips):
        sizes = jnp.where(slot == c, info_ref[c].astype(F32), sizes)
    share_ref[...] = picks / sizes
    for place, source in enumerate(origins(rank, sources)):
        low = pl.multiple_of(source * local, HEAD_DIM)
        scales = 1.0 + mods[:, pl.ds(pl.multiple_of(width + low, HEAD_DIM), local)]
        slopes = nt_dot(wt_buf[:, pl.ds(low, local)].astype(F32), scales, EXACT)
        slope_ref[place] = jnp.dot(slopes, picks, precision=EXACT, preferred_element_type=F32)
    offset_ref[...] = jnp.dot(shifts, picks, precision=EXACT, preferred_element_type=F32) - (
        noise_buf[...] - clean_buf[...]
    )
    row_clip = clip_index(info_ref, clips, (group_rows, clips), 0, 0)
    row_picks = (row_clip == lax.broadcasted_iota(jnp.int32, (group_rows, clips), 1)).astype(F32)
    mine = 1.0 + mods[:, pl.ds(pl.multiple_of(width + rank * local, HEAD_DIM), local)]
    scale_ref[...] = jnp.dot(row_picks, mine, precision=EXACT, preferred_element_type=F32)
    weight_ref[...] = wt_buf[:, pl.ds(pl.multiple_of(rank * local, HEAD_DIM), local)]
    for c in range(clips):
        copies[4 + c].wait()
        keys_ref[c] = kv_buf[c, :, 0, :]
        values_ref[c] = kv_buf[c, :, 1, :]


def text_kernel(sources, clips, window, info_ref, *refs):
    q_refs = refs[:sources]
    keys_ref, values_ref, out_ref, level_ref, q_all = refs[sources:]
    tok_dev, local = q_refs[0].shape[1:]
    heads = local // HEAD_DIM
    text_len = keys_ref.shape[1]
    for k, q_ref in enumerate(q_refs):
        q_all[source_rows(sources, k, tok_dev), :] = q_ref[0]
    slots = lax.broadcasted_iota(jnp.int32, (1, text_len), 1)
    ones = jnp.ones((text_len, HEAD_DIM), BF16)

    def one_clip(clip, start):
        first = pl.multiple_of(start // ALIGN * ALIGN, ALIGN)
        rows = pl.ds(first, window)
        edge = pl.ds(first, ALIGN)
        live = slots < info_ref[clips + clip]
        before = lax.broadcasted_iota(jnp.int32, (ALIGN, 1), 0) + first < start
        kept = [(out_ref[edge, head_cols(h)], level_ref[h, edge, :]) for h in range(heads)]
        scores = [nt_dot(q_all[rows, head_cols(h)], keys_ref[clip, :, head_cols(h)]) for h in range(heads)]
        weights, tops = [], []
        for score in scores:
            score = jnp.where(live, score, NEG)
            top = jnp.max(score, axis=1, keepdims=True)
            weights.append(jnp.exp2((score - top) * SCORE_SCALE).astype(BF16))
            tops.append(top)
        results = []
        for h in range(heads):
            beside = jnp.concatenate([values_ref[clip, :, head_cols(h)], ones], axis=1)
            mixed = jnp.dot(weights[h], beside, preferred_element_type=F32)
            total = mixed[:, HEAD_DIM:]
            results.append((mixed[:, :HEAD_DIM] / total, tops[h] * SCORE_SCALE + jnp.log2(total)))
        for h in range(heads):
            out_ref[rows, head_cols(h)] = results[h][0]
            level_ref[h, rows, :] = results[h][1]
            out_ref[edge, head_cols(h)] = jnp.where(before, kept[h][0], results[h][0][:ALIGN])
            level_ref[h, edge, :] = jnp.where(before, kept[h][1], results[h][1][:ALIGN])
        return start + info_ref[clip]

    lax.fori_loop(0, clips, one_clip, jnp.int32(0))


def reach_of(first, reach, group_rows):
    span = group_rows - reach[1]
    return jnp.clip(first - reach[0], 0, span) if span else jnp.int32(0)


def weigh_kernel(sources, clips, reach, info_ref, *refs):
    q_refs, k_refs = refs[:sources], refs[sources : 2 * sources - NEAR]
    text_ref, level_ref, weight_ref, base_ref, q_all, k_all = refs[2 * sources - NEAR :]
    tok_dev, local = q_refs[0].shape[1:]
    group_rows = q_all.shape[0]
    heads = local // HEAD_DIM
    for k in range(sources):
        rows = source_rows(sources, k, tok_dev)
        q_all[rows, :] = q_refs[k][0]
        k_all[rows, :] = q_refs[k][1] if k < NEAR else k_refs[k - NEAR][0]
    for first in range(0, group_rows, tok_dev):
        low = min(max(first - reach[0], 0), group_rows - reach[1])
        rows, span = slice(first, first + tok_dev), slice(low, low + reach[1])
        row_clip = clip_index(info_ref, clips, (tok_dev, 1), 0, first)
        live = row_clip == clip_index(info_ref, clips, (1, reach[1]), 1, low)
        scores = [nt_dot(q_all[rows, head_cols(h)], k_all[span, head_cols(h)]) for h in range(heads)]
        for h in range(heads):
            score = jnp.where(live, scores[h] * SCORE_SCALE, NEG)
            level = level_ref[h, rows, :]
            top = jnp.maximum(jnp.max(score, axis=1, keepdims=True), level)
            chunks = [slice(part, part + HEAD_DIM) for part in range(0, reach[1], HEAD_DIM)]
            weights = [jnp.exp2(score[:, cols] - top) for cols in chunks]
            fade = jnp.exp2(level - top)
            share = 1.0 / (jnp.sum(sum(weights[1:], weights[0]), axis=1, keepdims=True) + fade)
            for cols, weight in zip(chunks, weights):
                weight_ref[h, rows, cols] = (weight * share).astype(BF16)
            base_ref[rows, head_cols(h)] = (fade * share) * text_ref[rows, head_cols(h)]


def mix_kernel(sources, reach, k_target, *refs):
    v_refs = refs[:sources]
    weight_ref, base_ref, scale_ref, wt_ref, out_ref, v_all = refs[sources:]
    tok_dev, local = v_refs[0].shape[1:]
    group_rows = scale_ref.shape[0]
    heads = local // HEAD_DIM
    channels = wt_ref.shape[0]
    for k in range(sources):
        v_all[source_rows(sources, k, tok_dev), :] = v_refs[k][2 if k < NEAR else 0]
    count = out_ref.shape[1]
    first = pl.multiple_of(partner(lax.axis_index("seq"), k_target, sources) * tok_dev, tok_dev)
    rows = pl.ds(first, count)
    span = pl.ds(pl.multiple_of(reach_of(first, reach, group_rows), HEAD_DIM), reach[1])
    mixed = [
        jnp.dot(weight_ref[h, rows, :], v_all[span, head_cols(h)], preferred_element_type=F32) for h in range(heads)
    ]
    attended = jnp.concatenate([(mixed[h] + base_ref[rows, head_cols(h)]).astype(BF16) for h in range(heads)], axis=1)
    attended_full = attended.astype(F32)
    local_mean = jnp.sum(attended_full, axis=1, keepdims=True) * (1.0 / local)
    centred = attended_full - local_mean
    weight = wt_ref[...]
    every = jnp.ones((STAT_ROWS, local), BF16)
    out_ref[:channels, :] = nt_dot(weight, (centred * scale_ref[rows, :]).astype(BF16)).astype(BF16)
    row = lax.broadcasted_iota(jnp.int32, (STAT_ROWS, count), 0)
    rest = jnp.where(row < 3, nt_dot(every, attended), nt_dot(every, (centred * centred).astype(BF16)))
    terms = jnp.zeros((STAT_ROWS, count), F32)
    for place in range(3):
        term = rest.astype(BF16).astype(F32)
        terms = jnp.where((row == place) | (row == place + 3), term, terms)
        rest = rest - term
    out_ref[channels:, :] = terms.astype(BF16)


def read_part(part, channels):
    stat = part[channels:]
    return part[:channels], stat[0:1] + stat[1:2] + stat[2:3], stat[3:4] + stat[4:5] + stat[5:6]


def loss_kernel(sources, width, *refs):
    part_refs = refs[:sources]
    slope_ref, offset_ref, share_ref, out_ref = refs[sources:]
    channels = slope_ref.shape[1]
    clips = share_ref.shape[0]
    projected, sums, squares = [], [], []
    for ref in part_refs:
        for place, value in zip((projected, sums, squares), read_part(ref[...].astype(F32), channels)):
            place.append(value)
    center = sum(sums[1:], sums[0]) * (1.0 / width)
    strays = [value * (sources / width) - center for value in sums]
    spread = sum(squares[1:], squares[0]) * (1.0 / width) + sum(stray * stray for stray in strays) * (1.0 / sources)
    total = sum(projected[1:], projected[0])
    for place in range(sources):
        total = total + strays[place] * slope_ref[place]
    diff = total * lax.rsqrt(spread + EPS) + offset_ref[...]
    error = jnp.sum(diff * diff, axis=0, keepdims=True) * (1.0 / channels)
    sums = jnp.sum(share_ref[...] * error, axis=1, keepdims=True)
    lanes = lax.broadcasted_iota(jnp.int32, (clips, out_ref.shape[2]), 1)
    mine = lanes == lax.broadcasted_iota(jnp.int32, lanes.shape, 0)
    row = jnp.sum(jnp.where(mine, sums, 0.0), axis=0, keepdims=True)
    out_ref[...] = jnp.broadcast_to(row[None], out_ref.shape)


def pick_kernel(clips, losses_ref, order_ref, out_ref):
    losses = jnp.sum(losses_ref[...], axis=1)
    order = order_ref[...]
    column = lax.broadcasted_iota(jnp.int32, (losses.shape[1], order.shape[1]), 0)
    chosen = (column == lax.rem(order, clips)).astype(F32)
    by_group = jnp.dot(losses, chosen, precision=EXACT, preferred_element_type=F32)
    group = lax.broadcasted_iota(jnp.int32, by_group.shape, 0)
    out_ref[...] = jnp.sum(jnp.where(group == lax.div(order, clips), by_group, 0.0), axis=0, keepdims=True)


def smem():
    return pl.BlockSpec(memory_space=pltpu.SMEM)


def vmem():
    return pl.BlockSpec(memory_space=pltpu.VMEM)


def hbm():
    return pl.BlockSpec(memory_space=pltpu.HBM)


def call(kernel, name, operands, results, scratch=(), scalars=(), in_hbm=(), pinned=True, flops=0, traffic=0):
    return pl.pallas_call(
        kernel,
        in_specs=[smem()] * len(scalars) + [hbm() if i in in_hbm else vmem() for i in range(len(operands))],
        out_specs=[vmem()] * len(results),
        out_shape=[pltpu.VMEM(*r) if pinned else jax.ShapeDtypeStruct(*r) for r in results],
        scratch_shapes=list(scratch),
        compiler_params=pltpu.CompilerParams(vmem_limit_bytes=VMEM_LIMIT),
        cost_estimate=pl.CostEstimate(flops=flops, bytes_accessed=traffic, transcendentals=0),
        name=name,
    )(*scalars, *(pltpu.with_memory_space_constraint(x, pltpu.HBM) if i in in_hbm else x for i, x in enumerate(operands)))


def per_device(
    queries, keys, values, text_kv, text_lengths, clip_lengths, timesteps, mod_weight, final_weight, noise, clean,
    report_order,
):
    tok_dev, width = queries.shape
    sources = lax.axis_size("seq")
    groups = lax.axis_size("dp")
    local = width // sources
    heads = local // HEAD_DIM
    group_rows = tok_dev * sources
    clips = clip_lengths.shape[1]
    text_len = text_kv.shape[1]
    clip_most = 2 * group_rows // clips
    window = clip_most + ALIGN
    padded = group_rows + window
    reach = (clip_most, min(group_rows, tok_dev + 2 * clip_most))
    channels = final_weight.shape[1]
    info = jnp.concatenate([clip_lengths[0], text_lengths])

    def cut(arrays, plan, name):
        count = sum(len(which) for _, which in plan)
        return list(
            call(
                functools.partial(cut_kernel, sources, plan), name, arrays,
                [((len(which), tok_dev, local), BF16) for _, which in plan],
                [pltpu.SemaphoreType.DMA((count,))], in_hbm=range(len(arrays)), traffic=4 * tok_dev * local * count,
            )
        )

    def onward(x, k):
        return lax.ppermute(x, "seq", [(i, partner(i, k, sources)) for i in range(sources)]) if k else x

    far = [*range(NEAR, sources)]
    q_pieces = cut([queries], [(k, (0,)) for k in far], "cut_first")
    q_blocks = [onward(piece, k) for k, piece in zip(far, q_pieces)]
    q_pieces[0], keys = lax.optimization_barrier((q_pieces[0], keys))
    pieces = cut(
        [queries, keys, values],
        [(k, (0, 1, 2)) for k in reversed(range(NEAR))] + [(k, (i,)) for i in (1, 2) for k in far],
        "cut_rest",
    )
    near_blocks = [onward(pieces[NEAR - 1 - k], k) for k in range(NEAR)]
    q_blocks = near_blocks + q_blocks
    k_blocks = [onward(piece, k) for k, piece in zip(far, pieces[NEAR:])]

    weight_t = final_weight.T
    activated = jax.nn.silu(step_embedding(timesteps)).astype(BF16)
    scale_tok, slope, offset, share, weight_local, text_keys, text_values = call(
        functools.partial(prep_kernel, sources, clips), "prep",
        [activated, mod_weight, weight_t, noise.T, clean.T, text_kv],
        [
            ((group_rows, local), F32), ((sources, channels, tok_dev), F32), ((channels, tok_dev), F32),
            ((clips, tok_dev), F32),
            ((channels, local), BF16), ((clips, text_len, local), BF16), ((clips, text_len, local), BF16),
        ],
        [
            pltpu.VMEM((clips, 2 * width), F32), pltpu.VMEM(mod_weight.shape, BF16),
            pltpu.VMEM(weight_t.shape, BF16), pltpu.VMEM((channels, tok_dev), F32),
            pltpu.VMEM((channels, tok_dev), F32), pltpu.VMEM(text_kv.shape, BF16),
            pltpu.SemaphoreType.DMA((4 + clips,)),
        ],
        scalars=[info], in_hbm=range(1, 6),
    )

    v_pieces, scale_tok = lax.optimization_barrier((pieces[NEAR + len(far) :], scale_tok))
    v_blocks = [onward(piece, k) for k, piece in zip(far, v_pieces)]

    text_out, level = call(
        functools.partial(text_kernel, sources, clips, window), "text", [*q_blocks, text_keys, text_values],
        [((padded, local), F32), ((heads, padded, HEAD_DIM), F32)],
        [pltpu.VMEM((padded, local), BF16)], scalars=[info],
    )

    weights, base = call(
        functools.partial(weigh_kernel, sources, clips, reach), "weigh", [*q_blocks, *k_blocks, text_out, level],
        [((heads, group_rows, reach[1]), BF16), ((group_rows, local), F32)],
        [pltpu.VMEM((group_rows, local), BF16)] * 2, scalars=[info],
    )

    parts = []
    for k in reversed(range(sources)):
        (part,) = call(
            functools.partial(mix_kernel, sources, reach, k), "mix",
            [*near_blocks, *v_blocks, weights, base, scale_tok, weight_local],
            [((channels + STAT_ROWS, tok_dev), BF16)],
            [pltpu.VMEM((group_rows, local), BF16)], flops=4 * tok_dev * reach[1] * local, traffic=2**20,
        )
        parts.append(onward(part, k))

    (shares,) = call(
        functools.partial(loss_kernel, sources, width), "loss", [*parts, slope, offset, share],
        [((groups * sources, 1, HEAD_DIM), F32)],
    )
    everyone = lax.all_to_all(shares, ("dp", "seq"), split_axis=0, concat_axis=0, tiled=True)
    (scores,) = call(
        functools.partial(pick_kernel, clips), "pick",
        [everyone.reshape(groups, sources, HEAD_DIM), report_order.reshape(1, -1)],
        [((1, report_order.shape[0]), F32)], pinned=False,
    )
    return scores.reshape(-1)


def solution(mesh):
    in_specs = (
        P(("dp", "seq"), None),
        P(("dp", "seq"), None),
        P(("dp", "seq"), None),
        P("dp", None, None, "seq"),
        P("dp"),
        P("dp", None),
        P("dp"),
        P(),
        P(),
        P(("dp", "seq"), None),
        P(("dp", "seq"), None),
        P("dp"),
    )
    return jax.shard_map(per_device, mesh=mesh, in_specs=in_specs, out_specs=P("dp"), check_vma=False)
```

```python
import functools
import math

import jax
import jax.numpy as jnp
from jax import lax
from jax.experimental import pallas as pl
from jax.experimental.pallas import tpu as pltpu
from jax.sharding import PartitionSpec as P

HEAD_DIM = 128
FREQ = 256
EPS = 1e-06
NEG = -1e30
STAT_ROWS = 16
ALIGN = 16
NEAR = 2
F32 = jnp.float32
BF16 = jnp.bfloat16
EXACT = lax.Precision.HIGHEST
VMEM_LIMIT = 32 * 1024 * 1024
SCORE_SCALE = math.log2(math.e) / math.sqrt(HEAD_DIM)


def nt_dot(a, b, precision=None):
    return lax.dot_general(a, b, (((1,), (1,)), ((), ())), precision=precision, preferred_element_type=F32)


def head_cols(h):
    return slice(h * HEAD_DIM, (h + 1) * HEAD_DIM)


def step_embedding(timesteps):
    half_width = FREQ // 2
    frequency = jnp.exp(-math.log(10000.0) * jnp.arange(half_width, dtype=F32) / half_width)
    angles = timesteps.astype(F32)[:, None] * frequency[None, :]
    return jnp.concatenate([jnp.cos(angles), jnp.sin(angles)], axis=1)


def clip_index(info_ref, clips, shape, axis, first):
    places = lax.broadcasted_iota(jnp.int32, shape, axis) + first
    end = jnp.int32(0)
    index = jnp.zeros(shape, jnp.int32)
    for c in range(clips):
        end = end + info_ref[c]
        index = index + (places >= end).astype(jnp.int32)
    return index


def partner(rank, k, size):
    return rank ^ k if size & (size - 1) == 0 else (rank + k) % size


def source_rows(sources, k, tok_dev):
    rank = lax.axis_index("seq")
    source = partner(rank, k if sources & (sources - 1) == 0 else sources - k, sources)
    return pl.ds(pl.multiple_of(source * tok_dev, tok_dev), tok_dev)


def origins(rank, sources):
    ahead = reversed(range(sources))
    return [partner(rank, k if sources & (sources - 1) == 0 else sources - k, sources) for k in ahead]


def cut_kernel(sources, plan, *refs):
    count = len(refs) - 1 - len(plan)
    wholes, pieces, sems = refs[:count], refs[count:-1], refs[-1]
    local = pieces[0].shape[2]
    copies = []
    for (k, which), piece in zip(plan, pieces):
        target = partner(lax.axis_index("seq"), k, sources)
        for place, i in enumerate(which):
            columns = pl.ds(pl.multiple_of(target * local, HEAD_DIM), local)
            copies.append(pltpu.make_async_copy(wholes[i].at[:, columns], piece.at[place], sems.at[len(copies)]))
            copies[-1].start()
    for copy in copies:
        copy.wait()


def prep_kernel(
    sources, clips, info_ref, act_ref, mod_hbm, wt_hbm, noise_hbm, clean_hbm, kv_hbm,
    scale_ref, slope_ref, offset_ref, share_ref, weight_ref, keys_ref, values_ref,
    mods, mod_buf, wt_buf, noise_buf, clean_buf, kv_buf, sems,
):
    width = wt_buf.shape[1]
    group_rows, local = scale_ref.shape
    tok_dev = noise_buf.shape[1]
    rank = lax.axis_index("seq")
    pairs = [(mod_hbm, mod_buf), (wt_hbm, wt_buf), (noise_hbm, noise_buf), (clean_hbm, clean_buf)]
    pairs += [(kv_hbm.at[c], kv_buf.at[c]) for c in range(clips)]
    copies = [pltpu.make_async_copy(a, b, sems.at[i]) for i, (a, b) in enumerate(pairs)]
    for copy in copies:
        copy.start()
    for copy in copies[:4]:
        copy.wait()
    mods[...] = jnp.dot(act_ref[...], mod_buf[...], preferred_element_type=F32)
    weight = wt_buf[...].astype(F32)
    shifts = nt_dot(weight, mods[:, :width], EXACT)
    tok_clip = clip_index(info_ref, clips, (clips, tok_dev), 1, rank * tok_dev)
    picks = (tok_clip == lax.broadcasted_iota(jnp.int32, (clips, tok_dev), 0)).astype(F32)
    slot = lax.broadcasted_iota(jnp.int32, (clips, 1), 0)
    sizes = jnp.zeros((clips, 1), F32)
    for c in range(clips):
        sizes = jnp.where(slot == c, info_ref[c].astype(F32), sizes)
    share_ref[...] = picks / sizes
    for place, source in enumerate(origins(rank, sources)):
        low = pl.multiple_of(source * local, HEAD_DIM)
        scales = 1.0 + mods[:, pl.ds(pl.multiple_of(width + low, HEAD_DIM), local)]
        slopes = nt_dot(wt_buf[:, pl.ds(low, local)].astype(F32), scales, EXACT)
        slope_ref[place] = jnp.dot(slopes, picks, precision=EXACT, preferred_element_type=F32)
    offset_ref[...] = jnp.dot(shifts, picks, precision=EXACT, preferred_element_type=F32) - (
        noise_buf[...] - clean_buf[...]
    )
    row_clip = clip_index(info_ref, clips, (group_rows, clips), 0, 0)
    row_picks = (row_clip == lax.broadcasted_iota(jnp.int32, (group_rows, clips), 1)).astype(F32)
    mine = 1.0 + mods[:, pl.ds(pl.multiple_of(width + rank * local, HEAD_DIM), local)]
    scale_ref[...] = jnp.dot(row_picks, mine, precision=EXACT, preferred_element_type=F32)
    weight_ref[...] = wt_buf[:, pl.ds(pl.multiple_of(rank * local, HEAD_DIM), local)]
    for c in range(clips):
        copies[4 + c].wait()
        keys_ref[c] = kv_buf[c, :, 0, :]
        values_ref[c] = kv_buf[c, :, 1, :]


def text_kernel(sources, clips, window, info_ref, *refs):
    q_refs = refs[:sources]
    keys_ref, values_ref, out_ref, level_ref, q_all = refs[sources:]
    tok_dev, local = q_refs[0].shape[1:]
    heads = local // HEAD_DIM
    text_len = keys_ref.shape[1]
    for k, q_ref in enumerate(q_refs):
        q_all[source_rows(sources, k, tok_dev), :] = q_ref[0]
    slots = lax.broadcasted_iota(jnp.int32, (1, text_len), 1)
    ones = jnp.ones((text_len, HEAD_DIM), BF16)

    def one_clip(clip, start):
        first = pl.multiple_of(start // ALIGN * ALIGN, ALIGN)
        rows = pl.ds(first, window)
        edge = pl.ds(first, ALIGN)
        live = slots < info_ref[clips + clip]
        before = lax.broadcasted_iota(jnp.int32, (ALIGN, 1), 0) + first < start
        kept = [(out_ref[edge, head_cols(h)], level_ref[h, edge, :]) for h in range(heads)]
        scores = [nt_dot(q_all[rows, head_cols(h)], keys_ref[clip, :, head_cols(h)]) for h in range(heads)]
        weights, tops = [], []
        for score in scores:
            score = jnp.where(live, score, NEG)
            top = jnp.max(score, axis=1, keepdims=True)
            weights.append(jnp.exp2((score - top) * SCORE_SCALE).astype(BF16))
            tops.append(top)
        results = []
        for h in range(heads):
            beside = jnp.concatenate([values_ref[clip, :, head_cols(h)], ones], axis=1)
            mixed = jnp.dot(weights[h], beside, preferred_element_type=F32)
            total = mixed[:, HEAD_DIM:]
            results.append((mixed[:, :HEAD_DIM] / total, tops[h] * SCORE_SCALE + jnp.log2(total)))
        for h in range(heads):
            out_ref[rows, head_cols(h)] = results[h][0]
            level_ref[h, rows, :] = results[h][1]
            out_ref[edge, head_cols(h)] = jnp.where(before, kept[h][0], results[h][0][:ALIGN])
            level_ref[h, edge, :] = jnp.where(before, kept[h][1], results[h][1][:ALIGN])
        return start + info_ref[clip]

    lax.fori_loop(0, clips, one_clip, jnp.int32(0))


def reach_of(first, reach, group_rows):
    span = group_rows - reach[1]
    return jnp.clip(first - reach[0], 0, span) if span else jnp.int32(0)


def weigh_kernel(sources, clips, reach, info_ref, *refs):
    q_refs, k_refs = refs[:sources], refs[sources : 2 * sources - NEAR]
    text_ref, level_ref, weight_ref, base_ref, q_all, k_all = refs[2 * sources - NEAR :]
    tok_dev, local = q_refs[0].shape[1:]
    group_rows = q_all.shape[0]
    heads = local // HEAD_DIM
    for k in range(sources):
        rows = source_rows(sources, k, tok_dev)
        q_all[rows, :] = q_refs[k][0]
        k_all[rows, :] = q_refs[k][1] if k < NEAR else k_refs[k - NEAR][0]
    for first in range(0, group_rows, tok_dev):
        low = min(max(first - reach[0], 0), group_rows - reach[1])
        rows, span = slice(first, first + tok_dev), slice(low, low + reach[1])
        row_clip = clip_index(info_ref, clips, (tok_dev, 1), 0, first)
        live = row_clip == clip_index(info_ref, clips, (1, reach[1]), 1, low)
        scores = [nt_dot(q_all[rows, head_cols(h)], k_all[span, head_cols(h)]) for h in range(heads)]
        for h in range(heads):
            score = jnp.where(live, scores[h] * SCORE_SCALE, NEG)
            level = level_ref[h, rows, :]
            top = jnp.maximum(jnp.max(score, axis=1, keepdims=True), level)
            chunks = [slice(part, part + HEAD_DIM) for part in range(0, reach[1], HEAD_DIM)]
            weights = [jnp.exp2(score[:, cols] - top) for cols in chunks]
            fade = jnp.exp2(level - top)
            share = 1.0 / (jnp.sum(sum(weights[1:], weights[0]), axis=1, keepdims=True) + fade)
            for cols, weight in zip(chunks, weights):
                weight_ref[h, rows, cols] = (weight * share).astype(BF16)
            base_ref[rows, head_cols(h)] = (fade * share) * text_ref[rows, head_cols(h)]


def mix_kernel(sources, reach, k_target, have, *refs):
    v_refs = refs[:have]
    weight_ref, base_ref, scale_ref, wt_ref, out_ref, v_all = refs[have:]
    tok_dev, local = v_refs[0].shape[1:]
    group_rows = scale_ref.shape[0]
    heads = local // HEAD_DIM
    channels = wt_ref.shape[0]
    for k in range(sources):
        block = v_refs[k][2 if k < NEAR else 0] if k < have else jnp.zeros((tok_dev, local), BF16)
        v_all[source_rows(sources, k, tok_dev), :] = block
    count = out_ref.shape[1]
    first = pl.multiple_of(partner(lax.axis_index("seq"), k_target, sources) * tok_dev, tok_dev)
    rows = pl.ds(first, count)
    span = pl.ds(pl.multiple_of(reach_of(first, reach, group_rows), HEAD_DIM), reach[1])
    mixed = [
        jnp.dot(weight_ref[h, rows, :], v_all[span, head_cols(h)], preferred_element_type=F32) for h in range(heads)
    ]
    attended = jnp.concatenate([(mixed[h] + base_ref[rows, head_cols(h)]).astype(BF16) for h in range(heads)], axis=1)
    attended_full = attended.astype(F32)
    local_mean = jnp.sum(attended_full, axis=1, keepdims=True) * (1.0 / local)
    centred = attended_full - local_mean
    weight = wt_ref[...]
    every = jnp.ones((STAT_ROWS, local), BF16)
    out_ref[:channels, :] = nt_dot(weight, (centred * scale_ref[rows, :]).astype(BF16)).astype(BF16)
    row = lax.broadcasted_iota(jnp.int32, (STAT_ROWS, count), 0)
    rest = jnp.where(row < 3, nt_dot(every, attended), nt_dot(every, (centred * centred).astype(BF16)))
    terms = jnp.zeros((STAT_ROWS, count), F32)
    for place in range(3):
        term = rest.astype(BF16).astype(F32)
        terms = jnp.where((row == place) | (row == place + 3), term, terms)
        rest = rest - term
    out_ref[channels:, :] = terms.astype(BF16)


def read_part(part, channels):
    stat = part[channels:]
    return part[:channels], stat[0:1] + stat[1:2] + stat[2:3], stat[3:4] + stat[4:5] + stat[5:6]


def loss_kernel(sources, width, *refs):
    part_refs = refs[:sources]
    slope_ref, offset_ref, share_ref, out_ref = refs[sources:]
    channels = slope_ref.shape[1]
    clips = share_ref.shape[0]
    projected, sums, squares = [], [], []
    for ref in part_refs:
        for place, value in zip((projected, sums, squares), read_part(ref[...].astype(F32), channels)):
            place.append(value)
    center = sum(sums[1:], sums[0]) * (1.0 / width)
    strays = [value * (sources / width) - center for value in sums]
    spread = sum(squares[1:], squares[0]) * (1.0 / width) + sum(stray * stray for stray in strays) * (1.0 / sources)
    total = sum(projected[1:], projected[0])
    for place in range(sources):
        total = total + strays[place] * slope_ref[place]
    diff = total * lax.rsqrt(spread + EPS) + offset_ref[...]
    error = jnp.sum(diff * diff, axis=0, keepdims=True) * (1.0 / channels)
    sums = jnp.sum(share_ref[...] * error, axis=1, keepdims=True)
    lanes = lax.broadcasted_iota(jnp.int32, (clips, out_ref.shape[2]), 1)
    mine = lanes == lax.broadcasted_iota(jnp.int32, lanes.shape, 0)
    row = jnp.sum(jnp.where(mine, sums, 0.0), axis=0, keepdims=True)
    out_ref[...] = jnp.broadcast_to(row[None], out_ref.shape)


def pick_kernel(clips, losses_ref, order_ref, out_ref):
    losses = jnp.sum(losses_ref[...], axis=1)
    order = order_ref[...]
    column = lax.broadcasted_iota(jnp.int32, (losses.shape[1], order.shape[1]), 0)
    chosen = (column == lax.rem(order, clips)).astype(F32)
    by_group = jnp.dot(losses, chosen, precision=EXACT, preferred_element_type=F32)
    group = lax.broadcasted_iota(jnp.int32, by_group.shape, 0)
    out_ref[...] = jnp.sum(jnp.where(group == lax.div(order, clips), by_group, 0.0), axis=0, keepdims=True)


def smem():
    return pl.BlockSpec(memory_space=pltpu.SMEM)


def vmem():
    return pl.BlockSpec(memory_space=pltpu.VMEM)


def hbm():
    return pl.BlockSpec(memory_space=pltpu.HBM)


def call(kernel, name, operands, results, scratch=(), scalars=(), in_hbm=(), pinned=True, flops=0, traffic=0):
    return pl.pallas_call(
        kernel,
        in_specs=[smem()] * len(scalars) + [hbm() if i in in_hbm else vmem() for i in range(len(operands))],
        out_specs=[vmem()] * len(results),
        out_shape=[pltpu.VMEM(*r) if pinned else jax.ShapeDtypeStruct(*r) for r in results],
        scratch_shapes=list(scratch),
        compiler_params=pltpu.CompilerParams(vmem_limit_bytes=VMEM_LIMIT),
        cost_estimate=pl.CostEstimate(flops=flops, bytes_accessed=traffic, transcendentals=0),
        name=name,
    )(*scalars, *(pltpu.with_memory_space_constraint(x, pltpu.HBM) if i in in_hbm else x for i, x in enumerate(operands)))


def per_device(
    queries, keys, values, text_kv, text_lengths, clip_lengths, timesteps, mod_weight, final_weight, noise, clean,
    report_order,
):
    tok_dev, width = queries.shape
    sources = lax.axis_size("seq")
    groups = lax.axis_size("dp")
    local = width // sources
    heads = local // HEAD_DIM
    group_rows = tok_dev * sources
    clips = clip_lengths.shape[1]
    text_len = text_kv.shape[1]
    clip_most = 2 * group_rows // clips
    window = clip_most + ALIGN
    padded = group_rows + window
    reach = (clip_most, min(group_rows, tok_dev + 2 * clip_most))
    channels = final_weight.shape[1]
    info = jnp.concatenate([clip_lengths[0], text_lengths])

    def cut(arrays, plan, name):
        count = sum(len(which) for _, which in plan)
        return list(
            call(
                functools.partial(cut_kernel, sources, plan), name, arrays,
                [((len(which), tok_dev, local), BF16) for _, which in plan],
                [pltpu.SemaphoreType.DMA((count,))], in_hbm=range(len(arrays)), traffic=4 * tok_dev * local * count,
            )
        )

    def onward(x, k):
        return lax.ppermute(x, "seq", [(i, partner(i, k, sources)) for i in range(sources)]) if k else x

    far = [*range(NEAR, sources)]
    q_pieces = cut([queries], [(k, (0,)) for k in far], "cut_first")
    q_blocks = [onward(piece, k) for k, piece in zip(far, q_pieces)]
    q_pieces[0], keys = lax.optimization_barrier((q_pieces[0], keys))
    pieces = cut(
        [queries, keys, values],
        [(k, (0, 1, 2)) for k in reversed(range(NEAR))] + [(k, (i,)) for i in (1, 2) for k in far],
        "cut_rest",
    )
    near_blocks = [onward(pieces[NEAR - 1 - k], k) for k in range(NEAR)]
    q_blocks = near_blocks + q_blocks
    k_blocks = [onward(piece, k) for k, piece in zip(far, pieces[NEAR:])]

    weight_t = final_weight.T
    activated = jax.nn.silu(step_embedding(timesteps)).astype(BF16)
    scale_tok, slope, offset, share, weight_local, text_keys, text_values = call(
        functools.partial(prep_kernel, sources, clips), "prep",
        [activated, mod_weight, weight_t, noise.T, clean.T, text_kv],
        [
            ((group_rows, local), F32), ((sources, channels, tok_dev), F32), ((channels, tok_dev), F32),
            ((clips, tok_dev), F32),
            ((channels, local), BF16), ((clips, text_len, local), BF16), ((clips, text_len, local), BF16),
        ],
        [
            pltpu.VMEM((clips, 2 * width), F32), pltpu.VMEM(mod_weight.shape, BF16),
            pltpu.VMEM(weight_t.shape, BF16), pltpu.VMEM((channels, tok_dev), F32),
            pltpu.VMEM((channels, tok_dev), F32), pltpu.VMEM(text_kv.shape, BF16),
            pltpu.SemaphoreType.DMA((4 + clips,)),
        ],
        scalars=[info], in_hbm=range(1, 6),
    )

    v_pieces, scale_tok = lax.optimization_barrier((pieces[NEAR + len(far) :], scale_tok))
    v_blocks = [onward(piece, k) for k, piece in zip(far, v_pieces)]

    text_out, level = call(
        functools.partial(text_kernel, sources, clips, window), "text", [*q_blocks, text_keys, text_values],
        [((padded, local), F32), ((heads, padded, HEAD_DIM), F32)],
        [pltpu.VMEM((padded, local), BF16)], scalars=[info],
    )

    weights, base = call(
        functools.partial(weigh_kernel, sources, clips, reach), "weigh", [*q_blocks, *k_blocks, text_out, level],
        [((heads, group_rows, reach[1]), BF16), ((group_rows, local), F32)],
        [pltpu.VMEM((group_rows, local), BF16)] * 2, scalars=[info],
    )

    def mix(k, have):
        return call(
            functools.partial(mix_kernel, sources, reach, k, have), "mix",
            [*[*near_blocks, *v_blocks][:have], weights, base, scale_tok, weight_local],
            [((channels + STAT_ROWS, tok_dev), BF16)],
            [pltpu.VMEM((group_rows, local), BF16)], flops=4 * tok_dev * reach[1] * local, traffic=2**20,
        )[0]

    parts = [None] * sources
    if sources == 4 and clip_most <= tok_dev:
        first = mix(1, 3)
        parts[1] = onward(first, 1)
        v_blocks[-1], _ = lax.optimization_barrier((v_blocks[-1], first))
    for k in reversed(range(sources)):
        if parts[k] is None:
            parts[k] = onward(mix(k, sources), k)
        if k == 3 and parts[1] is not None:
            weights, parts[1] = lax.optimization_barrier((weights, parts[1]))
    parts = parts[::-1]

    (shares,) = call(
        functools.partial(loss_kernel, sources, width), "loss", [*parts, slope, offset, share],
        [((groups * sources, 1, HEAD_DIM), F32)],
    )
    everyone = lax.all_to_all(shares, ("dp", "seq"), split_axis=0, concat_axis=0, tiled=True)
    (scores,) = call(
        functools.partial(pick_kernel, clips), "pick",
        [everyone.reshape(groups, sources, HEAD_DIM), report_order.reshape(1, -1)],
        [((1, report_order.shape[0]), F32)], pinned=False,
    )
    return scores.reshape(-1)


def solution(mesh):
    in_specs = (
        P(("dp", "seq"), None),
        P(("dp", "seq"), None),
        P(("dp", "seq"), None),
        P("dp", None, None, "seq"),
        P("dp"),
        P("dp", None),
        P("dp"),
        P(),
        P(),
        P(("dp", "seq"), None),
        P(("dp", "seq"), None),
        P("dp"),
    )
    return jax.shard_map(per_device, mesh=mesh, in_specs=in_specs, out_specs=P("dp"), check_vma=False)
```

```python
import functools
import math

import jax
import jax.numpy as jnp
from jax import lax
from jax.experimental import pallas as pl
from jax.experimental.pallas import tpu as pltpu
from jax.sharding import PartitionSpec as P

HEAD_DIM = 128
FREQ = 256
EPS = 1e-06
NEG = -1e30
STAT_ROWS = 16
ALIGN = 16
NEAR = 2
F32 = jnp.float32
BF16 = jnp.bfloat16
EXACT = lax.Precision.HIGHEST
VMEM_LIMIT = 32 * 1024 * 1024
SCORE_SCALE = math.log2(math.e) / math.sqrt(HEAD_DIM)


def nt_dot(a, b, precision=None):
    return lax.dot_general(a, b, (((1,), (1,)), ((), ())), precision=precision, preferred_element_type=F32)


def head_cols(h):
    return slice(h * HEAD_DIM, (h + 1) * HEAD_DIM)


def step_embedding(timesteps):
    half_width = FREQ // 2
    frequency = jnp.exp(-math.log(10000.0) * jnp.arange(half_width, dtype=F32) / half_width)
    angles = timesteps.astype(F32)[:, None] * frequency[None, :]
    return jnp.concatenate([jnp.cos(angles), jnp.sin(angles)], axis=1)


def clip_index(info_ref, clips, shape, axis, first):
    places = lax.broadcasted_iota(jnp.int32, shape, axis) + first
    end = jnp.int32(0)
    index = jnp.zeros(shape, jnp.int32)
    for c in range(clips):
        end = end + info_ref[c]
        index = index + (places >= end).astype(jnp.int32)
    return index


def partner(rank, k, size):
    return rank ^ k if size & (size - 1) == 0 else (rank + k) % size


def source_rows(sources, k, tok_dev):
    rank = lax.axis_index("seq")
    source = partner(rank, k if sources & (sources - 1) == 0 else sources - k, sources)
    return pl.ds(pl.multiple_of(source * tok_dev, tok_dev), tok_dev)


def origins(rank, sources):
    ahead = reversed(range(sources))
    return [partner(rank, k if sources & (sources - 1) == 0 else sources - k, sources) for k in ahead]


def cut_kernel(sources, plan, *refs):
    count = len(refs) - 1 - len(plan)
    wholes, pieces, sems = refs[:count], refs[count:-1], refs[-1]
    local = pieces[0].shape[2]
    copies = []
    for (k, which), piece in zip(plan, pieces):
        target = partner(lax.axis_index("seq"), k, sources)
        for place, i in enumerate(which):
            columns = pl.ds(pl.multiple_of(target * local, HEAD_DIM), local)
            copies.append(pltpu.make_async_copy(wholes[i].at[:, columns], piece.at[place], sems.at[len(copies)]))
            copies[-1].start()
    for copy in copies:
        copy.wait()


def prep_kernel(
    sources, clips, info_ref, act_ref, mod_hbm, wt_hbm, noise_hbm, clean_hbm, kv_hbm,
    scale_ref, slope_ref, offset_ref, share_ref, weight_ref, keys_ref, values_ref,
    mods, mod_buf, wt_buf, noise_buf, clean_buf, kv_buf, sems,
):
    width = wt_buf.shape[1]
    group_rows, local = scale_ref.shape
    tok_dev = noise_buf.shape[1]
    rank = lax.axis_index("seq")
    pairs = [(mod_hbm, mod_buf), (wt_hbm, wt_buf), (noise_hbm, noise_buf), (clean_hbm, clean_buf)]
    pairs += [(kv_hbm.at[c], kv_buf.at[c]) for c in range(clips)]
    copies = [pltpu.make_async_copy(a, b, sems.at[i]) for i, (a, b) in enumerate(pairs)]
    for copy in copies:
        copy.start()
    for copy in copies[:4]:
        copy.wait()
    mods[...] = jnp.dot(act_ref[...], mod_buf[...], preferred_element_type=F32)
    weight = wt_buf[...].astype(F32)
    shifts = nt_dot(weight, mods[:, :width], EXACT)
    tok_clip = clip_index(info_ref, clips, (clips, tok_dev), 1, rank * tok_dev)
    picks = (tok_clip == lax.broadcasted_iota(jnp.int32, (clips, tok_dev), 0)).astype(F32)
    slot = lax.broadcasted_iota(jnp.int32, (clips, 1), 0)
    sizes = jnp.zeros((clips, 1), F32)
    for c in range(clips):
        sizes = jnp.where(slot == c, info_ref[c].astype(F32), sizes)
    share_ref[...] = picks / sizes
    for place, source in enumerate(origins(rank, sources)):
        low = pl.multiple_of(source * local, HEAD_DIM)
        scales = 1.0 + mods[:, pl.ds(pl.multiple_of(width + low, HEAD_DIM), local)]
        slopes = nt_dot(wt_buf[:, pl.ds(low, local)].astype(F32), scales, EXACT)
        slope_ref[place] = jnp.dot(slopes, picks, precision=EXACT, preferred_element_type=F32)
    offset_ref[...] = jnp.dot(shifts, picks, precision=EXACT, preferred_element_type=F32) - (
        noise_buf[...] - clean_buf[...]
    )
    row_clip = clip_index(info_ref, clips, (group_rows, clips), 0, 0)
    row_picks = (row_clip == lax.broadcasted_iota(jnp.int32, (group_rows, clips), 1)).astype(F32)
    mine = 1.0 + mods[:, pl.ds(pl.multiple_of(width + rank * local, HEAD_DIM), local)]
    scale_ref[...] = jnp.dot(row_picks, mine, precision=EXACT, preferred_element_type=F32)
    weight_ref[...] = wt_buf[:, pl.ds(pl.multiple_of(rank * local, HEAD_DIM), local)]
    for c in range(clips):
        copies[4 + c].wait()
        keys_ref[c] = kv_buf[c, :, 0, :]
        values_ref[c] = kv_buf[c, :, 1, :]


def text_kernel(sources, clips, window, info_ref, *refs):
    q_refs = refs[:sources]
    keys_ref, values_ref, out_ref, level_ref, q_all = refs[sources:]
    tok_dev, local = q_refs[0].shape[1:]
    heads = local // HEAD_DIM
    text_len = keys_ref.shape[1]
    for k, q_ref in enumerate(q_refs):
        q_all[source_rows(sources, k, tok_dev), :] = q_ref[0]
    slots = lax.broadcasted_iota(jnp.int32, (1, text_len), 1)
    ones = jnp.ones((text_len, HEAD_DIM), BF16)

    def one_clip(clip, start):
        first = pl.multiple_of(start // ALIGN * ALIGN, ALIGN)
        rows = pl.ds(first, window)
        edge = pl.ds(first, ALIGN)
        live = slots < info_ref[clips + clip]
        before = lax.broadcasted_iota(jnp.int32, (ALIGN, 1), 0) + first < start
        kept = [(out_ref[edge, head_cols(h)], level_ref[h, edge, :]) for h in range(heads)]
        scores = [nt_dot(q_all[rows, head_cols(h)], keys_ref[clip, :, head_cols(h)]) for h in range(heads)]
        weights, tops = [], []
        for score in scores:
            score = jnp.where(live, score, NEG)
            top = jnp.max(score, axis=1, keepdims=True)
            weights.append(jnp.exp2((score - top) * SCORE_SCALE).astype(BF16))
            tops.append(top)
        results = []
        for h in range(heads):
            beside = jnp.concatenate([values_ref[clip, :, head_cols(h)], ones], axis=1)
            mixed = jnp.dot(weights[h], beside, preferred_element_type=F32)
            total = mixed[:, HEAD_DIM:]
            results.append((mixed[:, :HEAD_DIM] / total, tops[h] * SCORE_SCALE + jnp.log2(total)))
        for h in range(heads):
            out_ref[rows, head_cols(h)] = results[h][0]
            level_ref[h, rows, :] = results[h][1]
            out_ref[edge, head_cols(h)] = jnp.where(before, kept[h][0], results[h][0][:ALIGN])
            level_ref[h, edge, :] = jnp.where(before, kept[h][1], results[h][1][:ALIGN])
        return start + info_ref[clip]

    lax.fori_loop(0, clips, one_clip, jnp.int32(0))


def reach_of(first, reach, group_rows):
    span = group_rows - reach[1]
    return jnp.clip(first - reach[0], 0, span) if span else jnp.int32(0)


def weigh_kernel(sources, clips, reach, info_ref, *refs):
    q_refs, k_refs = refs[:sources], refs[sources : 2 * sources - NEAR]
    text_ref, level_ref, weight_ref, base_ref, q_all, k_all = refs[2 * sources - NEAR :]
    tok_dev, local = q_refs[0].shape[1:]
    group_rows = q_all.shape[0]
    heads = local // HEAD_DIM
    for k in range(sources):
        rows = source_rows(sources, k, tok_dev)
        q_all[rows, :] = q_refs[k][0]
        k_all[rows, :] = q_refs[k][1] if k < NEAR else k_refs[k - NEAR][0]
    for first in range(0, group_rows, tok_dev):
        low = min(max(first - reach[0], 0), group_rows - reach[1])
        rows, span = slice(first, first + tok_dev), slice(low, low + reach[1])
        row_clip = clip_index(info_ref, clips, (tok_dev, 1), 0, first)
        live = row_clip == clip_index(info_ref, clips, (1, reach[1]), 1, low)
        scores = [nt_dot(q_all[rows, head_cols(h)], k_all[span, head_cols(h)]) for h in range(heads)]
        for h in range(heads):
            score = jnp.where(live, scores[h] * SCORE_SCALE, NEG)
            level = level_ref[h, rows, :]
            top = jnp.maximum(jnp.max(score, axis=1, keepdims=True), level)
            chunks = [slice(part, part + HEAD_DIM) for part in range(0, reach[1], HEAD_DIM)]
            weights = [jnp.exp2(score[:, cols] - top) for cols in chunks]
            fade = jnp.exp2(level - top)
            share = 1.0 / (jnp.sum(sum(weights[1:], weights[0]), axis=1, keepdims=True) + fade)
            for cols, weight in zip(chunks, weights):
                weight_ref[h, rows, cols] = (weight * share).astype(BF16)
            base_ref[rows, head_cols(h)] = (fade * share) * text_ref[rows, head_cols(h)]


def mix_kernel(sources, reach, k_target, have, *refs):
    v_refs = refs[:have]
    weight_ref, base_ref, scale_ref, wt_ref, out_ref, v_all = refs[have:]
    tok_dev, local = v_refs[0].shape[1:]
    group_rows = scale_ref.shape[0]
    heads = local // HEAD_DIM
    channels = wt_ref.shape[0]
    for k in range(sources):
        block = v_refs[k][2 if k < NEAR else 0] if k < have else jnp.zeros((tok_dev, local), BF16)
        v_all[source_rows(sources, k, tok_dev), :] = block
    count = out_ref.shape[1]
    first = pl.multiple_of(partner(lax.axis_index("seq"), k_target, sources) * tok_dev, tok_dev)
    rows = pl.ds(first, count)
    span = pl.ds(pl.multiple_of(reach_of(first, reach, group_rows), HEAD_DIM), reach[1])
    mixed = [
        jnp.dot(weight_ref[h, rows, :], v_all[span, head_cols(h)], preferred_element_type=F32) for h in range(heads)
    ]
    attended = jnp.concatenate([(mixed[h] + base_ref[rows, head_cols(h)]).astype(BF16) for h in range(heads)], axis=1)
    attended_full = attended.astype(F32)
    local_mean = jnp.sum(attended_full, axis=1, keepdims=True) * (1.0 / local)
    centred = attended_full - local_mean
    weight = wt_ref[...]
    every = jnp.ones((STAT_ROWS, local), BF16)
    out_ref[:channels, :] = nt_dot(weight, (centred * scale_ref[rows, :]).astype(BF16)).astype(BF16)
    row = lax.broadcasted_iota(jnp.int32, (STAT_ROWS, count), 0)
    rest = jnp.where(row < 3, nt_dot(every, attended), nt_dot(every, (centred * centred).astype(BF16)))
    terms = jnp.zeros((STAT_ROWS, count), F32)
    for place in range(3):
        term = rest.astype(BF16).astype(F32)
        terms = jnp.where((row == place) | (row == place + 3), term, terms)
        rest = rest - term
    out_ref[channels:, :] = terms.astype(BF16)


def read_part(part, channels):
    stat = part[channels:]
    return part[:channels], stat[0:1] + stat[1:2] + stat[2:3], stat[3:4] + stat[4:5] + stat[5:6]


def loss_kernel(sources, width, *refs):
    part_refs = refs[:sources]
    slope_ref, offset_ref, share_ref, out_ref = refs[sources:]
    channels = slope_ref.shape[1]
    clips = share_ref.shape[0]
    projected, sums, squares = [], [], []
    for ref in part_refs:
        for place, value in zip((projected, sums, squares), read_part(ref[...].astype(F32), channels)):
            place.append(value)
    center = sum(sums[1:], sums[0]) * (1.0 / width)
    strays = [value * (sources / width) - center for value in sums]
    spread = sum(squares[1:], squares[0]) * (1.0 / width) + sum(stray * stray for stray in strays) * (1.0 / sources)
    total = sum(projected[1:], projected[0])
    for place in range(sources):
        total = total + strays[place] * slope_ref[place]
    diff = total * lax.rsqrt(spread + EPS) + offset_ref[...]
    error = jnp.sum(diff * diff, axis=0, keepdims=True) * (1.0 / channels)
    sums = jnp.sum(share_ref[...] * error, axis=1, keepdims=True)
    lanes = lax.broadcasted_iota(jnp.int32, (clips, out_ref.shape[2]), 1)
    mine = lanes == lax.broadcasted_iota(jnp.int32, lanes.shape, 0)
    row = jnp.sum(jnp.where(mine, sums, 0.0), axis=0, keepdims=True)
    out_ref[...] = jnp.broadcast_to(row[None], out_ref.shape)


def pick_kernel(clips, losses_ref, order_ref, out_ref):
    losses = jnp.sum(losses_ref[...], axis=1)
    order = order_ref[...]
    column = lax.broadcasted_iota(jnp.int32, (losses.shape[1], order.shape[1]), 0)
    chosen = (column == lax.rem(order, clips)).astype(F32)
    by_group = jnp.dot(losses, chosen, precision=EXACT, preferred_element_type=F32)
    group = lax.broadcasted_iota(jnp.int32, by_group.shape, 0)
    out_ref[...] = jnp.sum(jnp.where(group == lax.div(order, clips), by_group, 0.0), axis=0, keepdims=True)


def smem():
    return pl.BlockSpec(memory_space=pltpu.SMEM)


def vmem():
    return pl.BlockSpec(memory_space=pltpu.VMEM)


def hbm():
    return pl.BlockSpec(memory_space=pltpu.HBM)


def call(kernel, name, operands, results, scratch=(), scalars=(), in_hbm=(), pinned=True, flops=0, traffic=0):
    return pl.pallas_call(
        kernel,
        in_specs=[smem()] * len(scalars) + [hbm() if i in in_hbm else vmem() for i in range(len(operands))],
        out_specs=[vmem()] * len(results),
        out_shape=[pltpu.VMEM(*r) if pinned else jax.ShapeDtypeStruct(*r) for r in results],
        scratch_shapes=list(scratch),
        compiler_params=pltpu.CompilerParams(vmem_limit_bytes=VMEM_LIMIT),
        cost_estimate=pl.CostEstimate(flops=flops, bytes_accessed=traffic, transcendentals=0),
        name=name,
    )(*scalars, *(pltpu.with_memory_space_constraint(x, pltpu.HBM) if i in in_hbm else x for i, x in enumerate(operands)))


def per_device(
    queries, keys, values, text_kv, text_lengths, clip_lengths, timesteps, mod_weight, final_weight, noise, clean,
    report_order,
):
    tok_dev, width = queries.shape
    sources = lax.axis_size("seq")
    groups = lax.axis_size("dp")
    local = width // sources
    heads = local // HEAD_DIM
    group_rows = tok_dev * sources
    clips = clip_lengths.shape[1]
    text_len = text_kv.shape[1]
    clip_most = 2 * group_rows // clips
    window = clip_most + ALIGN
    padded = group_rows + window
    reach = (clip_most, min(group_rows, tok_dev + 2 * clip_most))
    channels = final_weight.shape[1]
    info = jnp.concatenate([clip_lengths[0], text_lengths])

    def cut(arrays, plan, name):
        count = sum(len(which) for _, which in plan)
        return list(
            call(
                functools.partial(cut_kernel, sources, plan), name, arrays,
                [((len(which), tok_dev, local), BF16) for _, which in plan],
                [pltpu.SemaphoreType.DMA((count,))], in_hbm=range(len(arrays)), traffic=4 * tok_dev * local * count,
            )
        )

    def onward(x, k):
        return lax.ppermute(x, "seq", [(i, partner(i, k, sources)) for i in range(sources)]) if k else x

    far = [*range(NEAR, sources)]
    q_pieces = cut([queries], [(k, (0,)) for k in far], "cut_first")
    q_blocks = [onward(piece, k) for k, piece in zip(far, q_pieces)]
    q_pieces[0], keys = lax.optimization_barrier((q_pieces[0], keys))
    pieces = cut(
        [queries, keys, values],
        [(k, (0, 1, 2)) for k in reversed(range(NEAR))] + [(k, (i,)) for i in (1, 2) for k in far],
        "cut_rest",
    )
    near_blocks = [onward(pieces[NEAR - 1 - k], k) for k in range(NEAR)]
    q_blocks = near_blocks + q_blocks
    k_blocks = [onward(piece, k) for k, piece in zip(far, pieces[NEAR:])]

    weight_t = final_weight.T
    activated = jax.nn.silu(step_embedding(timesteps)).astype(BF16)
    scale_tok, slope, offset, share, weight_local, text_keys, text_values = call(
        functools.partial(prep_kernel, sources, clips), "prep",
        [activated, mod_weight, weight_t, noise.T, clean.T, text_kv],
        [
            ((group_rows, local), F32), ((sources, channels, tok_dev), F32), ((channels, tok_dev), F32),
            ((clips, tok_dev), F32),
            ((channels, local), BF16), ((clips, text_len, local), BF16), ((clips, text_len, local), BF16),
        ],
        [
            pltpu.VMEM((clips, 2 * width), F32), pltpu.VMEM(mod_weight.shape, BF16),
            pltpu.VMEM(weight_t.shape, BF16), pltpu.VMEM((channels, tok_dev), F32),
            pltpu.VMEM((channels, tok_dev), F32), pltpu.VMEM(text_kv.shape, BF16),
            pltpu.SemaphoreType.DMA((4 + clips,)),
        ],
        scalars=[info], in_hbm=range(1, 6),
    )

    v_pieces, scale_tok = lax.optimization_barrier((pieces[NEAR + len(far) :], scale_tok))
    v_blocks = [onward(piece, k) for k, piece in zip(far, v_pieces)]

    text_out, level = call(
        functools.partial(text_kernel, sources, clips, window), "text", [*q_blocks, text_keys, text_values],
        [((padded, local), F32), ((heads, padded, HEAD_DIM), F32)],
        [pltpu.VMEM((padded, local), BF16)], scalars=[info],
    )

    weights, base = call(
        functools.partial(weigh_kernel, sources, clips, reach), "weigh", [*q_blocks, *k_blocks, text_out, level],
        [((heads, group_rows, reach[1]), BF16), ((group_rows, local), F32)],
        [pltpu.VMEM((group_rows, local), BF16)] * 2, scalars=[info],
    )

    def mix(k, have):
        return call(
            functools.partial(mix_kernel, sources, reach, k, have), "mix",
            [*[*near_blocks, *v_blocks][:have], weights, base, scale_tok, weight_local],
            [((channels + STAT_ROWS, tok_dev), BF16)],
            [pltpu.VMEM((group_rows, local), BF16)], flops=4 * tok_dev * reach[1] * local, traffic=2**20,
        )[0]

    parts = [None] * sources
    if sources == 4 and clip_most <= tok_dev:
        first = mix(1, 3)
        parts[1] = onward(first, 1)
        v_blocks[-1], _ = lax.optimization_barrier((v_blocks[-1], first))
    for k in reversed(range(sources)):
        if parts[k] is None:
            parts[k] = onward(mix(k, sources), k)
        if k == 2 and parts[1] is not None:
            weights, parts[1] = lax.optimization_barrier((weights, parts[1]))
    parts = parts[::-1]

    (shares,) = call(
        functools.partial(loss_kernel, sources, width), "loss", [*parts, slope, offset, share],
        [((groups * sources, 1, HEAD_DIM), F32)],
    )
    everyone = lax.all_to_all(shares, ("dp", "seq"), split_axis=0, concat_axis=0, tiled=True)
    (scores,) = call(
        functools.partial(pick_kernel, clips), "pick",
        [everyone.reshape(groups, sources, HEAD_DIM), report_order.reshape(1, -1)],
        [((1, report_order.shape[0]), F32)], pinned=False,
    )
    return scores.reshape(-1)


def solution(mesh):
    in_specs = (
        P(("dp", "seq"), None),
        P(("dp", "seq"), None),
        P(("dp", "seq"), None),
        P("dp", None, None, "seq"),
        P("dp"),
        P("dp", None),
        P("dp"),
        P(),
        P(),
        P(("dp", "seq"), None),
        P(("dp", "seq"), None),
        P("dp"),
    )
    return jax.shard_map(per_device, mesh=mesh, in_specs=in_specs, out_specs=P("dp"), check_vma=False)
```
